32 devices in a mesh: replica: 4 (over z), shard: 8 (over y, x, core).
Axes of the slice: x: 2, y: 2, z: 4, core: 2. Of those that a mesh axis runs over, the one named last changes fastest.
Arguments:
- tokens: bfloat16 [2, 32, 512, 768], P(None, ('replica', 'shard')), may hold values from -6 to 6
- cotangent: bfloat16 [2, 32, 512, 768], P(None, ('replica', 'shard')), may hold values from -6 to 6
- lengths: int32 [64], replicated, may hold values from 128 to 512, as said below
- dealing: int32 [64], replicated, may hold values from 0 to 63, each once
- in_gain: float32 [2, 768], replicated, may hold values from 0.5 to 1.5
- w_in: bfloat16 [2, 768, 3352], P(None, 'shard'), may hold values from -0.21875 to 0.21875
- conv_w: float32 [2, 4, 1792], replicated, may hold values from -3 to 3
- conv_b: float32 [2, 1792], replicated, may hold values from -3 to 3
- dt_bias: float32 [2, 24], replicated, may hold values from -6.9 to -2.3
- a_log: float32 [2, 24], replicated, may hold values from 0 to 2.77
- d_skip: float32 [2, 24], replicated, may hold values from 0.1 to 1.9
- out_gain: float32 [2, 1536], replicated, may hold values from 0.5 to 1.5
- w_out: bfloat16 [2, 1536, 768], P(None, 'shard'), may hold values from -0.15625 to 0.15625
Outputs:
- outputs: bfloat16 [2, 32, 512, 768], P(None, ('replica', 'shard'))
- grad_tokens: float32 [2, 32, 512, 768], P(None, ('replica', 'shard'))
- grad_in_gain: float32 [2, 768], replicated
- grad_w_in: float32 [2, 768, 3352], P(None, 'shard')
- grad_conv_w: float32 [2, 4, 1792], replicated
- grad_conv_b: float32 [2, 1792], replicated
- grad_dt_bias: float32 [2, 24], replicated
- grad_a_log: float32 [2, 24], replicated
- grad_d_skip: float32 [2, 24], replicated
- grad_out_gain: float32 [2, 1536], replicated
- grad_w_out: float32 [2, 1536, 768], P(None, 'shard')
The draws below stay inside these ranges and needn't reach their ends.
Inputs may be any that keep to these rules, and one draw needn't show every extreme that they name: `lengths`: one sequence has exactly 512 tokens; the others at least a quarter of that.
All inputs are finite; a program needn't handle non-finite values.
Results may differ from the reference program's by a relative error of at most 0.011.
Values may be sent and summed in bfloat16 or wider, within the bound.
A program may use at most 208 MiB of HBM per device.

```python
import jax
import jax.numpy as jnp
from jax import lax

D = 768
DI = 1536
NH = 24
HEAD = 64
NSTATE = 128
KW = 4
SPAN = 256
CONV_CH = 1792
NIN = 3352
LAYERS = 2
MICRO = 2
ROW = 512
ROWS = 32
SEQS = 64


def draw_lengths(key, part):
    key = jax.random.fold_in(key, 11)
    first_key, second_key = jax.random.split(key)
    drawn_lengths = jax.random.randint(first_key, (SEQS,), ROW // 4, ROW + 1)
    chosen = jax.random.randint(second_key, (), 0, SEQS)
    return jnp.where(jnp.arange(SEQS) == chosen, ROW, drawn_lengths).astype(jnp.int32)


def strengthened(entries, rng, source, target, parts, factor):
    owner, partner = [(jnp.arange(entries.shape[position]) // (entries.shape[position] // parts)).reshape([-1 if axis == position else 1 for axis in range(entries.ndim)]) for position in (source, target)]
    chosen = jax.random.permutation(rng, parts)[partner]
    strong = (owner == chosen) | (owner == (partner + parts // 2) % parts)
    return jnp.where(strong, factor * entries, entries)


def steps_of(key, extent, cuts, low, high):
    factor_of = 1.0
    for axis_at, parts in cuts:
        steps = jax.random.uniform(jax.random.fold_in(jax.random.fold_in(key, 6), axis_at), (parts,), jnp.float32, low / len(cuts), high / len(cuts))
        factor_of = factor_of * jnp.repeat(jnp.exp(steps), extent[axis_at] // parts).reshape((-1,) + (1,) * (len(extent) - 1 - axis_at))
    return factor_of


def centred(own_key, dims, spread, limit, shards=(), kind=jnp.bfloat16):
    array = jax.random.normal(own_key, dims, jnp.float32) * spread
    if len(shards) > 0:
        array = steps_of(own_key, dims, shards, -0.22, 0.18) * array
    return jnp.clip(array, min=-limit, max=limit).astype(kind)


def noise_with(key, extent, width, bound, cuts, heavy, kind=jnp.bfloat16):
    drawn = width * jax.random.normal(key, extent, jnp.float32)
    if cuts:
        drawn = drawn * steps_of(key, extent, cuts, -0.22, 0.18)
    return jnp.clip(strengthened(drawn, jax.random.fold_in(key, 3), *heavy), -bound, bound).astype(kind)


def setup_inputs(seed: int = 0) -> dict:
    seeds = jax.random.split(jax.random.key(seed), 14)
    tokens = noise_with(seeds[0], (MICRO, ROWS, ROW, D), 1.0, 6.0, ((1, 32),), (1, 3, 32, 2.75))
    cotangent = centred(seeds[1], (MICRO, ROWS, ROW, D), 1.0, 6.0, ((1, 32),))
    lengths = draw_lengths(jax.random.fold_in(seeds[13], 71), 0)
    dealing = jax.random.permutation(seeds[3], SEQS).astype(jnp.int32)
    in_gain = jnp.clip(1.0 + 0.1 * jax.random.normal(seeds[4], (LAYERS, D), jnp.float32), 0.5, 1.5)
    w_in = centred(seeds[5], (LAYERS, D, NIN), D ** -0.5, 0.21875, ((1, 8),))
    conv_w = centred(seeds[6], (LAYERS, KW, CONV_CH), KW ** -0.5, 3.0, (), jnp.float32)
    conv_b = centred(seeds[7], (LAYERS, CONV_CH), 0.5, 3.0, (), jnp.float32)
    dt_bias = jnp.clip(jax.random.uniform(seeds[8], (LAYERS, NH), jnp.float32, -6.9, -2.3), -6.9, -2.3)
    a_log = jnp.clip(jax.random.uniform(seeds[9], (LAYERS, NH), jnp.float32, 0.0, 2.77), 0.0, 2.77)
    d_skip = jnp.clip(1.0 + 0.18 * jax.random.normal(seeds[10], (LAYERS, NH), jnp.float32), 0.1, 1.9)
    out_gain = jnp.clip(1.0 + 0.1 * jax.random.normal(seeds[11], (LAYERS, DI), jnp.float32), 0.5, 1.5)
    w_out = centred(seeds[12], (LAYERS, DI, D), DI ** -0.5, 0.15625, ((1, 8),))
    return dict(tokens=tokens, cotangent=cotangent, lengths=lengths, dealing=dealing, in_gain=in_gain, w_in=w_in, conv_w=conv_w, conv_b=conv_b, dt_bias=dt_bias, a_log=a_log, d_skip=d_skip, out_gain=out_gain, w_out=w_out)


@jax.custom_vjp
def low(v):
    return lax.optimization_barrier(v.astype(jnp.bfloat16)).astype(jnp.float32)

@jax.custom_vjp
def low_back(v):
    return v

def low_keep(v):
    return (low(v), None)

def low_pass(kept, grad):
    return (grad,)

def back_keep(v):
    return (v, None)

def back_low(kept, grad):
    return (low(grad),)
low.defvjp(low_keep, low_pass)
low_back.defvjp(back_keep, back_low)
epsilon = 1e-05
highest = lax.Precision.HIGHEST

def rms_scale(values, gain):
    return values * lax.rsqrt(lax.optimization_barrier(jnp.mean(values * values, axis=-1, keepdims=True)) + epsilon) * gain

def block_step(hidden_state, pieces):
    xs_block, b_block, c_block, decay_block, step_block = pieces
    length_q = decay_block.shape[0]
    cumulated = jnp.cumsum(decay_block, axis=0)
    causal_mask = (jnp.arange(length_q)[:, None] >= jnp.arange(length_q)[None, :])[None]
    differ = cumulated.T[:, :, None] - cumulated.T[:, None, :]
    kernel = jnp.where(causal_mask, jnp.exp(jnp.where(causal_mask, differ, 0.0)), 0.0)
    affinity = jnp.dot(c_block, b_block.T, precision=highest)
    mixing = kernel * affinity[None] * step_block.T[:, None, :]
    within = jnp.einsum('hts,shp->thp', mixing, xs_block, precision=highest)
    carried = jnp.einsum('tn,hpn->thp', c_block, hidden_state, precision=highest) * jnp.exp(cumulated)[:, :, None]
    remaining = jnp.exp(cumulated[-1:] - cumulated) * step_block
    new_state = jnp.exp(cumulated[-1])[:, None, None] * hidden_state + jnp.einsum('sh,shp,sn->hpn', remaining, xs_block, b_block, precision=highest)
    return (new_state, within + carried)

def mixer(projected, conv_w, conv_b, dt_bias, a_log, d_skip, out_gain):
    length_t = projected.shape[0]
    gate_part = projected[:, :DI]
    conv_part = projected[:, DI:DI + CONV_CH]
    step_raw = projected[:, DI + CONV_CH:]
    padded = jnp.pad(conv_part, ((KW - 1, 0), (0, 0)))
    convolved = conv_b[None, :] + jnp.zeros_like(conv_part)
    for offset in range(KW):
        convolved = convolved + conv_w[offset][None, :] * padded[offset:offset + length_t]
    activated = jax.nn.silu(convolved)
    xs_all = activated[:, :DI].reshape(length_t, NH, HEAD)
    b_all = activated[:, DI:DI + NSTATE]
    c_all = activated[:, DI + NSTATE:]
    step_all = jax.nn.softplus(step_raw + dt_bias)
    decay_all = -jnp.exp(a_log) * step_all
    blocks = length_t // SPAN

    def into_blocks(values):
        return values.reshape((blocks, SPAN) + values.shape[1:])
    initial = jnp.zeros((NH, HEAD, NSTATE), jnp.float32)
    final_state, scanned = lax.scan(jax.checkpoint(block_step), initial, (into_blocks(xs_all), into_blocks(b_all), into_blocks(c_all), into_blocks(decay_all), into_blocks(step_all)))
    outputs_ssm = scanned.reshape(length_t, NH, HEAD) + d_skip[:, None] * xs_all
    gated = outputs_ssm.reshape(length_t, DI) * jax.nn.silu(gate_part)
    return rms_scale(gated, out_gain)

def one_layer(stream, in_gain, w_in, conv_w, conv_b, dt_bias, a_log, d_skip, out_gain, w_out):
    normed = low(rms_scale(stream, in_gain))
    projected = low_back(jnp.dot(normed, w_in, precision=highest))
    mixed = low(mixer(projected, conv_w, conv_b, dt_bias, a_log, d_skip, out_gain))
    branch = low_back(jnp.dot(mixed, w_out, precision=highest))
    return stream + branch

def reference(tokens, cotangent, lengths, dealing, in_gain, w_in, conv_w, conv_b, dt_bias, a_log, d_skip, out_gain, w_out):
    slot_count = tokens.shape[2]
    row_lengths = lengths[dealing]
    valid_slots = (jnp.arange(slot_count)[None, :] < row_lengths[:, None]).astype(jnp.float32)
    flat_tokens = tokens.reshape(SEQS, slot_count, D).astype(jnp.float32)
    flat_cotangent = cotangent.reshape(SEQS, slot_count, D).astype(jnp.float32)
    weights = (in_gain.astype(jnp.float32), w_in.astype(jnp.float32), conv_w.astype(jnp.float32), conv_b.astype(jnp.float32), dt_bias.astype(jnp.float32), a_log.astype(jnp.float32), d_skip.astype(jnp.float32), out_gain.astype(jnp.float32), w_out.astype(jnp.float32))

    def forward(inputs, *params):

        def per_row(pieces):
            stream, valid_row = pieces
            for layer_id in range(LAYERS):
                stream = one_layer(stream, *[member[layer_id] for member in params])
            return stream * valid_row[:, None]
        return lax.map(jax.checkpoint(per_row), (inputs, valid_slots))
    results, pull = jax.vjp(forward, flat_tokens, *weights)
    grads = pull(flat_cotangent)
    shaped = (MICRO, SEQS // MICRO, slot_count, D)
    return (results.reshape(shaped).astype(jnp.bfloat16), grads[0].reshape(shaped), grads[1], grads[2], grads[3], grads[4], grads[5], grads[6], grads[7], grads[8], grads[9])
```

```python
import jax
import jax.numpy as jnp
from jax import lax
from jax.experimental import pallas as pl
from jax.experimental.pallas import tpu as pltpu
from jax.sharding import PartitionSpec as P

D = 768
DI = 1536
NH = 24
HEAD = 64
NSTATE = 128
KW = 4
CONV_CH = 1792
NIN = 3352
LAYERS = 2
MICRO = 2
CH = 128
PAIRS = NH // 2
LANE = 128
DUP = 32
LOG2E = 1.4426950408889634

epsilon = 1e-05
f32 = jnp.float32
bf16 = jnp.bfloat16
highest = lax.Precision.HIGHEST


def mm(a, b):
    return jnp.dot(a, b, preferred_element_type=f32)


def mm_t(a, b):
    return lax.dot_general(a, b, (((1,), (1,)), ((), ())), preferred_element_type=f32)


def t_mm(a, b):
    return lax.dot_general(a, b, (((0,), (0,)), ((), ())), preferred_element_type=f32)


def sigmoid(v):
    return 0.5 * jnp.tanh(0.5 * v) + 0.5


def softplus(v):
    return jnp.maximum(v, 0.0) + jnp.log1p(jnp.exp(-jnp.abs(v)))


def lanes(j, base=0):
    return slice(base + LANE * j, base + LANE * (j + 1))


def split_pair(v):
    left = lax.broadcasted_iota(jnp.int32, v.shape, 1) < HEAD
    zero = jnp.zeros_like(v)
    return jnp.concatenate([jnp.where(left, v, zero), jnp.where(left, zero, v)], axis=0)


def high_low(v):
    high = v.astype(bf16)
    return high, (v - high.astype(f32)).astype(bf16)


def widen(v, spread):
    high, low = high_low(v)
    first = lax.broadcasted_iota(jnp.int32, v.shape, 1) < DUP
    return mm(jnp.where(first, high, low), spread)


def step_parts(proj_ref, raw_ref, head_ref):
    raw = proj_ref[:, DI + CONV_CH :]
    raw_ref[:, 0:NH] = raw
    raw_ref[:, DUP : DUP + NH] = raw
    shifted = raw_ref[...] + head_ref[0:1]
    step = softplus(shifted)
    rows = lax.broadcasted_iota(jnp.int32, (CH, CH), 0)
    cols = lax.broadcasted_iota(jnp.int32, (CH, CH), 1)
    lower = (cols <= rows).astype(f32)
    cum = jnp.dot(lower, head_ref[1:2] * step, precision=highest, preferred_element_type=f32)
    grow = jnp.exp2(cum)
    remain = jnp.exp2(cum[CH - 1 : CH] - cum)
    return shifted, step, cum, cum.T, grow, remain, rows, cols


def conv_block(ext_ref, conv_ref, j):
    total = conv_ref[4:5, lanes(j)]
    for k in range(KW):
        total = total + conv_ref[k : k + 1, lanes(j)] * ext_ref[5 + k : 5 + k + CH, lanes(j)]
    return total


def forward_kernel(
    proj_ref, conv_ref, head_ref, wide_ref, spread_ref,
    mixed_ref, scan_ref, saved_ref,
    ext_ref, raw_ref, state_ref, gated_ref, keep_ref,
):
    @pl.when(pl.program_id(1) == 0)
    def _():
        state_ref[...] = jnp.zeros_like(state_ref)
        ext_ref[0:8] = jnp.zeros_like(ext_ref[0:8])

    @pl.when((pl.program_id(0) == 0) & (pl.program_id(1) == 0))
    def _():
        raw_ref[...] = jnp.zeros_like(raw_ref)

    ext_ref[8 : 8 + CH] = proj_ref[:, DI : DI + CONV_CH]
    shifted, step, cum, cum_t, grow, remain, rows, cols = step_parts(proj_ref, raw_ref, head_ref)
    spread = spread_ref[...]
    step_w = widen(step, spread)
    grow_w = widen(grow, spread)
    remain_w = widen(remain * step, spread)

    def activated(j):
        value = conv_block(ext_ref, conv_ref, j)
        return value * sigmoid(value)

    b_low = activated(PAIRS).astype(bf16)
    c_low = activated(PAIRS + 1).astype(bf16)
    affinity = jnp.where(cols <= rows, mm_t(c_low, b_low), 0.0)
    state_low = state_ref[...].astype(bf16)
    saved_ref[...] = state_low
    carried = grow_w * mm(c_low, state_low)
    square = jnp.zeros((CH, LANE), f32)
    for j in range(PAIRS):
        xs = activated(j)
        mixing = []
        for h in (2 * j, 2 * j + 1):
            differ = jnp.minimum(cum[:, h : h + 1] - cum_t[h : h + 1], 0.0)
            mixing.append((jnp.exp2(differ) * affinity).astype(bf16))
        keep_ref[:, lanes(j)] = (xs * remain_w[:, lanes(j)]).astype(bf16)
        x_split = split_pair((xs * step_w[:, lanes(j)]).astype(bf16))
        scanned = mm(jnp.concatenate(mixing, axis=1), x_split) + carried[:, lanes(j)]
        scan_ref[:, lanes(j)] = scanned
        gate = proj_ref[:, lanes(j)]
        gated = (scanned + wide_ref[0:1, lanes(j)] * xs) * (gate * sigmoid(gate))
        gated_ref[:, lanes(j)] = gated
        square = square + gated * gated
    state_ref[...] = grow_w[CH - 1 : CH] * state_ref[...] + t_mm(b_low, keep_ref[...])
    scale = lax.rsqrt(jnp.sum(square, axis=1, keepdims=True) * (1.0 / DI) + epsilon)
    mixed_ref[...] = (gated_ref[...] * scale * wide_ref[1:2]).astype(bf16)
    ext_ref[0:8] = ext_ref[CH : CH + 8]


def backward_kernel(
    proj_ref, tail_ref, scan_ref, saved_ref, grad_ref, conv_ref, head_ref, wide_ref, spread_ref, gather_ref,
    out_ref, sum_ref,
    ext_ref, raw_ref, state_ref, act_ref, slope_ref, gate_ref, dconv_ref, keep_ref, grown_ref, high_ref, low_ref, step_ref, row_ref,
):
    chunk = pl.num_programs(1) - 1 - pl.program_id(1)

    @pl.when(pl.program_id(1) == 0)
    def _():
        state_ref[...] = jnp.zeros_like(state_ref)
        dconv_ref[CH : CH + 8] = jnp.zeros_like(dconv_ref[CH : CH + 8])

    @pl.when((pl.program_id(0) == 0) & (pl.program_id(1) == 0))
    def _():
        raw_ref[...] = jnp.zeros_like(raw_ref)
        row_ref[...] = jnp.zeros_like(row_ref)
        sum_ref[...] = jnp.zeros_like(sum_ref)

    ext_ref[0:8] = jnp.where(chunk > 0, tail_ref[:, DI : DI + CONV_CH], 0.0)
    ext_ref[8 : 8 + CH] = proj_ref[:, DI : DI + CONV_CH]
    shifted, step, cum, cum_t, grow, remain, rows, cols = step_parts(proj_ref, raw_ref, head_ref)
    spread = spread_ref[...]
    step_w = widen(step, spread)
    grow_w = widen(grow, spread)
    remain_w = widen(remain, spread)

    square = jnp.zeros((CH, LANE), f32)
    along = jnp.zeros((CH, LANE), f32)
    for j in range(PAIRS + 2):
        value = conv_block(ext_ref, conv_ref, j)
        share = sigmoid(value)
        xs = value * share
        act_ref[:, lanes(j)] = xs
        slope_ref[:, lanes(j)] = share + xs * (1.0 - share)
        if j < PAIRS:
            gate = proj_ref[:, lanes(j)]
            open_share = sigmoid(gate)
            gate_ref[:, lanes(j)] = open_share
            gated = (scan_ref[:, lanes(j)] + wide_ref[0:1, lanes(j)] * xs) * (gate * open_share)
            square = square + gated * gated
            along = along + gated * (grad_ref[:, lanes(j)].astype(f32) * wide_ref[1:2, lanes(j)])
    scale = lax.rsqrt(jnp.sum(square, axis=1, keepdims=True) * (1.0 / DI) + epsilon)
    pull = scale * scale * scale * (jnp.sum(along, axis=1, keepdims=True) * (1.0 / DI))

    b_low = act_ref[:, lanes(PAIRS)].astype(bf16)
    c_low = act_ref[:, lanes(PAIRS + 1)].astype(bf16)
    affinity_t = jnp.where(rows <= cols, mm_t(b_low, c_low), 0.0)
    state = state_ref[...]
    state_low = state.astype(bf16)
    row_ref[1:2] = jnp.sum(saved_ref[...].astype(f32) * state, axis=0, keepdims=True)
    back = remain_w * mm(b_low, state_low)
    affinity_grad = jnp.zeros((CH, CH), f32)
    for j in range(PAIRS):
        xs = act_ref[:, lanes(j)]
        skip = wide_ref[0:1, lanes(j)]
        grad = grad_ref[:, lanes(j)].astype(f32)
        gate = proj_ref[:, lanes(j)]
        open_share = gate_ref[:, lanes(j)]
        opened = gate * open_share
        scanned = scan_ref[:, lanes(j)]
        outer = scanned + skip * xs
        gated = outer * opened
        gated_grad = scale * (grad * wide_ref[1:2, lanes(j)]) - pull * gated
        sum_ref[6:7, lanes(j)] += jnp.sum(grad * (gated * scale), axis=0, keepdims=True)
        dy = gated_grad * opened
        out_ref[:, lanes(j)] = (gated_grad * outer * (open_share + opened * (1.0 - open_share))).astype(bf16)
        sum_ref[5:6, lanes(j)] += jnp.sum(dy * xs, axis=0, keepdims=True)
        dy_low = dy.astype(bf16)
        grown_ref[:, lanes(j)] = (grow_w[:, lanes(j)] * dy).astype(bf16)
        scaled = xs * step_w[:, lanes(j)]
        x_low = scaled.astype(bf16)
        keep_ref[:, lanes(j)] = (scaled * remain_w[:, lanes(j)]).astype(bf16)
        dy_split = split_pair(dy_low)
        kernels = []
        for h in (2 * j, 2 * j + 1):
            differ = jnp.minimum(cum_t[h : h + 1] - cum[:, h : h + 1], 0.0)
            kernels.append(jnp.exp2(differ))
        mixing_t = jnp.concatenate([(k * affinity_t).astype(bf16) for k in kernels], axis=1)
        arrived = back[:, lanes(j)]
        x_grad = mm(mixing_t, dy_split) + arrived
        mixing_grad = mm_t(x_low, dy_split)
        affinity_grad = affinity_grad + mixing_grad[:, :CH] * kernels[0] + mixing_grad[:, CH:] * kernels[1]
        x_back = x_low.astype(f32)
        row_ref[0:1, lanes(j)] = jnp.sum(x_back * arrived, axis=0, keepdims=True)
        high, low = high_low(dy_low.astype(f32) * scanned - x_back * x_grad)
        high_ref[:, lanes(j)] = high
        low_ref[:, lanes(j)] = low
        step_ref[:, lanes(j)] = (x_grad * xs).astype(bf16)
        dconv_ref[0:CH, lanes(j)] = (step_w[:, lanes(j)] * x_grad + skip * dy) * slope_ref[:, lanes(j)]
    affinity_low = jnp.where(rows <= cols, affinity_grad, 0.0).astype(bf16)
    grown = grown_ref[...]
    b_grad = mm(affinity_low, c_low) + mm_t(keep_ref[...], state_low)
    c_grad = t_mm(affinity_low, b_low) + mm_t(grown, saved_ref[...])
    dconv_ref[0:CH, lanes(PAIRS)] = b_grad * slope_ref[:, lanes(PAIRS)]
    dconv_ref[0:CH, lanes(PAIRS + 1)] = c_grad * slope_ref[:, lanes(PAIRS + 1)]

    gather = gather_ref[...]
    row_high, row_low = high_low(row_ref[...])
    row_sums = mm(row_high, gather) + mm(row_low, gather)
    last_grad = row_sums[0:1] + grow[CH - 1 : CH] * row_sums[1:2]
    cum_grad = mm(high_ref[...], gather) + mm(low_ref[...], gather)
    upper = (cols >= rows).astype(f32)
    decay_grad = jnp.dot(upper, cum_grad, precision=highest, preferred_element_type=f32) + last_grad
    step_grad = mm(step_ref[...], gather) + head_ref[2:3] * decay_grad
    raw_grad = step_grad * sigmoid(shifted)
    out_ref[:, DI + CONV_CH :] = raw_grad[:, :NH].astype(bf16)
    sum_ref[7:8, 0:LANE] += jnp.sum(raw_grad, axis=0, keepdims=True)
    sum_ref[7:8, LANE : 2 * LANE] += jnp.sum(decay_grad * step, axis=0, keepdims=True)
    state_ref[...] = grow_w[CH - 1 : CH] * state + t_mm(c_low, grown)

    for j in range(PAIRS + 2):
        total = conv_ref[3:4, lanes(j)] * dconv_ref[0:CH, lanes(j)]
        for k in range(KW - 1):
            total = total + conv_ref[k : k + 1, lanes(j)] * dconv_ref[3 - k : 3 - k + CH, lanes(j)]
        out_ref[:, lanes(j, DI)] = total.astype(bf16)
        here = dconv_ref[0:CH, lanes(j)]
        for k in range(KW):
            sum_ref[k : k + 1, lanes(j)] += jnp.sum(here * ext_ref[5 + k : 5 + k + CH, lanes(j)], axis=0, keepdims=True)
        sum_ref[4:5, lanes(j)] += jnp.sum(here, axis=0, keepdims=True)
    dconv_ref[CH : CH + 8] = dconv_ref[0:8]


def fixed(shape):
    return pl.BlockSpec(shape, lambda r, c: (0,) * len(shape))


def mixer_forward(projected, tables, chunks):
    tokens = projected.shape[0]
    conv_t, head_t, wide_t, spread, _ = tables
    block = lambda r, c: (r * chunks + c, 0)
    return pl.pallas_call(
        forward_kernel,
        grid=(tokens // (chunks * CH), chunks),
        in_specs=[
            pl.BlockSpec((CH, NIN), block),
            fixed((8, CONV_CH)),
            fixed((8, LANE)),
            fixed((8, DI)),
            fixed((LANE, DI)),
        ],
        out_specs=[
            pl.BlockSpec((CH, DI), block),
            pl.BlockSpec((CH, DI), block),
            pl.BlockSpec((NSTATE, DI), block),
        ],
        out_shape=[
            jax.ShapeDtypeStruct((tokens, DI), bf16),
            jax.ShapeDtypeStruct((tokens, DI), f32),
            jax.ShapeDtypeStruct((tokens // CH * NSTATE, DI), bf16),
        ],
        scratch_shapes=[
            pltpu.VMEM((CH + 8, CONV_CH), f32),
            pltpu.VMEM((CH, LANE), f32),
            pltpu.VMEM((NSTATE, DI), f32),
            pltpu.VMEM((CH, DI), f32),
            pltpu.VMEM((CH, DI), bf16),
        ],
        compiler_params=pltpu.CompilerParams(
            dimension_semantics=("arbitrary", "arbitrary"), vmem_limit_bytes=48 * 2**20
        ),
        name="mixer_forward",
    )(projected, conv_t, head_t, wide_t, spread)


def mixer_backward(projected, scanned, saved, mixed_grad, tables, chunks):
    tokens = projected.shape[0]
    conv_t, head_t, wide_t, spread, gather = tables
    block = lambda r, c: (r * chunks + chunks - 1 - c, 0)
    ahead = lambda r, c: (jnp.maximum((r * chunks + chunks - 1 - c) * (CH // 8) - 1, 0), 0)
    return pl.pallas_call(
        backward_kernel,
        grid=(tokens // (chunks * CH), chunks),
        in_specs=[
            pl.BlockSpec((CH, NIN), block),
            pl.BlockSpec((8, NIN), ahead),
            pl.BlockSpec((CH, DI), block),
            pl.BlockSpec((NSTATE, DI), block),
            pl.BlockSpec((CH, DI), block),
            fixed((8, CONV_CH)),
            fixed((8, LANE)),
            fixed((8, DI)),
            fixed((LANE, DI)),
            fixed((DI, LANE)),
        ],
        out_specs=[
            pl.BlockSpec((CH, NIN), block),
            fixed((8, CONV_CH)),
        ],
        out_shape=[
            jax.ShapeDtypeStruct((tokens, NIN), bf16),
            jax.ShapeDtypeStruct((8, CONV_CH), f32),
        ],
        scratch_shapes=[
            pltpu.VMEM((CH + 8, CONV_CH), f32),
            pltpu.VMEM((CH, LANE), f32),
            pltpu.VMEM((NSTATE, DI), f32),
            pltpu.VMEM((CH, CONV_CH), f32),
            pltpu.VMEM((CH, CONV_CH), f32),
            pltpu.VMEM((CH, DI), f32),
            pltpu.VMEM((CH + 8, CONV_CH), f32),
            pltpu.VMEM((CH, DI), bf16),
            pltpu.VMEM((CH, DI), bf16),
            pltpu.VMEM((CH, DI), bf16),
            pltpu.VMEM((CH, DI), bf16),
            pltpu.VMEM((CH, DI), bf16),
            pltpu.VMEM((8, DI), f32),
        ],
        compiler_params=pltpu.CompilerParams(
            dimension_semantics=("arbitrary", "arbitrary"), vmem_limit_bytes=48 * 2**20
        ),
        name="mixer_backward",
    )(projected, projected, scanned, saved, mixed_grad, conv_t, head_t, wide_t, spread, gather)


def twice(v):
    return jnp.pad(jnp.concatenate([jnp.pad(v, (0, DUP - NH)), v]), (0, LANE - DUP - NH))


def mixer_tables(conv_w, conv_b, dt_bias, a_log, d_skip, out_gain):
    head = jnp.arange(DI) // HEAD
    column = jnp.arange(LANE)[:, None]
    spread = ((column % DUP == head[None]) & (column < 2 * DUP)).astype(bf16)
    rate = -jnp.exp(a_log)
    conv_t = jnp.concatenate([conv_w, conv_b[None], jnp.zeros((3, CONV_CH), f32)])
    head_t = jnp.concatenate(
        [jnp.stack([twice(dt_bias), twice(rate * LOG2E), twice(rate)]), jnp.zeros((5, LANE), f32)]
    )
    wide_t = jnp.concatenate([jnp.stack([jnp.repeat(d_skip, HEAD), out_gain]), jnp.zeros((6, DI), f32)])
    return conv_t, head_t, wide_t, spread, spread.T


def norm_parts(stream):
    return lax.rsqrt(jnp.mean(stream * stream, axis=-1, keepdims=True) + epsilon)


def shards(
    tokens, cotangent, lengths, dealing, in_gain, w_in, conv_w, conv_b, dt_bias, a_log, d_skip, out_gain, w_out,
):
    shard_count = lax.axis_size("shard")
    row_total = lax.axis_size("replica") * shard_count
    row_index = lax.axis_index("replica") * shard_count + lax.axis_index("shard")
    slot_count = tokens.shape[2]
    chunks = slot_count // CH
    token_count = MICRO * slot_count
    full_in = [lax.all_gather(w_in[l], "shard", axis=0, tiled=True) for l in range(LAYERS)]
    full_out = [lax.all_gather(w_out[l], "shard", axis=0, tiled=True) for l in range(LAYERS)]
    global_rows = jnp.arange(MICRO) * row_total + row_index
    sequence = jnp.sum(jnp.where(jnp.arange(dealing.shape[0])[None] == global_rows[:, None], dealing[None], 0), axis=1)
    seq_length = jnp.sum(jnp.where(jnp.arange(lengths.shape[0])[None] == sequence[:, None], lengths[None], 0), axis=1)
    valid = (jnp.arange(slot_count)[None] < seq_length[:, None]).astype(f32).reshape(token_count, 1)

    stream = tokens.reshape(token_count, D).astype(f32)
    saved = []
    for l in range(LAYERS):
        normed = (stream * norm_parts(stream) * in_gain[l]).astype(bf16)
        projected = mm(normed, full_in[l])
        tables = mixer_tables(conv_w[l], conv_b[l], dt_bias[l], a_log[l], d_skip[l], out_gain[l])
        mixed, scanned, states = mixer_forward(projected, tables, chunks)
        saved.append((stream, normed, projected, tables, mixed, scanned, states))
        stream = stream + mm(mixed, full_out[l])
    result = (stream * valid).astype(bf16)

    upstream = cotangent.reshape(token_count, D).astype(f32) * valid
    in_grads = [None] * LAYERS
    out_grads = [None] * LAYERS
    gain_grads = [None] * LAYERS
    sums = [None] * LAYERS
    for l in reversed(range(LAYERS)):
        entered, normed, projected, tables, mixed, scanned, states = saved[l]
        branch_grad = upstream.astype(bf16)
        out_grads[l] = lax.psum_scatter(t_mm(mixed, branch_grad).astype(bf16), "shard", scatter_dimension=0, tiled=True)
        mixed_grad = mm_t(branch_grad, full_out[l]).astype(bf16)
        project_grad, sums[l] = mixer_backward(projected, scanned, states, mixed_grad, tables, chunks)
        in_grads[l] = lax.psum_scatter(t_mm(normed, project_grad).astype(bf16), "shard", scatter_dimension=0, tiled=True)
        normed_grad = mm_t(project_grad, full_in[l])
        scale = norm_parts(entered)
        gain_grads[l] = jnp.sum(normed_grad * entered * scale, axis=0)
        inner = normed_grad * in_gain[l]
        pull = scale * scale * scale * jnp.mean(inner * entered, axis=-1, keepdims=True)
        upstream = upstream + scale * inner - pull * entered
    in_total = lax.psum(jnp.stack(in_grads).astype(f32), "replica")
    out_total = lax.psum(jnp.stack(out_grads).astype(f32), "replica")
    small, gain_total = lax.psum((jnp.stack(sums), jnp.stack(gain_grads)), ("replica", "shard"))
    rate = -jnp.exp(a_log)
    shape = (MICRO, 1, slot_count, D)
    return (
        result.reshape(shape),
        upstream.reshape(shape),
        gain_total,
        in_total,
        small[:, 0:4],
        small[:, 4],
        small[:, 7, 0:NH],
        small[:, 7, LANE : LANE + NH] * rate,
        small[:, 5, :DI].reshape(LAYERS, NH, HEAD).sum(-1),
        small[:, 6, :DI],
        out_total,
    )


def solution(mesh):
    rows = P(None, ("replica", "shard"), None, None)
    split = P(None, "shard", None)
    in_specs = (rows, rows, P(), P(), P(), split, P(), P(), P(), P(), P(), P(), split)
    out_specs = (rows, rows, P(), split, P(), P(), P(), P(), P(), P(), split)
    return jax.shard_map(shards, mesh=mesh, in_specs=in_specs, out_specs=out_specs, check_vma=False)
```

```python
import jax
import jax.numpy as jnp
from jax import lax
from jax.experimental import pallas as pl
from jax.experimental.pallas import tpu as pltpu
from jax.sharding import PartitionSpec as P

D = 768
DI = 1536
NH = 24
HEAD = 64
NSTATE = 128
KW = 4
CONV_CH = 1792
NIN = 3352
LAYERS = 2
MICRO = 2
CH = 128
PAIRS = NH // 2
LANE = 128
DUP = 32
LOG2E = 1.4426950408889634

epsilon = 1e-05
f32 = jnp.float32
bf16 = jnp.bfloat16
highest = lax.Precision.HIGHEST
MESH = pl.DeviceIdType.MESH


def mm(a, b):
    return jnp.dot(a, b, preferred_element_type=f32)


def mm_t(a, b):
    return lax.dot_general(a, b, (((1,), (1,)), ((), ())), preferred_element_type=f32)


def t_mm(a, b):
    return lax.dot_general(a, b, (((0,), (0,)), ((), ())), preferred_element_type=f32)


def sigmoid(v):
    return 0.5 * jnp.tanh(0.5 * v) + 0.5


def softplus(v):
    return jnp.maximum(v, 0.0) + jnp.log1p(jnp.exp(-jnp.abs(v)))


def lanes(j, base=0):
    return slice(base + LANE * j, base + LANE * (j + 1))


def split_pair(v):
    left = lax.broadcasted_iota(jnp.int32, v.shape, 1) < HEAD
    zero = jnp.zeros_like(v)
    return jnp.concatenate([jnp.where(left, v, zero), jnp.where(left, zero, v)], axis=0)


def high_low(v):
    high = v.astype(bf16)
    return high, (v - high.astype(f32)).astype(bf16)


def widen(v, spread):
    high, low = high_low(v)
    first = lax.broadcasted_iota(jnp.int32, v.shape, 1) < DUP
    return mm(jnp.where(first, high, low), spread)


def step_parts(proj_ref, raw_ref, head_ref):
    raw = proj_ref[:, DI + CONV_CH :]
    raw_ref[:, 0:NH] = raw
    raw_ref[:, DUP : DUP + NH] = raw
    shifted = raw_ref[...] + head_ref[0:1]
    step = softplus(shifted)
    rows = lax.broadcasted_iota(jnp.int32, (CH, CH), 0)
    cols = lax.broadcasted_iota(jnp.int32, (CH, CH), 1)
    lower = (cols <= rows).astype(f32)
    cum = jnp.dot(lower, head_ref[1:2] * step, precision=highest, preferred_element_type=f32)
    grow = jnp.exp2(cum)
    remain = jnp.exp2(cum[CH - 1 : CH] - cum)
    return shifted, step, cum, cum.T, grow, remain, rows, cols


def conv_block(ext_ref, conv_ref, j):
    total = conv_ref[4:5, lanes(j)]
    for k in range(KW):
        total = total + conv_ref[k : k + 1, lanes(j)] * ext_ref[5 + k : 5 + k + CH, lanes(j)]
    return total


def forward_kernel(
    proj_ref, conv_ref, head_ref, wide_ref, spread_ref,
    mixed_ref, scan_ref, saved_ref,
    ext_ref, raw_ref, state_ref, gated_ref, keep_ref,
):
    @pl.when(pl.program_id(1) == 0)
    def _():
        state_ref[...] = jnp.zeros_like(state_ref)
        ext_ref[0:8] = jnp.zeros_like(ext_ref[0:8])

    @pl.when((pl.program_id(0) == 0) & (pl.program_id(1) == 0))
    def _():
        raw_ref[...] = jnp.zeros_like(raw_ref)

    ext_ref[8 : 8 + CH] = proj_ref[:, DI : DI + CONV_CH]
    shifted, step, cum, cum_t, grow, remain, rows, cols = step_parts(proj_ref, raw_ref, head_ref)
    spread = spread_ref[...]
    step_w = widen(step, spread)
    grow_w = widen(grow, spread)
    remain_w = widen(remain * step, spread)

    def activated(j):
        value = conv_block(ext_ref, conv_ref, j)
        return value * sigmoid(value)

    b_low = activated(PAIRS).astype(bf16)
    c_low = activated(PAIRS + 1).astype(bf16)
    affinity = jnp.where(cols <= rows, mm_t(c_low, b_low), 0.0)
    state_low = state_ref[...].astype(bf16)
    saved_ref[...] = state_low
    carried = grow_w * mm(c_low, state_low)
    square = jnp.zeros((CH, LANE), f32)
    for j in range(PAIRS):
        xs = activated(j)
        mixing = []
        for h in (2 * j, 2 * j + 1):
            differ = jnp.minimum(cum[:, h : h + 1] - cum_t[h : h + 1], 0.0)
            mixing.append((jnp.exp2(differ) * affinity).astype(bf16))
        keep_ref[:, lanes(j)] = (xs * remain_w[:, lanes(j)]).astype(bf16)
        x_split = split_pair((xs * step_w[:, lanes(j)]).astype(bf16))
        scanned = mm(jnp.concatenate(mixing, axis=1), x_split) + carried[:, lanes(j)]
        scan_ref[:, lanes(j)] = scanned
        gate = proj_ref[:, lanes(j)]
        gated = (scanned + wide_ref[0:1, lanes(j)] * xs) * (gate * sigmoid(gate))
        gated_ref[:, lanes(j)] = gated
        square = square + gated * gated
    state_ref[...] = grow_w[CH - 1 : CH] * state_ref[...] + t_mm(b_low, keep_ref[...])
    scale = lax.rsqrt(jnp.sum(square, axis=1, keepdims=True) * (1.0 / DI) + epsilon)
    mixed_ref[...] = (gated_ref[...] * scale * wide_ref[1:2]).astype(bf16)
    ext_ref[0:8] = ext_ref[CH : CH + 8]


def backward_kernel(
    proj_ref, tail_ref, scan_ref, saved_ref, grad_ref, conv_ref, head_ref, wide_ref, spread_ref, gather_ref,
    out_ref, sum_ref,
    ext_ref, raw_ref, state_ref, act_ref, slope_ref, gate_ref, dconv_ref, keep_ref, grown_ref, high_ref, low_ref, step_ref, row_ref,
):
    chunk = pl.num_programs(1) - 1 - pl.program_id(1)

    @pl.when(pl.program_id(1) == 0)
    def _():
        state_ref[...] = jnp.zeros_like(state_ref)
        dconv_ref[CH : CH + 8] = jnp.zeros_like(dconv_ref[CH : CH + 8])

    @pl.when((pl.program_id(0) == 0) & (pl.program_id(1) == 0))
    def _():
        raw_ref[...] = jnp.zeros_like(raw_ref)
        row_ref[...] = jnp.zeros_like(row_ref)
        sum_ref[...] = jnp.zeros_like(sum_ref)

    ext_ref[0:8] = jnp.where(chunk > 0, tail_ref[:, DI : DI + CONV_CH], 0.0)
    ext_ref[8 : 8 + CH] = proj_ref[:, DI : DI + CONV_CH]
    shifted, step, cum, cum_t, grow, remain, rows, cols = step_parts(proj_ref, raw_ref, head_ref)
    spread = spread_ref[...]
    step_w = widen(step, spread)
    grow_w = widen(grow, spread)
    remain_w = widen(remain, spread)

    square = jnp.zeros((CH, LANE), f32)
    along = jnp.zeros((CH, LANE), f32)
    for j in range(PAIRS + 2):
        value = conv_block(ext_ref, conv_ref, j)
        share = sigmoid(value)
        xs = value * share
        act_ref[:, lanes(j)] = xs
        slope_ref[:, lanes(j)] = share + xs * (1.0 - share)
        if j < PAIRS:
            gate = proj_ref[:, lanes(j)]
            open_share = sigmoid(gate)
            gate_ref[:, lanes(j)] = open_share
            gated = (scan_ref[:, lanes(j)] + wide_ref[0:1, lanes(j)] * xs) * (gate * open_share)
            square = square + gated * gated
            along = along + gated * (grad_ref[:, lanes(j)].astype(f32) * wide_ref[1:2, lanes(j)])
    scale = lax.rsqrt(jnp.sum(square, axis=1, keepdims=True) * (1.0 / DI) + epsilon)
    pull = scale * scale * scale * (jnp.sum(along, axis=1, keepdims=True) * (1.0 / DI))

    b_low = act_ref[:, lanes(PAIRS)].astype(bf16)
    c_low = act_ref[:, lanes(PAIRS + 1)].astype(bf16)
    affinity_t = jnp.where(rows <= cols, mm_t(b_low, c_low), 0.0)
    state = state_ref[...]
    state_low = state.astype(bf16)
    row_ref[1:2] = jnp.sum(saved_ref[...].astype(f32) * state, axis=0, keepdims=True)
    back = remain_w * mm(b_low, state_low)
    affinity_grad = jnp.zeros((CH, CH), f32)
    for j in range(PAIRS):
        xs = act_ref[:, lanes(j)]
        skip = wide_ref[0:1, lanes(j)]
        grad = grad_ref[:, lanes(j)].astype(f32)
        gate = proj_ref[:, lanes(j)]
        open_share = gate_ref[:, lanes(j)]
        opened = gate * open_share
        scanned = scan_ref[:, lanes(j)]
        outer = scanned + skip * xs
        gated = outer * opened
        gated_grad = scale * (grad * wide_ref[1:2, lanes(j)]) - pull * gated
        sum_ref[6:7, lanes(j)] += jnp.sum(grad * (gated * scale), axis=0, keepdims=True)
        dy = gated_grad * opened
        out_ref[:, lanes(j)] = (gated_grad * outer * (open_share + opened * (1.0 - open_share))).astype(bf16)
        sum_ref[5:6, lanes(j)] += jnp.sum(dy * xs, axis=0, keepdims=True)
        dy_low = dy.astype(bf16)
        grown_ref[:, lanes(j)] = (grow_w[:, lanes(j)] * dy).astype(bf16)
        scaled = xs * step_w[:, lanes(j)]
        x_low = scaled.astype(bf16)
        keep_ref[:, lanes(j)] = (scaled * remain_w[:, lanes(j)]).astype(bf16)
        dy_split = split_pair(dy_low)
        kernels = []
        for h in (2 * j, 2 * j + 1):
            differ = jnp.minimum(cum_t[h : h + 1] - cum[:, h : h + 1], 0.0)
            kernels.append(jnp.exp2(differ))
        mixing_t = jnp.concatenate([(k * affinity_t).astype(bf16) for k in kernels], axis=1)
        arrived = back[:, lanes(j)]
        x_grad = mm(mixing_t, dy_split) + arrived
        mixing_grad = mm_t(x_low, dy_split)
        affinity_grad = affinity_grad + mixing_grad[:, :CH] * kernels[0] + mixing_grad[:, CH:] * kernels[1]
        x_back = x_low.astype(f32)
        row_ref[0:1, lanes(j)] = jnp.sum(x_back * arrived, axis=0, keepdims=True)
        high, low = high_low(dy_low.astype(f32) * scanned - x_back * x_grad)
        high_ref[:, lanes(j)] = high
        low_ref[:, lanes(j)] = low
        step_ref[:, lanes(j)] = (x_grad * xs).astype(bf16)
        dconv_ref[0:CH, lanes(j)] = (step_w[:, lanes(j)] * x_grad + skip * dy) * slope_ref[:, lanes(j)]
    affinity_low = jnp.where(rows <= cols, affinity_grad, 0.0).astype(bf16)
    grown = grown_ref[...]
    b_grad = mm(affinity_low, c_low) + mm_t(keep_ref[...], state_low)
    c_grad = t_mm(affinity_low, b_low) + mm_t(grown, saved_ref[...])
    dconv_ref[0:CH, lanes(PAIRS)] = b_grad * slope_ref[:, lanes(PAIRS)]
    dconv_ref[0:CH, lanes(PAIRS + 1)] = c_grad * slope_ref[:, lanes(PAIRS + 1)]

    gather = gather_ref[...]
    row_high, row_low = high_low(row_ref[...])
    row_sums = mm(row_high, gather) + mm(row_low, gather)
    last_grad = row_sums[0:1] + grow[CH - 1 : CH] * row_sums[1:2]
    cum_grad = mm(high_ref[...], gather) + mm(low_ref[...], gather)
    upper = (cols >= rows).astype(f32)
    decay_grad = jnp.dot(upper, cum_grad, precision=highest, preferred_element_type=f32) + last_grad
    step_grad = mm(step_ref[...], gather) + head_ref[2:3] * decay_grad
    raw_grad = step_grad * sigmoid(shifted)
    out_ref[:, DI + CONV_CH :] = raw_grad[:, :NH].astype(bf16)
    sum_ref[7:8, 0:LANE] += jnp.sum(raw_grad, axis=0, keepdims=True)
    sum_ref[7:8, LANE : 2 * LANE] += jnp.sum(decay_grad * step, axis=0, keepdims=True)
    state_ref[...] = grow_w[CH - 1 : CH] * state + t_mm(c_low, grown)

    for j in range(PAIRS + 2):
        total = conv_ref[3:4, lanes(j)] * dconv_ref[0:CH, lanes(j)]
        for k in range(KW - 1):
            total = total + conv_ref[k : k + 1, lanes(j)] * dconv_ref[3 - k : 3 - k + CH, lanes(j)]
        out_ref[:, lanes(j, DI)] = total.astype(bf16)
        here = dconv_ref[0:CH, lanes(j)]
        for k in range(KW):
            sum_ref[k : k + 1, lanes(j)] += jnp.sum(here * ext_ref[5 + k : 5 + k + CH, lanes(j)], axis=0, keepdims=True)
        sum_ref[4:5, lanes(j)] += jnp.sum(here, axis=0, keepdims=True)
    dconv_ref[CH : CH + 8] = dconv_ref[0:8]


def fixed(shape):
    return pl.BlockSpec(shape, lambda r, c: (0,) * len(shape))


def mixer_forward(projected, tables, chunks):
    tokens = projected.shape[0]
    conv_t, head_t, wide_t, spread, _ = tables
    block = lambda r, c: (r * chunks + c, 0)
    return pl.pallas_call(
        forward_kernel,
        grid=(tokens // (chunks * CH), chunks),
        in_specs=[
            pl.BlockSpec((CH, NIN), block),
            fixed((8, CONV_CH)),
            fixed((8, LANE)),
            fixed((8, DI)),
            fixed((LANE, DI)),
        ],
        out_specs=[
            pl.BlockSpec((CH, DI), block),
            pl.BlockSpec((CH, DI), block),
            pl.BlockSpec((NSTATE, DI), block),
        ],
        out_shape=[
            jax.ShapeDtypeStruct((tokens, DI), bf16),
            jax.ShapeDtypeStruct((tokens, DI), f32),
            jax.ShapeDtypeStruct((tokens // CH * NSTATE, DI), bf16),
        ],
        scratch_shapes=[
            pltpu.VMEM((CH + 8, CONV_CH), f32),
            pltpu.VMEM((CH, LANE), f32),
            pltpu.VMEM((NSTATE, DI), f32),
            pltpu.VMEM((CH, DI), f32),
            pltpu.VMEM((CH, DI), bf16),
        ],
        compiler_params=pltpu.CompilerParams(
            dimension_semantics=("arbitrary", "arbitrary"), vmem_limit_bytes=48 * 2**20
        ),
        name="mixer_forward",
    )(projected, conv_t, head_t, wide_t, spread)


def mixer_backward(projected, scanned, saved, mixed_grad, tables, chunks):
    tokens = projected.shape[0]
    conv_t, head_t, wide_t, spread, gather = tables
    block = lambda r, c: (r * chunks + chunks - 1 - c, 0)
    ahead = lambda r, c: (jnp.maximum((r * chunks + chunks - 1 - c) * (CH // 8) - 1, 0), 0)
    return pl.pallas_call(
        backward_kernel,
        grid=(tokens // (chunks * CH), chunks),
        in_specs=[
            pl.BlockSpec((CH, NIN), block),
            pl.BlockSpec((8, NIN), ahead),
            pl.BlockSpec((CH, DI), block),
            pl.BlockSpec((NSTATE, DI), block),
            pl.BlockSpec((CH, DI), block),
            fixed((8, CONV_CH)),
            fixed((8, LANE)),
            fixed((8, DI)),
            fixed((LANE, DI)),
            fixed((DI, LANE)),
        ],
        out_specs=[
            pl.BlockSpec((CH, NIN), block),
            fixed((8, CONV_CH)),
        ],
        out_shape=[
            jax.ShapeDtypeStruct((tokens, NIN), bf16),
            jax.ShapeDtypeStruct((8, CONV_CH), f32),
        ],
        scratch_shapes=[
            pltpu.VMEM((CH + 8, CONV_CH), f32),
            pltpu.VMEM((CH, LANE), f32),
            pltpu.VMEM((NSTATE, DI), f32),
            pltpu.VMEM((CH, CONV_CH), f32),
            pltpu.VMEM((CH, CONV_CH), f32),
            pltpu.VMEM((CH, DI), f32),
            pltpu.VMEM((CH + 8, CONV_CH), f32),
            pltpu.VMEM((CH, DI), bf16),
            pltpu.VMEM((CH, DI), bf16),
            pltpu.VMEM((CH, DI), bf16),
            pltpu.VMEM((CH, DI), bf16),
            pltpu.VMEM((CH, DI), bf16),
            pltpu.VMEM((8, DI), f32),
        ],
        compiler_params=pltpu.CompilerParams(
            dimension_semantics=("arbitrary", "arbitrary"), vmem_limit_bytes=48 * 2**20
        ),
        name="mixer_backward",
    )(projected, projected, scanned, saved, mixed_grad, conv_t, head_t, wide_t, spread, gather)


def ring_place(n):
    wide = n // 4
    me = lax.axis_index("shard")
    chip, core = me // 2, me % 2
    row, col = chip // wide, chip % wide
    place = row * col_last(wide, col) + (1 - row) * col
    def shard_of(p, c):
        p = p % (2 * wide)
        r = p // wide
        x = r * (2 * wide - 1 - p) + (1 - r) * p
        return (r * wide + x) * 2 + c
    return place, core, shard_of

def col_last(wide, col):
    return 2 * wide - 1 - col

def halves(rows):
    first = rows // 2 // 16 * 16
    return (0, first), (first, rows - first)

def gather_kernel(n, *refs):
    count = (len(refs) - 4) // 2
    parts, wholes = refs[:count], refs[count:2*count]
    send_sem, recv_sem, pair_sem, own_sem = refs[2*count:]
    half = n // 4
    place, core, shard_of = ring_place(n)
    right, left, pair = shard_of(place + 1, core), shard_of(place + n // 2 - 1, core), shard_of(place, 1 - core)
    barrier = pltpu.get_barrier_semaphore()
    for to in (right, left, pair):
        pl.semaphore_signal(barrier, inc=1, device_id={"shard": to}, device_id_type=MESH)
    pl.semaphore_wait(barrier, 3)
    def span(a, owner, part):
        rows = parts[a].shape[0]
        start, size = part
        return pl.ds(pl.multiple_of(owner * rows + start, 16), size)
    sent = []
    def send(a, src, owner, part, to, sems, k):
        rows = span(a, owner, part)
        c = pltpu.make_async_remote_copy(src_ref=src if src is not None else wholes[a].at[rows], dst_ref=wholes[a].at[rows],
            send_sem=sems[0], recv_sem=sems[1], device_id={"shard": to}, device_id_type=MESH)
        c.start(); sent.append(c)
        return c
    me = shard_of(place, core)
    local = []
    for a in range(count):
        whole = (0, parts[a].shape[0])
        c = pltpu.make_async_copy(parts[a], wholes[a].at[span(a, me, whole)], own_sem.at[a]); c.start(); local.append(c)
    got = {}
    pairs = []
    k = 0
    def piece_rows(a, s, d):
        rows = parts[a].shape[0]
        return (0, rows) if s < half else halves(rows)[d]
    for a in range(count):
        for d, to in ((0, right), (1, left)):
            got[a, 1, d] = send(a, parts[a], me, piece_rows(a, 1, d), to, (send_sem.at[a, 0, d], recv_sem.at[a, 0, d]), 0) if half > 1 else None
        pairs.append(send(a, parts[a], me, (0, parts[a].shape[0]), pair, (send_sem.at[a, half, 0], pair_sem.at[a, 0, 0]), 0))
    for s in range(1, half + 1):
        for a in range(count):
            for d, to in ((0, right), (1, left)):
                got[a, s, d].wait_recv()
                owner = shard_of(place + (n // 2 - s if d == 0 else s), core)
                rows = piece_rows(a, s, d)
                if s < half:
                    ahead = piece_rows(a, s + 1, d)
                    got[a, s + 1, d] = send(a, None, owner, ahead, to, (send_sem.at[a, s, d], recv_sem.at[a, s, d]), 0)
                pairs.append(send(a, None, owner, rows, pair, (send_sem.at[a, half + s, d], pair_sem.at[a, s, d]), 0))
    for c in pairs: c.wait_recv()
    for c in sent: c.wait_send()
    for c in local: c.wait()

def gather(parts, n, collective_id):
    count=len(parts); half=n//4
    return pl.pallas_call(
        lambda *refs: gather_kernel(n, *refs),
        out_shape=[jax.ShapeDtypeStruct((p.shape[0]*n, p.shape[1]), p.dtype) for p in parts],
        in_specs=[pl.BlockSpec(memory_space=pl.ANY)]*count, out_specs=[pl.BlockSpec(memory_space=pl.ANY)]*count,
        scratch_shapes=[pltpu.SemaphoreType.DMA((count, 2*half+1, 2)), pltpu.SemaphoreType.DMA((count, half, 2)),
            pltpu.SemaphoreType.DMA((count, half+1, 2)), pltpu.SemaphoreType.DMA((count,))],
        compiler_params=pltpu.CompilerParams(collective_id=collective_id, has_side_effects=True),
        name="gather_first",
    )(*parts)

def column_groups(width, replicas, parts):
    unit = 128 * replicas
    units = -(-width // unit)
    parts = min(parts, units)
    groups, start = [], 0
    for g in range(parts):
        size = (units // parts + (g < units % parts)) * unit
        groups.append((start, size, min(size, width - start)))
        start += size
    return groups, start

def reduce_kernel(n, replicas, groups, grad_ref, small_ref, out_ref, total_ref,
    pair_buf, out_buf, in_buf, sum_buf, cross_buf, share_buf, whole_buf, small_buf, small_cross,
    pair_send, pair_recv, ring_send, ring_recv, cross_send, cross_recv, share_send, share_recv, small_sems, cross_sems):
    chips = n // 2
    half = chips // 2
    rows = grad_ref.shape[0] // n
    place, core, shard_of = ring_place(n)
    right, left, pair = shard_of(place + 1, core), shard_of(place + chips - 1, core), shard_of(place, 1 - core)
    me, mine = lax.axis_index("shard"), lax.axis_index("replica")
    barrier = pltpu.get_barrier_semaphore()
    for s in range(1, n):
        pl.semaphore_signal(barrier, inc=1, device_id={"shard": (me + s) % n}, device_id_type=MESH)
    for s in range(1, replicas):
        pl.semaphore_signal(barrier, inc=1, device_id={"replica": (mine + s) % replicas}, device_id_type=MESH)
    pl.semaphore_wait(barrier, n + replicas - 2)
    started = []
    def copy(src, dst, send, recv, to):
        c = pltpu.make_async_remote_copy(src_ref=src, dst_ref=dst, send_sem=send, recv_sem=recv, device_id=to, device_id_type=MESH)
        c.start(); started.append(c)
        return c
    def piece(owner, cols, part=None):
        start, size = part if part is not None else (0, rows)
        return pl.ds(pl.multiple_of(owner * rows + start, 16), size), cols
    order = [half] + [v for s in range(half - 1, 0, -1) for v in (s, chips - s)] + [0]
    paired = {}
    for g, (start, size, wide) in enumerate(groups):
        cols = slice(start, start + wide)
        for q in order:
            owner = shard_of(place + q, 1 - core)
            paired[g, q] = copy(grad_ref.at[piece(owner, cols)], pair_buf.at[q, :, cols], pair_send.at[g, q], pair_recv.at[g, q], {"shard": pair})
        if g == 0:
            small = [copy(small_ref, small_buf.at[s], small_sems.at[0, s], small_sems.at[1, s], {"shard": (me + s) % n}) for s in range(1, n)]
    def own(g, q, part):
        start, size, wide = groups[g]
        cols = slice(start, start + wide)
        first, count = part
        return grad_ref[piece(shard_of(place + q, core), cols, part)].astype(f32) + pair_buf[q, first:first + count, cols].astype(f32)
    ring = {}
    every = (0, rows)
    for k in range(1, half + 1):
        for g, (start, size, wide) in enumerate(groups):
            cols = slice(start, start + wide)
            for d, to in ((0, right), (1, left)):
                q = half - k + 1 if d == 0 else chips - (half - k + 1)
                if k == 1:
                    if d == 0: paired[g, q].wait_recv()
                    part = halves(rows)[d]
                    first, count = part
                    out_buf[k - 1, d, first:first + count, cols] = own(g, q, part).astype(bf16)
                else:
                    part = every
                    first, count = part
                    paired[g, q].wait_recv()
                    ring[g, k - 1, d].wait_recv()
                    if k == 2:
                        for e in (0, 1):
                            at, many = halves(rows)[e]
                            value = own(g, q, (at, many))
                            if e == d: value = value + in_buf[k - 2, d, at:at + many, cols].astype(f32)
                            out_buf[k - 1, d, at:at + many, cols] = value.astype(bf16)
                    else:
                        out_buf[k - 1, d, :, cols] = (own(g, q, every) + in_buf[k - 2, d, :, cols].astype(f32)).astype(bf16)
                ring[g, k, d] = copy(out_buf.at[k - 1, d, first:first + count, cols], in_buf.at[k - 1, d, first:first + count, cols],
                    ring_send.at[g, k - 1, d], ring_recv.at[g, k - 1, d], {"shard": to})
        if k == 1:
            for c in small: c.wait_recv()
            small_buf[0] = small_ref[...]
            def add(i, acc):
                return acc + small_buf[(me - i + n) % n]
            small_cross[0] = lax.fori_loop(0, n, add, jnp.zeros(small_ref.shape, f32))
            across = [copy(small_cross.at[0], small_cross.at[s], cross_sems.at[0, s], cross_sems.at[1, s], {"replica": (mine + s) % replicas}) for s in range(1, replicas)]
    cross = {}
    for g, (start, size, wide) in enumerate(groups):
        cols = slice(start, start + wide)
        paired[g, 0].wait_recv()
        ring[g, half, 0].wait_recv(); ring[g, half, 1].wait_recv()
        value = own(g, 0, every) + in_buf[half - 1, 0, :, cols].astype(f32) + in_buf[half - 1, 1, :, cols].astype(f32)
        sum_buf[:, cols] = value.astype(bf16)
        if wide < size:
            sum_buf[:, start + wide:start + size] = jnp.zeros((rows, size - wide), bf16)
        each = size // replicas
        at = start // replicas
        for s in range(1, replicas):
            to = (mine + s) % replicas
            cross[g, s] = copy(sum_buf.at[:, pl.ds(pl.multiple_of(start + to * each, 128), each)], cross_buf.at[s, :, at:at + each],
                cross_send.at[g, s], cross_recv.at[g, s], {"replica": to})
    shared = {}
    for g, (start, size, wide) in enumerate(groups):
        each = size // replicas
        at = start // replicas
        for s in range(1, replicas): cross[g, s].wait_recv()
        cross_buf[0, :, at:at + each] = sum_buf[:, pl.ds(pl.multiple_of(start + mine * each, 128), each)]
        value = cross_buf[0, :, at:at + each].astype(f32)
        for s in range(1, replicas): value = value + cross_buf[s, :, at:at + each].astype(f32)
        share_buf[:, at:at + each] = value.astype(bf16)
        for s in range(1, replicas):
            to = (mine + s) % replicas
            shared[g, s] = copy(share_buf.at[:, at:at + each], whole_buf.at[:, pl.ds(pl.multiple_of(start + mine * each, 128), each)],
                share_send.at[g, s], share_recv.at[g, s], {"replica": to})
        whole_buf[:, pl.ds(pl.multiple_of(start + mine * each, 128), each)] = share_buf[:, at:at + each]
    for c in across: c.wait_recv()
    def add_cross(i, acc):
        return acc + small_cross[(mine - i + replicas) % replicas]
    total_ref[...] = lax.fori_loop(0, replicas, add_cross, jnp.zeros(small_ref.shape, f32))
    for g, (start, size, wide) in enumerate(groups):
        for s in range(1, replicas): shared[g, s].wait_recv()
        cols = slice(start, start + wide)
        out_ref[:, cols] = whole_buf[:, cols].astype(f32)
    for c in started: c.wait_send()

def reduce_last(grad, small, n, replicas, collective_id, parts=3):
    total, width = grad.shape
    rows = total // n
    chips, half = n // 2, n // 4
    groups, padded = column_groups(width, replicas, parts)
    count = len(groups)
    dma = pltpu.SemaphoreType.DMA
    return pl.pallas_call(
        lambda *refs: reduce_kernel(n, replicas, groups, *refs),
        out_shape=[jax.ShapeDtypeStruct((rows, width), f32), jax.ShapeDtypeStruct(small.shape, f32)],
        in_specs=[pl.BlockSpec(memory_space=pltpu.VMEM)] * 2, out_specs=[pl.BlockSpec(memory_space=pltpu.VMEM)] * 2,
        scratch_shapes=[
            pltpu.VMEM((chips, rows, width), bf16), pltpu.VMEM((half, 2, rows, width), bf16), pltpu.VMEM((half, 2, rows, width), bf16),
            pltpu.VMEM((rows, padded), bf16), pltpu.VMEM((replicas, rows, padded // replicas), bf16), pltpu.VMEM((rows, padded // replicas), bf16),
            pltpu.VMEM((rows, padded), bf16), pltpu.VMEM((n,) + small.shape, f32), pltpu.VMEM((replicas,) + small.shape, f32),
            dma((count, chips)), dma((count, chips)), dma((count, half, 2)), dma((count, half, 2)),
            dma((count, replicas)), dma((count, replicas)), dma((count, replicas)), dma((count, replicas)), dma((2, n)), dma((2, replicas)),
        ],
        compiler_params=pltpu.CompilerParams(collective_id=collective_id, has_side_effects=True, vmem_limit_bytes=48 * 2**20),
        name="reduce_last",
    )(grad, small)


def twice(v):
    return jnp.pad(jnp.concatenate([jnp.pad(v, (0, DUP - NH)), v]), (0, LANE - DUP - NH))


def mixer_tables(conv_w, conv_b, dt_bias, a_log, d_skip, out_gain):
    head = jnp.arange(DI) // HEAD
    column = jnp.arange(LANE)[:, None]
    spread = ((column % DUP == head[None]) & (column < 2 * DUP)).astype(bf16)
    rate = -jnp.exp(a_log)
    conv_t = jnp.concatenate([conv_w, conv_b[None], jnp.zeros((3, CONV_CH), f32)])
    head_t = jnp.concatenate(
        [jnp.stack([twice(dt_bias), twice(rate * LOG2E), twice(rate)]), jnp.zeros((5, LANE), f32)]
    )
    wide_t = jnp.concatenate([jnp.stack([jnp.repeat(d_skip, HEAD), out_gain]), jnp.zeros((6, DI), f32)])
    return conv_t, head_t, wide_t, spread, spread.T


def norm_parts(stream):
    return lax.rsqrt(jnp.mean(stream * stream, axis=-1, keepdims=True) + epsilon)


def shards(
    tokens, cotangent, lengths, dealing, in_gain, w_in, conv_w, conv_b, dt_bias, a_log, d_skip, out_gain, w_out,
):
    shard_count = lax.axis_size("shard")
    row_total = lax.axis_size("replica") * shard_count
    row_index = lax.axis_index("replica") * shard_count + lax.axis_index("shard")
    slot_count = tokens.shape[2]
    chunks = slot_count // CH
    token_count = MICRO * slot_count
    replicas = lax.axis_size("replica")
    first_in, first_out = gather([w_in[0], w_out[0]], shard_count, 1)
    full_in, full_out = [first_in], [first_out]
    for l in range(1, LAYERS):
        part_in, part_out, first_in = lax.optimization_barrier((w_in[l], w_out[l], first_in))
        full_in.append(lax.all_gather(part_in, "shard", axis=0, tiled=True))
        full_out.append(lax.all_gather(part_out, "shard", axis=0, tiled=True))
    full_in[0] = first_in
    global_rows = jnp.arange(MICRO) * row_total + row_index
    sequence = jnp.sum(jnp.where(jnp.arange(dealing.shape[0])[None] == global_rows[:, None], dealing[None], 0), axis=1)
    seq_length = jnp.sum(jnp.where(jnp.arange(lengths.shape[0])[None] == sequence[:, None], lengths[None], 0), axis=1)
    valid = (jnp.arange(slot_count)[None] < seq_length[:, None]).astype(f32).reshape(token_count, 1)

    stream = tokens.reshape(token_count, D).astype(f32)
    saved = []
    for l in range(LAYERS):
        normed = (stream * norm_parts(stream) * in_gain[l]).astype(bf16)
        projected = mm(normed, full_in[l])
        tables = mixer_tables(conv_w[l], conv_b[l], dt_bias[l], a_log[l], d_skip[l], out_gain[l])
        mixed, scanned, states = mixer_forward(projected, tables, chunks)
        saved.append((stream, normed, projected, tables, mixed, scanned, states))
        stream = stream + mm(mixed, full_out[l])
    result = (stream * valid).astype(bf16)

    upstream = cotangent.reshape(token_count, D).astype(f32) * valid
    in_grads = [None] * LAYERS
    out_grads = [None] * LAYERS
    gain_grads = [None] * LAYERS
    sums = [None] * LAYERS
    for l in reversed(range(LAYERS)):
        entered, normed, projected, tables, mixed, scanned, states = saved[l]
        branch_grad = upstream.astype(bf16)
        out_grads[l] = lax.psum_scatter(t_mm(mixed, branch_grad).astype(bf16), "shard", scatter_dimension=0, tiled=True)
        mixed_grad = mm_t(branch_grad, full_out[l]).astype(bf16)
        project_grad, sums[l] = mixer_backward(projected, scanned, states, mixed_grad, tables, chunks)
        in_grads[l] = t_mm(normed, project_grad).astype(bf16)
        if l > 0:
            in_grads[l] = lax.psum_scatter(in_grads[l], "shard", scatter_dimension=0, tiled=True)
        normed_grad = mm_t(project_grad, full_in[l])
        scale = norm_parts(entered)
        gain_grads[l] = jnp.sum(normed_grad * entered * scale, axis=0)
        inner = normed_grad * in_gain[l]
        pull = scale * scale * scale * jnp.mean(inner * entered, axis=-1, keepdims=True)
        upstream = upstream + scale * inner - pull * entered
    later, out_total = lax.psum((jnp.stack(in_grads[1:]).astype(f32), jnp.stack(out_grads).astype(f32)), "replica")
    small = jnp.stack(sums).at[:, 7, 2 * LANE : 2 * LANE + D].set(jnp.stack(gain_grads))
    first, small = reduce_last(in_grads[0], small.reshape(LAYERS * 8, CONV_CH), shard_count, replicas, 2)
    small = small.reshape(LAYERS, 8, CONV_CH)
    in_total = jnp.concatenate([first[None], later])
    rate = -jnp.exp(a_log)
    shape = (MICRO, 1, slot_count, D)
    return (
        result.reshape(shape),
        upstream.reshape(shape),
        small[:, 7, 2 * LANE : 2 * LANE + D],
        in_total,
        small[:, 0:4],
        small[:, 4],
        small[:, 7, 0:NH],
        small[:, 7, LANE : LANE + NH] * rate,
        small[:, 5, :DI].reshape(LAYERS, NH, HEAD).sum(-1),
        small[:, 6, :DI],
        out_total,
    )


def solution(mesh):
    rows = P(None, ("replica", "shard"), None, None)
    split = P(None, "shard", None)
    in_specs = (rows, rows, P(), P(), P(), split, P(), P(), P(), P(), P(), P(), split)
    out_specs = (rows, rows, P(), split, P(), P(), P(), P(), P(), P(), split)
    return jax.shard_map(shards, mesh=mesh, in_specs=in_specs, out_specs=out_specs, check_vma=False)
```

```python
import jax
import jax.numpy as jnp
from jax import lax
from jax.experimental import pallas as pl
from jax.experimental.pallas import tpu as pltpu
from jax.sharding import PartitionSpec as P

D = 768
DI = 1536
NH = 24
HEAD = 64
NSTATE = 128
KW = 4
CONV_CH = 1792
NIN = 3352
LAYERS = 2
MICRO = 2
CH = 128
PAIRS = NH // 2
LANE = 128
DUP = 32
LOG2E = 1.4426950408889634

epsilon = 1e-05
f32 = jnp.float32
bf16 = jnp.bfloat16
highest = lax.Precision.HIGHEST
MESH = pl.DeviceIdType.MESH


def mm(a, b):
    return jnp.dot(a, b, preferred_element_type=f32)


def mm_t(a, b):
    return lax.dot_general(a, b, (((1,), (1,)), ((), ())), preferred_element_type=f32)


def t_mm(a, b):
    return lax.dot_general(a, b, (((0,), (0,)), ((), ())), preferred_element_type=f32)


def sigmoid(v):
    return 0.5 * jnp.tanh(0.5 * v) + 0.5


def softplus(v):
    return jnp.maximum(v, 0.0) + jnp.log1p(jnp.exp(-jnp.abs(v)))


def lanes(j, base=0):
    return slice(base + LANE * j, base + LANE * (j + 1))


def split_pair(v):
    left = lax.broadcasted_iota(jnp.int32, v.shape, 1) < HEAD
    zero = jnp.zeros_like(v)
    return jnp.concatenate([jnp.where(left, v, zero), jnp.where(left, zero, v)], axis=0)


def high_low(v):
    high = v.astype(bf16)
    return high, (v - high.astype(f32)).astype(bf16)


def widen(v, spread):
    high, low = high_low(v)
    first = lax.broadcasted_iota(jnp.int32, v.shape, 1) < DUP
    return mm(jnp.where(first, high, low), spread)


def step_parts(proj_ref, raw_ref, head_ref):
    raw = proj_ref[:, DI + CONV_CH :]
    raw_ref[:, 0:NH] = raw
    raw_ref[:, DUP : DUP + NH] = raw
    shifted = raw_ref[...] + head_ref[0:1]
    step = softplus(shifted)
    rows = lax.broadcasted_iota(jnp.int32, (CH, CH), 0)
    cols = lax.broadcasted_iota(jnp.int32, (CH, CH), 1)
    lower = (cols <= rows).astype(f32)
    cum = jnp.dot(lower, head_ref[1:2] * step, precision=highest, preferred_element_type=f32)
    grow = jnp.exp2(cum)
    remain = jnp.exp2(cum[CH - 1 : CH] - cum)
    return shifted, step, cum, cum.T, grow, remain, rows, cols


def conv_block(ext_ref, conv_ref, j):
    total = conv_ref[4:5, lanes(j)]
    for k in range(KW):
        total = total + conv_ref[k : k + 1, lanes(j)] * ext_ref[5 + k : 5 + k + CH, lanes(j)]
    return total


def forward_kernel(
    proj_ref, conv_ref, head_ref, wide_ref, spread_ref,
    mixed_ref, scan_ref, saved_ref,
    ext_ref, raw_ref, state_ref, gated_ref, keep_ref,
):
    @pl.when(pl.program_id(1) == 0)
    def _():
        state_ref[...] = jnp.zeros_like(state_ref)
        ext_ref[0:8] = jnp.zeros_like(ext_ref[0:8])

    @pl.when((pl.program_id(0) == 0) & (pl.program_id(1) == 0))
    def _():
        raw_ref[...] = jnp.zeros_like(raw_ref)

    ext_ref[8 : 8 + CH] = proj_ref[:, DI : DI + CONV_CH]
    shifted, step, cum, cum_t, grow, remain, rows, cols = step_parts(proj_ref, raw_ref, head_ref)
    spread = spread_ref[...]
    step_w = widen(step, spread)
    grow_w = widen(grow, spread)
    remain_w = widen(remain * step, spread)

    def activated(j):
        value = conv_block(ext_ref, conv_ref, j)
        return value * sigmoid(value)

    b_low = activated(PAIRS).astype(bf16)
    c_low = activated(PAIRS + 1).astype(bf16)
    affinity = jnp.where(cols <= rows, mm_t(c_low, b_low), 0.0)
    state_low = state_ref[...].astype(bf16)
    saved_ref[...] = state_low
    carried = grow_w * mm(c_low, state_low)
    square = jnp.zeros((CH, LANE), f32)
    for j in range(PAIRS):
        xs = activated(j)
        mixing = []
        for h in (2 * j, 2 * j + 1):
            differ = jnp.minimum(cum[:, h : h + 1] - cum_t[h : h + 1], 0.0)
            mixing.append((jnp.exp2(differ) * affinity).astype(bf16))
        keep_ref[:, lanes(j)] = (xs * remain_w[:, lanes(j)]).astype(bf16)
        x_split = split_pair((xs * step_w[:, lanes(j)]).astype(bf16))
        scanned = mm(jnp.concatenate(mixing, axis=1), x_split) + carried[:, lanes(j)]
        scan_ref[:, lanes(j)] = scanned
        gate = proj_ref[:, lanes(j)]
        gated = (scanned + wide_ref[0:1, lanes(j)] * xs) * (gate * sigmoid(gate))
        gated_ref[:, lanes(j)] = gated
        square = square + gated * gated
    state_ref[...] = grow_w[CH - 1 : CH] * state_ref[...] + t_mm(b_low, keep_ref[...])
    scale = lax.rsqrt(jnp.sum(square, axis=1, keepdims=True) * (1.0 / DI) + epsilon)
    mixed_ref[...] = (gated_ref[...] * scale * wide_ref[1:2]).astype(bf16)
    ext_ref[0:8] = ext_ref[CH : CH + 8]


def backward_kernel(
    proj_ref, tail_ref, scan_ref, saved_ref, grad_ref, conv_ref, head_ref, wide_ref, spread_ref, gather_ref,
    out_ref, sum_ref,
    ext_ref, raw_ref, state_ref, act_ref, slope_ref, gate_ref, dconv_ref, keep_ref, grown_ref, high_ref, low_ref, step_ref, row_ref,
):
    chunk = pl.num_programs(1) - 1 - pl.program_id(1)

    @pl.when(pl.program_id(1) == 0)
    def _():
        state_ref[...] = jnp.zeros_like(state_ref)
        dconv_ref[CH : CH + 8] = jnp.zeros_like(dconv_ref[CH : CH + 8])

    @pl.when((pl.program_id(0) == 0) & (pl.program_id(1) == 0))
    def _():
        raw_ref[...] = jnp.zeros_like(raw_ref)
        row_ref[...] = jnp.zeros_like(row_ref)
        sum_ref[...] = jnp.zeros_like(sum_ref)

    ext_ref[0:8] = jnp.where(chunk > 0, tail_ref[:, DI : DI + CONV_CH], 0.0)
    ext_ref[8 : 8 + CH] = proj_ref[:, DI : DI + CONV_CH]
    shifted, step, cum, cum_t, grow, remain, rows, cols = step_parts(proj_ref, raw_ref, head_ref)
    spread = spread_ref[...]
    step_w = widen(step, spread)
    grow_w = widen(grow, spread)
    remain_w = widen(remain, spread)

    square = jnp.zeros((CH, LANE), f32)
    along = jnp.zeros((CH, LANE), f32)
    for j in range(PAIRS + 2):
        value = conv_block(ext_ref, conv_ref, j)
        share = sigmoid(value)
        xs = value * share
        act_ref[:, lanes(j)] = xs
        slope_ref[:, lanes(j)] = share + xs * (1.0 - share)
        if j < PAIRS:
            gate = proj_ref[:, lanes(j)]
            open_share = sigmoid(gate)
            gate_ref[:, lanes(j)] = open_share
            gated = (scan_ref[:, lanes(j)] + wide_ref[0:1, lanes(j)] * xs) * (gate * open_share)
            square = square + gated * gated
            along = along + gated * (grad_ref[:, lanes(j)].astype(f32) * wide_ref[1:2, lanes(j)])
    scale = lax.rsqrt(jnp.sum(square, axis=1, keepdims=True) * (1.0 / DI) + epsilon)
    pull = scale * scale * scale * (jnp.sum(along, axis=1, keepdims=True) * (1.0 / DI))

    b_low = act_ref[:, lanes(PAIRS)].astype(bf16)
    c_low = act_ref[:, lanes(PAIRS + 1)].astype(bf16)
    affinity_t = jnp.where(rows <= cols, mm_t(b_low, c_low), 0.0)
    state = state_ref[...]
    state_low = state.astype(bf16)
    row_ref[1:2] = jnp.sum(saved_ref[...].astype(f32) * state, axis=0, keepdims=True)
    back = remain_w * mm(b_low, state_low)
    affinity_grad = jnp.zeros((CH, CH), f32)
    for j in range(PAIRS):
        xs = act_ref[:, lanes(j)]
        skip = wide_ref[0:1, lanes(j)]
        grad = grad_ref[:, lanes(j)].astype(f32)
        gate = proj_ref[:, lanes(j)]
        open_share = gate_ref[:, lanes(j)]
        opened = gate * open_share
        scanned = scan_ref[:, lanes(j)]
        outer = scanned + skip * xs
        gated = outer * opened
        gated_grad = scale * (grad * wide_ref[1:2, lanes(j)]) - pull * gated
        sum_ref[6:7, lanes(j)] += jnp.sum(grad * (gated * scale), axis=0, keepdims=True)
        dy = gated_grad * opened
        out_ref[:, lanes(j)] = (gated_grad * outer * (open_share + opened * (1.0 - open_share))).astype(bf16)
        sum_ref[5:6, lanes(j)] += jnp.sum(dy * xs, axis=0, keepdims=True)
        dy_low = dy.astype(bf16)
        grown_ref[:, lanes(j)] = (grow_w[:, lanes(j)] * dy).astype(bf16)
        scaled = xs * step_w[:, lanes(j)]
        x_low = scaled.astype(bf16)
        keep_ref[:, lanes(j)] = (scaled * remain_w[:, lanes(j)]).astype(bf16)
        dy_split = split_pair(dy_low)
        kernels = []
        for h in (2 * j, 2 * j + 1):
            differ = jnp.minimum(cum_t[h : h + 1] - cum[:, h : h + 1], 0.0)
            kernels.append(jnp.exp2(differ))
        mixing_t = jnp.concatenate([(k * affinity_t).astype(bf16) for k in kernels], axis=1)
        arrived = back[:, lanes(j)]
        x_grad = mm(mixing_t, dy_split) + arrived
        mixing_grad = mm_t(x_low, dy_split)
        affinity_grad = affinity_grad + mixing_grad[:, :CH] * kernels[0] + mixing_grad[:, CH:] * kernels[1]
        x_back = x_low.astype(f32)
        row_ref[0:1, lanes(j)] = jnp.sum(x_back * arrived, axis=0, keepdims=True)
        high, low = high_low(dy_low.astype(f32) * scanned - x_back * x_grad)
        high_ref[:, lanes(j)] = high
        low_ref[:, lanes(j)] = low
        step_ref[:, lanes(j)] = (x_grad * xs).astype(bf16)
        dconv_ref[0:CH, lanes(j)] = (step_w[:, lanes(j)] * x_grad + skip * dy) * slope_ref[:, lanes(j)]
    affinity_low = jnp.where(rows <= cols, affinity_grad, 0.0).astype(bf16)
    grown = grown_ref[...]
    b_grad = mm(affinity_low, c_low) + mm_t(keep_ref[...], state_low)
    c_grad = t_mm(affinity_low, b_low) + mm_t(grown, saved_ref[...])
    dconv_ref[0:CH, lanes(PAIRS)] = b_grad * slope_ref[:, lanes(PAIRS)]
    dconv_ref[0:CH, lanes(PAIRS + 1)] = c_grad * slope_ref[:, lanes(PAIRS + 1)]

    gather = gather_ref[...]
    row_high, row_low = high_low(row_ref[...])
    row_sums = mm(row_high, gather) + mm(row_low, gather)
    last_grad = row_sums[0:1] + grow[CH - 1 : CH] * row_sums[1:2]
    cum_grad = mm(high_ref[...], gather) + mm(low_ref[...], gather)
    upper = (cols >= rows).astype(f32)
    decay_grad = jnp.dot(upper, cum_grad, precision=highest, preferred_element_type=f32) + last_grad
    step_grad = mm(step_ref[...], gather) + head_ref[2:3] * decay_grad
    raw_grad = step_grad * sigmoid(shifted)
    out_ref[:, DI + CONV_CH :] = raw_grad[:, :NH].astype(bf16)
    sum_ref[7:8, 0:LANE] += jnp.sum(raw_grad, axis=0, keepdims=True)
    sum_ref[7:8, LANE : 2 * LANE] += jnp.sum(decay_grad * step, axis=0, keepdims=True)
    state_ref[...] = grow_w[CH - 1 : CH] * state + t_mm(c_low, grown)

    for j in range(PAIRS + 2):
        total = conv_ref[3:4, lanes(j)] * dconv_ref[0:CH, lanes(j)]
        for k in range(KW - 1):
            total = total + conv_ref[k : k + 1, lanes(j)] * dconv_ref[3 - k : 3 - k + CH, lanes(j)]
        out_ref[:, lanes(j, DI)] = total.astype(bf16)
        here = dconv_ref[0:CH, lanes(j)]
        for k in range(KW):
            sum_ref[k : k + 1, lanes(j)] += jnp.sum(here * ext_ref[5 + k : 5 + k + CH, lanes(j)], axis=0, keepdims=True)
        sum_ref[4:5, lanes(j)] += jnp.sum(here, axis=0, keepdims=True)
    dconv_ref[CH : CH + 8] = dconv_ref[0:8]


def ring_place(n):
    wide = n // 4
    me = lax.axis_index("shard")
    chip, core = me // 2, me % 2
    row, col = chip // wide, chip % wide
    place = row * (2 * wide - 1 - col) + (1 - row) * col

    def shard_of(at, c):
        at = at % (2 * wide)
        r = at // wide
        x = r * (2 * wide - 1 - at) + (1 - r) * at
        return (r * wide + x) * 2 + c

    return place, core, shard_of


def halves(rows):
    first = rows // 2 // 16 * 16
    return (0, first), (first, rows - first)


def aligned(start, size, unit=16):
    return pl.ds(pl.multiple_of(start, unit), size)


def column_groups(width, replicas, parts):
    unit = LANE * replicas
    units = -(-width // unit)
    parts = min(parts, units)
    groups, start = [], 0
    for g in range(parts):
        size = (units // parts + (g < units % parts)) * unit
        groups.append((start, size, min(size, width - start)))
        start += size
    return groups, start


def remote(src, dst, send, recv, axis, to):
    return pltpu.make_async_remote_copy(
        src_ref=src, dst_ref=dst, send_sem=send, recv_sem=recv, device_id={axis: to}, device_id_type=MESH
    )


class Gather:
    def __init__(self, n, parts):
        self.n, self.half = n, n // 4
        self.shapes = [p.shape for p in parts]
        self.dtypes = [p.dtype for p in parts]
        self.stage_count = self.half + 2

    def in_count(self):
        return len(self.shapes)

    def out_count(self):
        return len(self.shapes)

    def in_specs(self):
        return [pl.BlockSpec(memory_space=pl.ANY)] * len(self.shapes)

    out_specs = in_specs

    def out_shapes(self):
        return [jax.ShapeDtypeStruct((r * self.n, w), t) for (r, w), t in zip(self.shapes, self.dtypes)]

    def scratch(self):
        count = len(self.shapes)
        dma = pltpu.SemaphoreType.DMA
        return [
            dma((count, self.half, 2)), dma((count, self.half, 2)),
            dma((count, self.half + 1, 2)), dma((count, self.half + 1, 2)), dma((count,)),
        ]

    def stages(self, parts, wholes, scratch):
        ring_send, ring_recv, pair_send, pair_recv, own_sem = scratch
        n, half = self.n, self.half
        place, core, shard_of = ring_place(n)
        right, left, pair = shard_of(place + 1, core), shard_of(place + n // 2 - 1, core), shard_of(place, 1 - core)
        me = shard_of(place, core)
        arrays = range(len(self.shapes))
        ways = ((0, right), (1, left))

        def rows_of(a, s, d):
            rows = self.shapes[a][0]
            return (0, rows) if s < half else halves(rows)[d]

        def span(a, owner, part):
            return aligned(owner * self.shapes[a][0] + part[0], part[1])

        def hop(a, s, d, to):
            owner = shard_of(place + (n // 2 - (s - 1) if d == 0 else s - 1), core)
            part = rows_of(a, s, d)
            src = parts[a].at[aligned(part[0], part[1])] if s == 1 else wholes[a].at[span(a, owner, part)]
            return remote(src, wholes[a].at[span(a, owner, part)], ring_send.at[a, s - 1, d], ring_recv.at[a, s - 1, d], "shard", to)

        def cross(a, s, d):
            owner = me if s == 0 else shard_of(place + (n // 2 - s if d == 0 else s), core)
            part = (0, self.shapes[a][0]) if s == 0 else rows_of(a, s, d)
            src = parts[a] if s == 0 else wholes[a].at[span(a, owner, part)]
            return remote(src, wholes[a].at[span(a, owner, part)], pair_send.at[a, s, d], pair_recv.at[a, s, d], "shard", pair)

        def own(a):
            return pltpu.make_async_copy(parts[a], wholes[a].at[span(a, me, (0, self.shapes[a][0]))], own_sem.at[a])

        crossings = [(0, 0)] + [(s, d) for s in range(1, half + 1) for d in (0, 1)]

        def first():
            barrier = pltpu.get_barrier_semaphore()
            for to in (right, left, pair):
                pl.semaphore_signal(barrier, inc=1, device_id={"shard": to}, device_id_type=MESH)
            pl.semaphore_wait(barrier, 3)
            for a in arrays:
                for d, to in ways:
                    hop(a, 1, d, to).start()
                cross(a, 0, 0).start()
                own(a).start()

        def forward(s):
            for a in arrays:
                for d, to in ways:
                    hop(a, s, d, to).wait_recv()
                    if s < half:
                        hop(a, s + 1, d, to).start()
                    cross(a, s, d).start()

        def last():
            for a in arrays:
                for s, d in crossings:
                    cross(a, s, d).wait_recv()
                for s, d in crossings:
                    cross(a, s, d).wait_send()
                for s in range(1, half + 1):
                    for d, to in ways:
                        hop(a, s, d, to).wait_send()
                own(a).wait()

        return [first] + [lambda s=s: forward(s) for s in range(1, half + 1)] + [last]


class Reduce:
    def __init__(self, n, replicas, grads, groups, small=None):
        self.n, self.replicas = n, replicas
        self.chips, self.half = n // 2, n // 4
        self.shapes = [(g.shape[0] // n, g.shape[1]) for g in grads]
        self.groups = [column_groups(w, replicas, count) for (_, w), count in zip(self.shapes, groups)]
        self.small = small
        self.stage_count = self.half + 4

    def in_count(self):
        return len(self.shapes) + (self.small is not None)

    out_count = in_count

    def in_specs(self):
        specs = [pl.BlockSpec(memory_space=pl.ANY)] * len(self.shapes)
        return specs + ([pl.BlockSpec(memory_space=pltpu.VMEM)] if self.small is not None else [])

    def out_specs(self):
        specs = [pl.BlockSpec(memory_space=pl.ANY)] * len(self.shapes)
        return specs + ([pl.BlockSpec(memory_space=pltpu.VMEM)] if self.small is not None else [])

    def out_shapes(self):
        shapes = [jax.ShapeDtypeStruct(s, f32) for s in self.shapes]
        return shapes + ([jax.ShapeDtypeStruct(self.small.shape, f32)] if self.small is not None else [])

    def scratch(self):
        dma = pltpu.SemaphoreType.DMA
        items = []
        for (rows, width), (groups, padded) in zip(self.shapes, self.groups):
            g, each = len(groups), padded // self.replicas
            items += [
                pltpu.VMEM((self.chips, rows, width), bf16),
                pltpu.VMEM((self.chips, rows, width), bf16),
                pltpu.VMEM((self.half, 2, rows, width), bf16),
                pltpu.VMEM((self.half, 2, rows, width), bf16),
                pltpu.VMEM((rows, padded), bf16),
                pltpu.VMEM((self.replicas, rows, each), bf16),
                pltpu.VMEM((rows, each), bf16),
                pltpu.VMEM((rows, padded), bf16),
                pltpu.VMEM((rows, width), f32),
                dma((g, self.chips, 3)), dma((g, self.half, 2, 2)), dma((g, self.replicas, 4)), dma((1,)),
            ]
        if self.small is not None:
            items += [
                pltpu.VMEM((self.n,) + self.small.shape, f32),
                pltpu.VMEM((self.replicas,) + self.small.shape, f32),
                dma((2, self.n)), dma((2, self.replicas)),
            ]
        return items

    def stages(self, ins, outs, scratch):
        n, replicas, chips, half = self.n, self.replicas, self.chips, self.half
        place, core, shard_of = ring_place(n)
        right, left, pair = shard_of(place + 1, core), shard_of(place + chips - 1, core), shard_of(place, 1 - core)
        me, mine = lax.axis_index("shard"), lax.axis_index("replica")
        ways = ((0, right), (1, left))
        order = [half] + [v for s in range(half - 1, 0, -1) for v in (s, chips - s)] + [0]
        work = [(a, g) for a in range(len(self.shapes)) for g in range(len(self.groups[a][0]))]
        buffers = [scratch[13 * a : 13 * a + 13] for a in range(len(self.shapes))]
        if self.small is not None:
            small_ref, total_ref = ins[-1], outs[-1]
            small_buf, small_cross, small_sem, cross_sem = scratch[13 * len(self.shapes) :]

        def cols_of(a, g):
            start, _, wide = self.groups[a][0][g]
            return slice(start, start + wide)

        def piece(a, g, owner):
            rows = self.shapes[a][0]
            return ins[a].at[aligned(owner * rows, rows), cols_of(a, g)]

        def pairing(a, g, q):
            sem = buffers[a][9]
            return remote(piece(a, g, shard_of(place + q, 1 - core)), buffers[a][1].at[q, :, cols_of(a, g)],
                          sem.at[g, q, 0], sem.at[g, q, 1], "shard", pair)

        def loading(a, g, q):
            return pltpu.make_async_copy(piece(a, g, shard_of(place + q, core)), buffers[a][0].at[q, :, cols_of(a, g)], buffers[a][9].at[g, q, 2])

        def part_of(a, k, d):
            rows = self.shapes[a][0]
            return halves(rows)[d] if k == 1 else (0, rows)

        def ringing(a, g, k, d, to):
            first, count = part_of(a, k, d)
            sem = buffers[a][10]
            return remote(buffers[a][2].at[k - 1, d, first : first + count, cols_of(a, g)],
                          buffers[a][3].at[k - 1, d, first : first + count, cols_of(a, g)],
                          sem.at[g, k - 1, d, 0], sem.at[g, k - 1, d, 1], "shard", to)

        def block(a, g, index):
            start, size, _ = self.groups[a][0][g]
            return aligned(start + index * (size // replicas), size // replicas, LANE)

        def slot(a, g):
            start, size, _ = self.groups[a][0][g]
            return slice(start // replicas, (start + size) // replicas)

        def crossing(a, g, s):
            to = (mine + s) % replicas
            sem = buffers[a][11]
            return remote(buffers[a][4].at[:, block(a, g, to)], buffers[a][5].at[s, :, slot(a, g)],
                          sem.at[g, s, 0], sem.at[g, s, 1], "replica", to)

        def sharing(a, g, s):
            to = (mine + s) % replicas
            sem = buffers[a][11]
            return remote(buffers[a][6].at[:, slot(a, g)], buffers[a][7].at[:, block(a, g, mine)],
                          sem.at[g, s, 2], sem.at[g, s, 3], "replica", to)

        def storing(a):
            return pltpu.make_async_copy(buffers[a][8], outs[a], buffers[a][12].at[0])

        def small_plane(s):
            return remote(small_ref, small_buf.at[s], small_sem.at[0, s], small_sem.at[1, s], "shard", (me + s) % n)

        def small_across(s):
            return remote(small_cross.at[0], small_cross.at[s], cross_sem.at[0, s], cross_sem.at[1, s], "replica", (mine + s) % replicas)

        def both(a, g, q, part):
            first, count = part
            rows, cols = slice(first, first + count), cols_of(a, g)
            return buffers[a][0][q, rows, cols].astype(f32) + buffers[a][1][q, rows, cols].astype(f32)

        def arrived(a, g, q):
            loading(a, g, q).wait()
            pairing(a, g, q).wait_recv()

        def first():
            barrier = pltpu.get_barrier_semaphore()
            near = [(me + s) % n for s in range(1, n)] if self.small is not None else [right, left, pair]
            for to in near:
                pl.semaphore_signal(barrier, inc=1, device_id={"shard": to}, device_id_type=MESH)
            for s in range(1, replicas):
                pl.semaphore_signal(barrier, inc=1, device_id={"replica": (mine + s) % replicas}, device_id_type=MESH)
            pl.semaphore_wait(barrier, len(near) + replicas - 1)
            for i, (a, g) in enumerate(work):
                for q in order:
                    pairing(a, g, q).start()
                    loading(a, g, q).start()
                if i == 0 and self.small is not None:
                    for s in range(1, n):
                        small_plane(s).start()

        def turn(k):
            for a, g in work:
                cols = cols_of(a, g)
                for d, to in ways:
                    q = half - k + 1 if d == 0 else chips - (half - k + 1)
                    if k > 1 or d == 0:
                        arrived(a, g, q)
                    if k > 1:
                        ringing(a, g, k - 1, d, to).wait_recv()
                    pieces = [part_of(a, 1, d)] if k == 1 else halves(self.shapes[a][0]) if k == 2 else [part_of(a, k, d)]
                    for e, (at, many) in enumerate(pieces):
                        value = both(a, g, q, (at, many))
                        if k > 2 or (k == 2 and e == d):
                            value = value + buffers[a][3][k - 2, d, at : at + many, cols].astype(f32)
                        buffers[a][2][k - 1, d, at : at + many, cols] = value.astype(bf16)
                    ringing(a, g, k, d, to).start()
            if k == 1 and self.small is not None:
                for s in range(1, n):
                    small_plane(s).wait_recv()
                small_buf[0] = small_ref[...]
                small_cross[0] = lax.fori_loop(
                    0, n, lambda i, acc: acc + small_buf[(me - i + n) % n], jnp.zeros(self.small.shape, f32)
                )
                for s in range(1, replicas):
                    small_across(s).start()

        def settle():
            for a, g in work:
                cols = cols_of(a, g)
                start, size, wide = self.groups[a][0][g]
                rows = self.shapes[a][0]
                arrived(a, g, 0)
                value = both(a, g, 0, (0, rows))
                for d, to in ways:
                    ringing(a, g, half, d, to).wait_recv()
                    value = value + buffers[a][3][half - 1, d, :, cols].astype(f32)
                buffers[a][4][:, cols] = value.astype(bf16)
                if wide < size:
                    buffers[a][4][:, start + wide : start + size] = jnp.zeros((rows, size - wide), bf16)
                for s in range(1, replicas):
                    crossing(a, g, s).start()

        def share():
            for a, g in work:
                cols = slot(a, g)
                for s in range(1, replicas):
                    crossing(a, g, s).wait_recv()
                value = buffers[a][4][:, block(a, g, mine)].astype(f32)
                for s in range(1, replicas):
                    value = value + buffers[a][5][s, :, cols].astype(f32)
                buffers[a][6][:, cols] = value.astype(bf16)
                for s in range(1, replicas):
                    sharing(a, g, s).start()
                buffers[a][7][:, block(a, g, mine)] = value.astype(bf16)

        def last():
            if self.small is not None:
                for s in range(1, replicas):
                    small_across(s).wait_recv()
                total_ref[...] = lax.fori_loop(
                    0, replicas, lambda i, acc: acc + small_cross[(mine - i + replicas) % replicas],
                    jnp.zeros(self.small.shape, f32),
                )
            for a, g in work:
                cols = cols_of(a, g)
                for s in range(1, replicas):
                    sharing(a, g, s).wait_recv()
                buffers[a][8][:, cols] = buffers[a][7][:, cols].astype(f32)
            for a in range(len(self.shapes)):
                storing(a).start()
            for a, g in work:
                for q in order:
                    pairing(a, g, q).wait_send()
                for k in range(1, half + 1):
                    for d, to in ways:
                        ringing(a, g, k, d, to).wait_send()
                for s in range(1, replicas):
                    crossing(a, g, s).wait_send()
                    sharing(a, g, s).wait_send()
            if self.small is not None:
                for s in range(1, n):
                    small_plane(s).wait_send()
                for s in range(1, replicas):
                    small_across(s).wait_send()
            for a in range(len(self.shapes)):
                storing(a).wait()

        return [first] + [lambda k=k: turn(k) for k in range(1, half + 1)] + [settle, share, last]


def move(engine, operands, collective_id, name):
    def kernel(*refs):
        i, o = engine.in_count(), engine.out_count()
        for stage in engine.stages(refs[:i], refs[i : i + o], refs[i + o :]):
            stage()

    return pl.pallas_call(
        kernel,
        out_shape=engine.out_shapes(),
        in_specs=engine.in_specs(),
        out_specs=engine.out_specs(),
        scratch_shapes=engine.scratch(),
        compiler_params=pltpu.CompilerParams(
            collective_id=collective_id, has_side_effects=True, vmem_limit_bytes=56 * 2**20
        ),
        name=name,
    )(*operands)


def beside(body, counts, engine, steps, total):
    ins, outs, scratch = counts

    def kernel(*refs):
        i, o = engine.in_count(), engine.out_count()
        own_in, refs = refs[:ins], refs[ins:]
        far_in, refs = refs[:i], refs[i:]
        own_out, refs = refs[:outs], refs[outs:]
        far_out, refs = refs[:o], refs[o:]
        own_scratch, far_scratch = refs[:scratch], refs[scratch:]
        stages = engine.stages(far_in, far_out, far_scratch)
        step = pl.program_id(0) * pl.num_programs(1) + pl.program_id(1)
        for at, stage in zip(steps, stages[:-1]):
            pl.when(step == at)(stage)
        body(*own_in, *own_out, *own_scratch)
        pl.when(step == total - 1)(stages[-1])

    return kernel


def fixed(shape):
    return pl.BlockSpec(shape, lambda r, c: (0,) * len(shape))


def grid_call(body, grid, operands, in_specs, out_specs, out_shapes, scratch, name, limit, extra):
    if extra is None:
        return pl.pallas_call(
            body, grid=grid, in_specs=in_specs, out_specs=out_specs, out_shape=out_shapes, scratch_shapes=scratch,
            compiler_params=pltpu.CompilerParams(dimension_semantics=("arbitrary", "arbitrary"), vmem_limit_bytes=limit),
            name=name,
        )(*operands)
    engine, given, steps, collective_id = extra
    total = grid[0] * grid[1]
    kernel = beside(body, (len(in_specs), len(out_specs), len(scratch)), engine, [min(s, total - 1) for s in steps], total)
    return pl.pallas_call(
        kernel, grid=grid, in_specs=in_specs + engine.in_specs(), out_specs=out_specs + engine.out_specs(),
        out_shape=out_shapes + engine.out_shapes(), scratch_shapes=scratch + engine.scratch(),
        compiler_params=pltpu.CompilerParams(
            dimension_semantics=("arbitrary", "arbitrary"), vmem_limit_bytes=limit,
            collective_id=collective_id, has_side_effects=True,
        ),
        name=name + "_sending",
    )(*operands, *given)


def mixer_forward(projected, tables, chunks, extra=None):
    tokens = projected.shape[0]
    conv_t, head_t, wide_t, spread, _ = tables
    block = lambda r, c: (r * chunks + c, 0)
    return grid_call(
        forward_kernel,
        (tokens // (chunks * CH), chunks),
        (projected, conv_t, head_t, wide_t, spread),
        [pl.BlockSpec((CH, NIN), block), fixed((8, CONV_CH)), fixed((8, LANE)), fixed((8, DI)), fixed((LANE, DI))],
        [pl.BlockSpec((CH, DI), block), pl.BlockSpec((CH, DI), block), pl.BlockSpec((NSTATE, DI), block)],
        [
            jax.ShapeDtypeStruct((tokens, DI), bf16),
            jax.ShapeDtypeStruct((tokens, DI), f32),
            jax.ShapeDtypeStruct((tokens // CH * NSTATE, DI), bf16),
        ],
        [
            pltpu.VMEM((CH + 8, CONV_CH), f32),
            pltpu.VMEM((CH, LANE), f32),
            pltpu.VMEM((NSTATE, DI), f32),
            pltpu.VMEM((CH, DI), f32),
            pltpu.VMEM((CH, DI), bf16),
        ],
        "mixer_forward", 48 * 2**20, extra,
    )


def mixer_backward(projected, scanned, saved, mixed_grad, tables, chunks, extra=None):
    tokens = projected.shape[0]
    conv_t, head_t, wide_t, spread, gather = tables
    block = lambda r, c: (r * chunks + chunks - 1 - c, 0)
    ahead = lambda r, c: (jnp.maximum((r * chunks + chunks - 1 - c) * (CH // 8) - 1, 0), 0)
    return grid_call(
        backward_kernel,
        (tokens // (chunks * CH), chunks),
        (projected, projected, scanned, saved, mixed_grad, conv_t, head_t, wide_t, spread, gather),
        [
            pl.BlockSpec((CH, NIN), block),
            pl.BlockSpec((8, NIN), ahead),
            pl.BlockSpec((CH, DI), block),
            pl.BlockSpec((NSTATE, DI), block),
            pl.BlockSpec((CH, DI), block),
            fixed((8, CONV_CH)),
            fixed((8, LANE)),
            fixed((8, DI)),
            fixed((LANE, DI)),
            fixed((DI, LANE)),
        ],
        [pl.BlockSpec((CH, NIN), block), fixed((8, CONV_CH))],
        [jax.ShapeDtypeStruct((tokens, NIN), bf16), jax.ShapeDtypeStruct((8, CONV_CH), f32)],
        [
            pltpu.VMEM((CH + 8, CONV_CH), f32),
            pltpu.VMEM((CH, LANE), f32),
            pltpu.VMEM((NSTATE, DI), f32),
            pltpu.VMEM((CH, CONV_CH), f32),
            pltpu.VMEM((CH, CONV_CH), f32),
            pltpu.VMEM((CH, DI), f32),
            pltpu.VMEM((CH + 8, CONV_CH), f32),
            pltpu.VMEM((CH, DI), bf16),
            pltpu.VMEM((CH, DI), bf16),
            pltpu.VMEM((CH, DI), bf16),
            pltpu.VMEM((CH, DI), bf16),
            pltpu.VMEM((CH, DI), bf16),
            pltpu.VMEM((8, DI), f32),
        ],
        "mixer_backward", 60 * 2**20, extra,
    )


def twice(v):
    return jnp.pad(jnp.concatenate([jnp.pad(v, (0, DUP - NH)), v]), (0, LANE - DUP - NH))


def mixer_tables(conv_w, conv_b, dt_bias, a_log, d_skip, out_gain):
    head = jnp.arange(DI) // HEAD
    column = jnp.arange(LANE)[:, None]
    spread = ((column % DUP == head[None]) & (column < 2 * DUP)).astype(bf16)
    rate = -jnp.exp(a_log)
    conv_t = jnp.concatenate([conv_w, conv_b[None], jnp.zeros((3, CONV_CH), f32)])
    head_t = jnp.concatenate(
        [jnp.stack([twice(dt_bias), twice(rate * LOG2E), twice(rate)]), jnp.zeros((5, LANE), f32)]
    )
    wide_t = jnp.concatenate([jnp.stack([jnp.repeat(d_skip, HEAD), out_gain]), jnp.zeros((6, DI), f32)])
    return conv_t, head_t, wide_t, spread, spread.T


def norm_parts(stream):
    return lax.rsqrt(jnp.mean(stream * stream, axis=-1, keepdims=True) + epsilon)


def shards(
    tokens, cotangent, lengths, dealing, in_gain, w_in, conv_w, conv_b, dt_bias, a_log, d_skip, out_gain, w_out,
):
    shard_count = lax.axis_size("shard")
    row_total = lax.axis_size("replica") * shard_count
    row_index = lax.axis_index("replica") * shard_count + lax.axis_index("shard")
    slot_count = tokens.shape[2]
    chunks = slot_count // CH
    token_count = MICRO * slot_count
    replicas = lax.axis_size("replica")
    engine = Gather(shard_count, [w_in[0], w_out[0]])
    first_in, first_out = move(engine, (w_in[0], w_out[0]), 1, "gather_first")
    full_in, full_out = [first_in, None], [first_out, None]
    global_rows = jnp.arange(MICRO) * row_total + row_index
    sequence = jnp.sum(jnp.where(jnp.arange(dealing.shape[0])[None] == global_rows[:, None], dealing[None], 0), axis=1)
    seq_length = jnp.sum(jnp.where(jnp.arange(lengths.shape[0])[None] == sequence[:, None], lengths[None], 0), axis=1)
    valid = (jnp.arange(slot_count)[None] < seq_length[:, None]).astype(f32).reshape(token_count, 1)

    stream = tokens.reshape(token_count, D).astype(f32)
    saved = []
    for l in range(LAYERS):
        normed = (stream * norm_parts(stream) * in_gain[l]).astype(bf16)
        projected = mm(normed, full_in[l])
        tables = mixer_tables(conv_w[l], conv_b[l], dt_bias[l], a_log[l], d_skip[l], out_gain[l])
        later = w_in[1] if l == 0 else w_out[1]
        engine = Gather(shard_count, [later])
        mixed, scanned, states, whole = mixer_forward(projected, tables, chunks, (engine, (later,), (0, 4, 7, 7), 2 + l))
        if l == 0:
            full_in[1] = whole
        else:
            full_out[1] = whole
        saved.append((stream, normed, projected, tables, mixed, scanned, states))
        stream = stream + mm(mixed, full_out[l])
    result = (stream * valid).astype(bf16)

    upstream = cotangent.reshape(token_count, D).astype(f32) * valid
    in_grads = [None] * LAYERS
    out_grads = [None] * LAYERS
    gain_grads = [None] * LAYERS
    sums = [None] * LAYERS
    for l in reversed(range(LAYERS)):
        entered, normed, projected, tables, mixed, scanned, states = saved[l]
        branch_grad = upstream.astype(bf16)
        out_grad = t_mm(mixed, branch_grad).astype(bf16)
        mixed_grad = mm_t(branch_grad, full_out[l]).astype(bf16)
        given = (out_grad,) if l > 0 else (in_grad, out_grad)
        engine = Reduce(shard_count, replicas, given, [1] * len(given))
        steps = (0, 1, 2, 3, 4, 5, 6) if l > 0 else (0, 1, 3, 6, 7, 7, 7)
        project_grad, sums[l], *done = mixer_backward(
            projected, scanned, states, mixed_grad, tables, chunks, (engine, given, steps, 4 + l)
        )
        if l > 0:
            out_grads[1] = done[0]
        else:
            in_grads[1], out_grads[0] = done
        in_grad = t_mm(normed, project_grad).astype(bf16)
        normed_grad = mm_t(project_grad, full_in[l])
        scale = norm_parts(entered)
        gain_grads[l] = jnp.sum(normed_grad * entered * scale, axis=0)
        inner = normed_grad * in_gain[l]
        pull = scale * scale * scale * jnp.mean(inner * entered, axis=-1, keepdims=True)
        upstream = upstream + scale * inner - pull * entered
    small = jnp.stack(sums).at[:, 7, 2 * LANE : 2 * LANE + D].set(jnp.stack(gain_grads)).reshape(LAYERS * 8, CONV_CH)
    engine = Reduce(shard_count, replicas, (in_grad,), [3], small)
    in_grads[0], small = move(engine, (in_grad, small), 6, "reduce_last")
    small = small.reshape(LAYERS, 8, CONV_CH)
    in_total, out_total = jnp.stack(in_grads), jnp.stack(out_grads)
    rate = -jnp.exp(a_log)
    shape = (MICRO, 1, slot_count, D)
    return (
        result.reshape(shape),
        upstream.reshape(shape),
        small[:, 7, 2 * LANE : 2 * LANE + D],
        in_total,
        small[:, 0:4],
        small[:, 4],
        small[:, 7, 0:NH],
        small[:, 7, LANE : LANE + NH] * rate,
        small[:, 5, :DI].reshape(LAYERS, NH, HEAD).sum(-1),
        small[:, 6, :DI],
        out_total,
    )


def solution(mesh):
    rows = P(None, ("replica", "shard"), None, None)
    split = P(None, "shard", None)
    in_specs = (rows, rows, P(), P(), P(), split, P(), P(), P(), P(), P(), P(), split)
    out_specs = (rows, rows, P(), split, P(), P(), P(), P(), P(), P(), split)
    return jax.shard_map(shards, mesh=mesh, in_specs=in_specs, out_specs=out_specs, check_vma=False)
```

```python
import jax
import jax.numpy as jnp
from jax import lax
from jax.experimental import pallas as pl
from jax.experimental.pallas import tpu as pltpu
from jax.sharding import PartitionSpec as P

D = 768
DI = 1536
NH = 24
HEAD = 64
NSTATE = 128
KW = 4
CONV_CH = 1792
NIN = 3352
LAYERS = 2
MICRO = 2
CH = 128
PAIRS = NH // 2
LANE = 128
DUP = 32
LOG2E = 1.4426950408889634
SUMS = 2048
CUT = 1664
GATHER_BOTH = ((0, 3, 7, 8), (0, 5, 8, 8), (0, 7, 8, 8))
GATHER_LAST = ((1, 4, 6, 8),)
REDUCE_OUT = ((1, 2, 3, 4, 5, 6, 7, 8),)
REDUCE_BOTH = ((0, 1, 2, 3, 4, 5, 6, 7), (0, 1, 2, 4, 5, 6, 7, 8), (0, 1, 3, 4, 5, 6, 7, 8))

epsilon = 1e-05
f32 = jnp.float32
bf16 = jnp.bfloat16
highest = lax.Precision.HIGHEST
MESH = pl.DeviceIdType.MESH


def mm(a, b):
    return jnp.dot(a, b, preferred_element_type=f32)


def mm_t(a, b):
    return lax.dot_general(a, b, (((1,), (1,)), ((), ())), preferred_element_type=f32)


def t_mm(a, b):
    return lax.dot_general(a, b, (((0,), (0,)), ((), ())), preferred_element_type=f32)


def sigmoid(v):
    return 0.5 * jnp.tanh(0.5 * v) + 0.5


def softplus(v):
    return jnp.maximum(v, 0.0) + jnp.log1p(jnp.exp(-jnp.abs(v)))


def lanes(j, base=0):
    return slice(base + LANE * j, base + LANE * (j + 1))


def norm_scale(stream):
    return lax.rsqrt(jnp.mean(stream * stream, axis=-1, keepdims=True) + epsilon)


def split_pair(v):
    left = lax.broadcasted_iota(jnp.int32, v.shape, 1) < HEAD
    zero = jnp.zeros_like(v)
    return jnp.concatenate([jnp.where(left, v, zero), jnp.where(left, zero, v)], axis=0)


def high_low(v):
    high = v.astype(bf16)
    return high, (v - high.astype(f32)).astype(bf16)


def widen(v, spread):
    high, low = high_low(v)
    first = lax.broadcasted_iota(jnp.int32, v.shape, 1) < DUP
    return mm(jnp.where(first, high, low), spread)


def step_parts(proj_ref, raw_ref, head_ref):
    raw = proj_ref[:, DI + CONV_CH :]
    raw_ref[:, 0:NH] = raw
    raw_ref[:, DUP : DUP + NH] = raw
    shifted = raw_ref[...] + head_ref[0:1]
    step = softplus(shifted)
    rows = lax.broadcasted_iota(jnp.int32, (CH, CH), 0)
    cols = lax.broadcasted_iota(jnp.int32, (CH, CH), 1)
    lower = (cols <= rows).astype(f32)
    cum = jnp.dot(lower, head_ref[1:2] * step, precision=highest, preferred_element_type=f32)
    grow = jnp.exp2(cum)
    remain = jnp.exp2(cum[CH - 1 : CH] - cum)
    return shifted, step, cum, cum.T, grow, remain, rows, cols


def conv_block(ext_ref, conv_ref, j):
    total = conv_ref[4:5, lanes(j)]
    for k in range(KW):
        total = total + conv_ref[k : k + 1, lanes(j)] * ext_ref[5 + k : 5 + k + CH, lanes(j)]
    return total


def prepare(layer, params, tables, gather_ref=None):
    in_gain_ref, conv_w_ref, conv_b_ref, dt_bias_ref, a_log_ref, d_skip_ref, out_gain_ref = params
    conv_ref, head_ref, wide_ref, spread_ref = tables
    conv_ref[0:KW] = conv_w_ref[layer]
    conv_ref[KW : KW + 1] = conv_b_ref[layer : layer + 1]
    head_ref[...] = jnp.zeros_like(head_ref)
    rate = -jnp.exp(a_log_ref[layer : layer + 1])
    for row, value in enumerate((dt_bias_ref[layer : layer + 1], rate * LOG2E, rate, d_skip_ref[layer : layer + 1])):
        head_ref[row : row + 1, 0:NH] = value
        head_ref[row : row + 1, DUP : DUP + NH] = value
    column = lax.broadcasted_iota(jnp.int32, (LANE, DI), 0)
    owner = lax.broadcasted_iota(jnp.int32, (LANE, DI), 1) // HEAD
    spread_ref[...] = ((column % DUP == owner) & (column < 2 * DUP)).astype(f32).astype(bf16)
    wide_ref[...] = widen(head_ref[...], spread_ref[...])
    wide_ref[0:1] = wide_ref[3:4]
    wide_ref[1:2] = out_gain_ref[layer : layer + 1]
    if gather_ref is not None:
        column = lax.broadcasted_iota(jnp.int32, (DI, LANE), 1)
        owner = lax.broadcasted_iota(jnp.int32, (DI, LANE), 0) // HEAD
        gather_ref[...] = ((column % DUP == owner) & (column < 2 * DUP)).astype(f32).astype(bf16)


def table_scratch():
    return [
        pltpu.VMEM((8, CONV_CH), f32), pltpu.VMEM((8, LANE), f32), pltpu.VMEM((8, DI), f32), pltpu.VMEM((LANE, DI), bf16),
    ]


def forward_kernel(layer, *refs):
    params, (tokens_ref, w_in_ref), refs = refs[:7], refs[7:9], refs[9:]
    if layer > 0:
        before_ref, w_out_ref, stream_ref, *refs = refs
    normed_ref, proj_ref, mixed_ref, scan_ref, saved_ref, *refs = refs
    tables, (ext_ref, raw_ref, state_ref, gated_ref, keep_ref) = refs[:4], refs[4:]
    conv_ref, head_ref, wide_ref, spread_ref = tables

    @pl.when(pl.program_id(1) == 0)
    def _():
        state_ref[...] = jnp.zeros_like(state_ref)
        ext_ref[0:8] = jnp.zeros_like(ext_ref[0:8])

    @pl.when((pl.program_id(0) == 0) & (pl.program_id(1) == 0))
    def _():
        raw_ref[...] = jnp.zeros_like(raw_ref)
        prepare(layer, params, tables)

    stream = tokens_ref[...].astype(f32)
    if layer > 0:
        stream = stream + mm(before_ref[...], w_out_ref[...])
        stream_ref[...] = stream
    normed = stream * norm_scale(stream) * params[0][layer : layer + 1]
    normed_ref[...] = normed.T.astype(bf16)
    proj_ref[...] = mm(normed.astype(bf16), w_in_ref[...])
    ext_ref[8 : 8 + CH] = proj_ref[:, DI : DI + CONV_CH]
    shifted, step, cum, cum_t, grow, remain, rows, cols = step_parts(proj_ref, raw_ref, head_ref)
    spread = spread_ref[...]
    step_w = widen(step, spread)
    grow_w = widen(grow, spread)
    remain_w = widen(remain * step, spread)

    def activated(j):
        value = conv_block(ext_ref, conv_ref, j)
        return value * sigmoid(value)

    b_low = activated(PAIRS).astype(bf16)
    c_low = activated(PAIRS + 1).astype(bf16)
    affinity = jnp.where(cols <= rows, mm_t(c_low, b_low), 0.0)
    state_low = state_ref[...].astype(bf16)
    saved_ref[...] = state_low
    carried = grow_w * mm(c_low, state_low)
    square = jnp.zeros((CH, LANE), f32)
    for j in range(PAIRS):
        xs = activated(j)
        mixing = []
        for h in (2 * j, 2 * j + 1):
            differ = jnp.minimum(cum[:, h : h + 1] - cum_t[h : h + 1], 0.0)
            mixing.append((jnp.exp2(differ) * affinity).astype(bf16))
        keep_ref[:, lanes(j)] = (xs * remain_w[:, lanes(j)]).astype(bf16)
        x_split = split_pair((xs * step_w[:, lanes(j)]).astype(bf16))
        scanned = mm(jnp.concatenate(mixing, axis=1), x_split) + carried[:, lanes(j)]
        scan_ref[:, lanes(j)] = scanned
        gate = proj_ref[:, lanes(j)]
        gated = (scanned + wide_ref[0:1, lanes(j)] * xs) * (gate * sigmoid(gate))
        gated_ref[:, lanes(j)] = gated
        square = square + gated * gated
    state_ref[...] = grow_w[CH - 1 : CH] * state_ref[...] + t_mm(b_low, keep_ref[...])
    scale = lax.rsqrt(jnp.sum(square, axis=1, keepdims=True) * (1.0 / DI) + epsilon)
    mixed_ref[...] = (gated_ref[...] * scale * wide_ref[1:2]).astype(bf16)
    ext_ref[0:8] = ext_ref[CH : CH + 8]


def backward_kernel(layer, *refs):
    params, refs = refs[:7], refs[7:]
    upstream_ref, stream_ref, w_in_ref, w_out_ref, proj_ref, tail_ref, scan_ref, saved_ref, *refs = refs
    top = layer == LAYERS - 1
    if top:
        mixed_ref, length_ref, result_ref, *refs = refs
    out_ref, down_ref, sum_ref, *refs = refs
    tables, refs = refs[:4], refs[4:]
    conv_ref, head_ref, wide_ref, spread_ref = tables
    gather_ref, grad_ref, ext_ref, raw_ref, state_ref, act_ref, slope_ref, gate_ref, dconv_ref, *refs = refs
    keep_ref, grown_ref, high_ref, low_ref, step_ref, row_ref = refs
    chunk = pl.num_programs(1) - 1 - pl.program_id(1)

    @pl.when(pl.program_id(1) == 0)
    def _():
        state_ref[...] = jnp.zeros_like(state_ref)
        dconv_ref[CH : CH + 8] = jnp.zeros_like(dconv_ref[CH : CH + 8])

    @pl.when((pl.program_id(0) == 0) & (pl.program_id(1) == 0))
    def _():
        raw_ref[...] = jnp.zeros_like(raw_ref)
        row_ref[...] = jnp.zeros_like(row_ref)
        sum_ref[...] = jnp.zeros_like(sum_ref)
        prepare(layer, params, tables, gather_ref)

    if top:
        slot = lax.broadcasted_iota(jnp.int32, (CH, D), 0) + chunk * CH
        result = stream_ref[...] + mm(mixed_ref[...], w_out_ref[...])
        result_ref[...] = jnp.where(slot < length_ref[0:1, 0:1], result, 0.0).astype(bf16)
    upstream = upstream_ref[...].astype(f32)
    grad_ref[...] = mm_t(upstream.astype(bf16), w_out_ref[...]).astype(bf16)
    ext_ref[0:8] = jnp.where(chunk > 0, tail_ref[:, DI : DI + CONV_CH], 0.0)
    ext_ref[8 : 8 + CH] = proj_ref[:, DI : DI + CONV_CH]
    shifted, step, cum, cum_t, grow, remain, rows, cols = step_parts(proj_ref, raw_ref, head_ref)
    spread = spread_ref[...]
    step_w = widen(step, spread)
    grow_w = widen(grow, spread)
    remain_w = widen(remain, spread)

    square = jnp.zeros((CH, LANE), f32)
    along = jnp.zeros((CH, LANE), f32)
    for j in range(PAIRS + 2):
        value = conv_block(ext_ref, conv_ref, j)
        share = sigmoid(value)
        xs = value * share
        act_ref[:, lanes(j)] = xs
        slope_ref[:, lanes(j)] = share + xs * (1.0 - share)
        if j < PAIRS:
            gate = proj_ref[:, lanes(j)]
            open_share = sigmoid(gate)
            gate_ref[:, lanes(j)] = open_share
            gated = (scan_ref[:, lanes(j)] + wide_ref[0:1, lanes(j)] * xs) * (gate * open_share)
            square = square + gated * gated
            along = along + gated * (grad_ref[:, lanes(j)].astype(f32) * wide_ref[1:2, lanes(j)])
    scale = lax.rsqrt(jnp.sum(square, axis=1, keepdims=True) * (1.0 / DI) + epsilon)
    pull = scale * scale * scale * (jnp.sum(along, axis=1, keepdims=True) * (1.0 / DI))

    b_low = act_ref[:, lanes(PAIRS)].astype(bf16)
    c_low = act_ref[:, lanes(PAIRS + 1)].astype(bf16)
    affinity_t = jnp.where(rows <= cols, mm_t(b_low, c_low), 0.0)
    state = state_ref[...]
    state_low = state.astype(bf16)
    row_ref[1:2] = jnp.sum(saved_ref[...].astype(f32) * state, axis=0, keepdims=True)
    back = remain_w * mm(b_low, state_low)
    affinity_grad = jnp.zeros((CH, CH), f32)
    for j in range(PAIRS):
        xs = act_ref[:, lanes(j)]
        skip = wide_ref[0:1, lanes(j)]
        grad = grad_ref[:, lanes(j)].astype(f32)
        gate = proj_ref[:, lanes(j)]
        open_share = gate_ref[:, lanes(j)]
        opened = gate * open_share
        scanned = scan_ref[:, lanes(j)]
        outer = scanned + skip * xs
        gated = outer * opened
        gated_grad = scale * (grad * wide_ref[1:2, lanes(j)]) - pull * gated
        sum_ref[6:7, lanes(j)] += jnp.sum(grad * (gated * scale), axis=0, keepdims=True)
        dy = gated_grad * opened
        out_ref[:, lanes(j)] = (gated_grad * outer * (open_share + opened * (1.0 - open_share))).astype(bf16)
        sum_ref[5:6, lanes(j)] += jnp.sum(dy * xs, axis=0, keepdims=True)
        dy_low = dy.astype(bf16)
        grown_ref[:, lanes(j)] = (grow_w[:, lanes(j)] * dy).astype(bf16)
        scaled = xs * step_w[:, lanes(j)]
        x_low = scaled.astype(bf16)
        keep_ref[:, lanes(j)] = (scaled * remain_w[:, lanes(j)]).astype(bf16)
        dy_split = split_pair(dy_low)
        kernels = []
        for h in (2 * j, 2 * j + 1):
            differ = jnp.minimum(cum_t[h : h + 1] - cum[:, h : h + 1], 0.0)
            kernels.append(jnp.exp2(differ))
        mixing_t = jnp.concatenate([(k * affinity_t).astype(bf16) for k in kernels], axis=1)
        arrived = back[:, lanes(j)]
        x_grad = mm(mixing_t, dy_split) + arrived
        mixing_grad = mm_t(x_low, dy_split)
        affinity_grad = affinity_grad + mixing_grad[:, :CH] * kernels[0] + mixing_grad[:, CH:] * kernels[1]
        x_back = x_low.astype(f32)
        row_ref[0:1, lanes(j)] = jnp.sum(x_back * arrived, axis=0, keepdims=True)
        high, low = high_low(dy_low.astype(f32) * scanned - x_back * x_grad)
        high_ref[:, lanes(j)] = high
        low_ref[:, lanes(j)] = low
        step_ref[:, lanes(j)] = (x_grad * xs).astype(bf16)
        dconv_ref[0:CH, lanes(j)] = (step_w[:, lanes(j)] * x_grad + skip * dy) * slope_ref[:, lanes(j)]
    affinity_low = jnp.where(rows <= cols, affinity_grad, 0.0).astype(bf16)
    grown = grown_ref[...]
    b_grad = mm(affinity_low, c_low) + mm_t(keep_ref[...], state_low)
    c_grad = t_mm(affinity_low, b_low) + mm_t(grown, saved_ref[...])
    dconv_ref[0:CH, lanes(PAIRS)] = b_grad * slope_ref[:, lanes(PAIRS)]
    dconv_ref[0:CH, lanes(PAIRS + 1)] = c_grad * slope_ref[:, lanes(PAIRS + 1)]

    gather = gather_ref[...]
    row_high, row_low = high_low(row_ref[...])
    row_sums = mm(row_high, gather) + mm(row_low, gather)
    last_grad = row_sums[0:1] + grow[CH - 1 : CH] * row_sums[1:2]
    cum_grad = mm(high_ref[...], gather) + mm(low_ref[...], gather)
    upper = (cols >= rows).astype(f32)
    decay_grad = jnp.dot(upper, cum_grad, precision=highest, preferred_element_type=f32) + last_grad
    step_grad = mm(step_ref[...], gather) + head_ref[2:3] * decay_grad
    raw_grad = step_grad * sigmoid(shifted)
    out_ref[:, DI + CONV_CH :] = raw_grad[:, :NH].astype(bf16)
    sum_ref[7:8, 0:LANE] += jnp.sum(raw_grad, axis=0, keepdims=True)
    sum_ref[7:8, LANE : 2 * LANE] += jnp.sum(decay_grad * step, axis=0, keepdims=True)
    state_ref[...] = grow_w[CH - 1 : CH] * state + t_mm(c_low, grown)

    for j in range(PAIRS + 2):
        total = conv_ref[3:4, lanes(j)] * dconv_ref[0:CH, lanes(j)]
        for k in range(KW - 1):
            total = total + conv_ref[k : k + 1, lanes(j)] * dconv_ref[3 - k : 3 - k + CH, lanes(j)]
        out_ref[:, lanes(j, DI)] = total.astype(bf16)
        here = dconv_ref[0:CH, lanes(j)]
        for k in range(KW):
            sum_ref[k : k + 1, lanes(j)] += jnp.sum(here * ext_ref[5 + k : 5 + k + CH, lanes(j)], axis=0, keepdims=True)
        sum_ref[4:5, lanes(j)] += jnp.sum(here, axis=0, keepdims=True)
    dconv_ref[CH : CH + 8] = dconv_ref[0:8]

    edge = DI + CONV_CH
    normed_grad = mm_t(out_ref[:, :edge], w_in_ref[:, :edge]) + mm_t(out_ref[:, edge:], w_in_ref[:, edge:])
    stream = stream_ref[...].astype(f32)
    scale = norm_scale(stream)
    sum_ref[7:8, 2 * LANE : 2 * LANE + D] += jnp.sum(normed_grad * (stream * scale), axis=0, keepdims=True)
    inner = normed_grad * params[0][layer : layer + 1]
    pull = scale * scale * scale * jnp.mean(inner * stream, axis=-1, keepdims=True)
    down_ref[...] = upstream_ref[...].astype(f32) + scale * inner - pull * stream


def ring_place(n):
    wide = n // 4
    me = lax.axis_index("shard")
    chip, core = me // 2, me % 2
    row, col = chip // wide, chip % wide
    place = row * (2 * wide - 1 - col) + (1 - row) * col

    def shard_of(at, c):
        at = at % (2 * wide)
        r = at // wide
        x = r * (2 * wide - 1 - at) + (1 - r) * at
        return (r * wide + x) * 2 + c

    return place, core, shard_of


def halves(rows):
    first = rows // 2 // 16 * 16
    return (0, first), (first, rows - first)


def aligned(start, size, unit=16):
    return pl.ds(pl.multiple_of(start, unit), size)


def column_groups(width, replicas, parts):
    unit = LANE * replicas
    units = -(-width // unit)
    parts = min(parts, units)
    groups, start = [], 0
    for g in range(parts):
        size = (units // parts + (g < units % parts)) * unit
        groups.append((start, size, min(size, width - start)))
        start += size
    return groups, start


def remote(src, dst, send, recv, axis, to):
    return pltpu.make_async_remote_copy(
        src_ref=src, dst_ref=dst, send_sem=send, recv_sem=recv, device_id={axis: to}, device_id_type=MESH
    )


def greet(near, across):
    barrier = pltpu.get_barrier_semaphore()
    for to in near:
        pl.semaphore_signal(barrier, inc=1, device_id={"shard": to}, device_id_type=MESH)
    for to in across:
        pl.semaphore_signal(barrier, inc=1, device_id={"replica": to}, device_id_type=MESH)


def meet(count):
    pl.semaphore_wait(pltpu.get_barrier_semaphore(), count)


def bits(count):
    levels = count.bit_length() - 1
    assert 1 << levels == count
    return levels


class Gather:
    def __init__(self, n, arrays, items):
        self.n, self.half = n, n // 4
        self.arrays, self.items = arrays, items
        self.rows = [arrays[i[0]].shape[1] for i in items]

    def in_specs(self):
        return [pl.BlockSpec(memory_space=pl.ANY)] * len(self.arrays)

    out_specs = in_specs

    def out_shapes(self):
        return [jax.ShapeDtypeStruct((a.shape[1] * self.n, a.shape[2]), a.dtype) for a in self.arrays]

    def scratch(self):
        count = len(self.items)
        dma = pltpu.SemaphoreType.DMA
        own = [pltpu.VMEM((rows, i[3]), self.arrays[i[0]].dtype) for rows, i in zip(self.rows, self.items)]
        return [dma((count, self.half, 2, 2)), dma((count, self.half + 1, 2, 2)), dma((count, 2))] + own

    def tracks(self, parts, wholes, scratch):
        ring_sem, pair_sem, own_sem, *own_refs = scratch
        n, half = self.n, self.half
        place, core, shard_of = ring_place(n)
        right, left, pair = shard_of(place + 1, core), shard_of(place + n // 2 - 1, core), shard_of(place, 1 - core)
        me = shard_of(place, core)
        ways = ((0, right), (1, left))

        def rows_of(i, s, d):
            return (0, self.rows[i]) if s < half else halves(self.rows[i])[d]

        def part_at(i, part):
            a, layer, first, wide = self.items[i]
            return parts[a].at[layer, part[0] : part[0] + part[1], first : first + wide]

        def whole_at(i, owner, part):
            a, _, first, wide = self.items[i]
            return wholes[a].at[aligned(owner * self.rows[i] + part[0], part[1]), first : first + wide]

        def hop(i, s, d, to):
            owner = shard_of(place + (n // 2 - (s - 1) if d == 0 else s - 1), core)
            part = rows_of(i, s, d)
            src = part_at(i, part) if s == 1 else whole_at(i, owner, part)
            return remote(src, whole_at(i, owner, part), ring_sem.at[i, s - 1, d, 0], ring_sem.at[i, s - 1, d, 1], "shard", to)

        def cross(i, s, d):
            owner = me if s == 0 else shard_of(place + (n // 2 - s if d == 0 else s), core)
            part = (0, self.rows[i]) if s == 0 else rows_of(i, s, d)
            src = part_at(i, part) if s == 0 else whole_at(i, owner, part)
            return remote(src, whole_at(i, owner, part), pair_sem.at[i, s, d, 0], pair_sem.at[i, s, d, 1], "shard", pair)

        def own_in(i):
            return pltpu.make_async_copy(part_at(i, (0, self.rows[i])), own_refs[i], own_sem.at[i, 0])

        def own_out(i):
            return pltpu.make_async_copy(own_refs[i], whole_at(i, me, (0, self.rows[i])), own_sem.at[i, 1])

        crossings = [(0, 0)] + [(s, d) for s in range(1, half + 1) for d in (0, 1)]

        def start(i):
            for d, to in ways:
                hop(i, 1, d, to).start()
            cross(i, 0, 0).start()
            own_in(i).start()

        def forward(i, s):
            if s == 1:
                own_in(i).wait()
                own_out(i).start()
            for d, to in ways:
                hop(i, s, d, to).wait_recv()
                if s < half:
                    hop(i, s + 1, d, to).start()
                cross(i, s, d).start()

        def last(i):
            for s, d in crossings:
                cross(i, s, d).wait_recv()
            for s, d in crossings:
                cross(i, s, d).wait_send()
            for s in range(1, half + 1):
                for d, to in ways:
                    hop(i, s, d, to).wait_send()
            own_out(i).wait()

        hello = [lambda: greet((right, left, pair), ()), lambda: meet(3)]
        return hello, [
            [lambda i=i: start(i)]
            + [lambda i=i, s=s: forward(i, s) for s in range(1, half + 1)]
            + [lambda i=i: last(i)]
            for i in range(len(self.items))
        ]


class Reduce:
    def __init__(self, n, replicas, shapes, groups):
        self.n, self.replicas = n, replicas
        self.chips, self.half, self.levels = n // 2, n // 4, bits(replicas)
        self.shapes = [(r // n, w) for r, w in shapes]
        self.groups = [column_groups(w, replicas, count) for (_, w), count in zip(self.shapes, groups)]
        self.work = [(a, g) for a in range(len(shapes)) for g in range(len(self.groups[a][0]))]

    def in_specs(self):
        return [pl.BlockSpec(memory_space=pl.ANY)] * len(self.shapes)

    out_specs = in_specs

    def out_shapes(self):
        return [jax.ShapeDtypeStruct(s, f32) for s in self.shapes]

    each = 12

    def scratch(self):
        dma = pltpu.SemaphoreType.DMA
        items = []
        for (rows, width), (groups, padded) in zip(self.shapes, self.groups):
            g = len(groups)
            items += [
                pltpu.VMEM((self.chips, rows, width), bf16),
                pltpu.VMEM((self.chips, rows, width), bf16),
                pltpu.VMEM((self.half, 2, rows, width), bf16),
                pltpu.VMEM((self.half, 2, rows, width), bf16),
                pltpu.VMEM((rows, padded), bf16),
                pltpu.VMEM((self.levels, rows, padded), bf16),
                pltpu.VMEM((rows, padded), bf16),
                pltpu.VMEM((rows, width), f32),
                dma((g, self.chips, 3)), dma((g, self.half, 2, 2)), dma((g, 2 * self.levels, 2)), dma((g,)),
            ]
        return items

    def tracks(self, ins, outs, scratch, feed=None):
        n, replicas, chips, half, levels = self.n, self.replicas, self.chips, self.half, self.levels
        place, core, shard_of = ring_place(n)
        right, left, pair = shard_of(place + 1, core), shard_of(place + chips - 1, core), shard_of(place, 1 - core)
        mine = lax.axis_index("replica")
        ways = ((0, right), (1, left))
        order = [half] + [v for s in range(half - 1, 0, -1) for v in (s, chips - s)] + [0]
        buffers = [scratch[self.each * a : self.each * (a + 1)] for a in range(len(self.shapes))]

        def partner(j):
            bit = mine // (1 << j) % 2
            return mine + (1 - 2 * bit) * (1 << j), bit

        def cols_of(a, g):
            start, _, wide = self.groups[a][0][g]
            return slice(start, start + wide)

        def piece(a, g, owner):
            rows = self.shapes[a][0]
            return ins[a].at[aligned(owner * rows, rows), cols_of(a, g)]

        def pairing(a, g, q):
            sem = buffers[a][8]
            src = feed.sent(a, g, q) if feed else piece(a, g, shard_of(place + q, 1 - core))
            return remote(src, buffers[a][1].at[q, :, cols_of(a, g)], sem.at[g, q, 0], sem.at[g, q, 1], "shard", pair)

        def loading(a, g, q):
            return pltpu.make_async_copy(
                piece(a, g, shard_of(place + q, core)), buffers[a][0].at[q, :, cols_of(a, g)], buffers[a][8].at[g, q, 2]
            )

        def part_of(a, k, d):
            rows = self.shapes[a][0]
            return halves(rows)[d] if k == 1 else (0, rows)

        def ringing(a, g, k, d, to):
            first, count = part_of(a, k, d)
            sem = buffers[a][9]
            return remote(
                buffers[a][2].at[k - 1, d, first : first + count, cols_of(a, g)],
                buffers[a][3].at[k - 1, d, first : first + count, cols_of(a, g)],
                sem.at[g, k - 1, d, 0], sem.at[g, k - 1, d, 1], "shard", to,
            )

        def region(a, g, j, keep):
            start, size, _ = self.groups[a][0][g]
            at = start
            for i in range(j + 1):
                bit = mine // (1 << i) % 2
                at = at + (bit if keep or i < j else 1 - bit) * (size >> (i + 1))
            return aligned(at, size >> (j + 1), LANE)

        def halving(a, g, j):
            cols = region(a, g, j, False)
            sem = buffers[a][10]
            return remote(
                buffers[a][4].at[:, cols], buffers[a][5].at[j, :, cols], sem.at[g, j, 0], sem.at[g, j, 1], "replica", partner(j)[0]
            )

        def doubling(a, g, j):
            cols = region(a, g, j, True)
            sem = buffers[a][10]
            return remote(
                buffers[a][6].at[:, cols], buffers[a][6].at[:, cols],
                sem.at[g, levels + j, 0], sem.at[g, levels + j, 1], "replica", partner(j)[0],
            )

        def storing(a, g):
            cols = cols_of(a, g)
            return pltpu.make_async_copy(buffers[a][7].at[:, cols], outs[a].at[:, cols], buffers[a][11].at[g])

        def both(a, g, q, part):
            first, count = part
            rows, cols = slice(first, first + count), cols_of(a, g)
            return buffers[a][0][q, rows, cols].astype(f32) + buffers[a][1][q, rows, cols].astype(f32)

        def arrived(a, g, q):
            if not feed:
                loading(a, g, q).wait()
            pairing(a, g, q).wait_recv()

        def begin(a, g):
            for q in order:
                if feed:
                    feed.make(a, g, q, shard_of(place + q, 0), core, buffers[a][0])
                pairing(a, g, q).start()
                if not feed:
                    loading(a, g, q).start()

        def turn(a, g, k):
            cols = cols_of(a, g)
            for d, to in ways:
                q = half - k + 1 if d == 0 else chips - (half - k + 1)
                if k > 1 or d == 0:
                    arrived(a, g, q)
                if k > 1:
                    ringing(a, g, k - 1, d, to).wait_recv()
                pieces = [part_of(a, 1, d)] if k == 1 else halves(self.shapes[a][0]) if k == 2 else [part_of(a, k, d)]
                for e, (at, many) in enumerate(pieces):
                    value = both(a, g, q, (at, many))
                    if k > 2 or (k == 2 and e == d):
                        value = value + buffers[a][3][k - 2, d, at : at + many, cols].astype(f32)
                    buffers[a][2][k - 1, d, at : at + many, cols] = value.astype(bf16)
                ringing(a, g, k, d, to).start()

        def settle(a, g):
            cols = cols_of(a, g)
            start, size, wide = self.groups[a][0][g]
            rows = self.shapes[a][0]
            arrived(a, g, 0)
            value = both(a, g, 0, (0, rows))
            for d, to in ways:
                ringing(a, g, half, d, to).wait_recv()
                value = value + buffers[a][3][half - 1, d, :, cols].astype(f32)
            buffers[a][4][:, cols] = value.astype(bf16)
            if wide < size:
                buffers[a][4][:, start + wide : start + size] = jnp.zeros((rows, size - wide), bf16)
            halving(a, g, 0).start()

        def halve(a, g, j):
            halving(a, g, j).wait_recv()
            cols = region(a, g, j, True)
            value = (buffers[a][4][:, cols].astype(f32) + buffers[a][5][j, :, cols].astype(f32)).astype(bf16)
            if j + 1 < levels:
                buffers[a][4][:, cols] = value
                halving(a, g, j + 1).start()
            else:
                buffers[a][6][:, cols] = value
                doubling(a, g, j).start()

        def double(a, g, j):
            doubling(a, g, j).wait_recv()
            if j > 0:
                doubling(a, g, j - 1).start()

        def last(a, g):
            double(a, g, 0)
            cols = cols_of(a, g)
            buffers[a][7][:, cols] = buffers[a][6][:, cols].astype(f32)
            storing(a, g).start()
            for q in order:
                pairing(a, g, q).wait_send()
            for k in range(1, half + 1):
                for d, to in ways:
                    ringing(a, g, k, d, to).wait_send()
            for j in range(levels):
                halving(a, g, j).wait_send()
                doubling(a, g, j).wait_send()
            storing(a, g).wait()

        across = [partner(j)[0] for j in range(levels)]
        hello = [lambda: greet((right, left, pair), across), lambda: meet(3 + levels)]
        return hello, [
            [lambda a=a, g=g: begin(a, g)]
            + [lambda a=a, g=g, k=k: turn(a, g, k) for k in range(1, half + 1)]
            + [lambda a=a, g=g: settle(a, g)]
            + [lambda a=a, g=g, j=j: halve(a, g, j) for j in range(levels)]
            + [lambda a=a, g=g, j=j: double(a, g, j) for j in range(levels - 1, 0, -1)]
            + [lambda a=a, g=g: last(a, g)]
            for a, g in self.work
        ]


def beside(body, counts, engine, times, hooks):
    ins, outs, scratch = counts

    def kernel(*refs):
        i = len(engine.in_specs())
        o = len(engine.out_specs())
        own_in, refs = refs[:ins], refs[ins:]
        far_in, refs = refs[:i], refs[i:]
        own_out, refs = refs[:outs], refs[outs:]
        far_out, refs = refs[:o], refs[o:]
        own_scratch, far_scratch = refs[:scratch], refs[scratch:]
        hello, tracks = engine.tracks(far_in, far_out, far_scratch)
        plan = {}
        plan[0] = [hello[0]]
        plan.setdefault(min(t[0] for t in times), []).append(hello[1])
        for t, track in enumerate(tracks):
            wanted = times[t]
            if len(wanted) != len(track):
                first = wanted[0]
                wanted = [first + (hooks - first) * i // (len(track) - 1) for i in range(len(track))]
            for at, stage in zip(wanted, track):
                plan.setdefault(min(at, hooks), []).append(stage)
        step = pl.program_id(0) * pl.num_programs(1) + pl.program_id(1)

        def run(at):
            for stage in plan[at]:
                stage()

        pl.when(step == 0)(lambda: run(0))
        body(*own_in, *own_out, *own_scratch)
        for at in sorted(plan):
            if at > 0:
                pl.when(step == at - 1)(lambda at=at: run(at))

    return kernel


def move(engine, operands, collective_id, name):
    def kernel(*refs):
        i, o = len(engine.in_specs()), len(engine.out_specs())
        hello, tracks = engine.tracks(refs[:i], refs[i : i + o], refs[i + o :])
        for stage in hello:
            stage()
        for at in range(max(map(len, tracks))):
            for track in tracks:
                if at < len(track):
                    track[at]()

    return pl.pallas_call(
        kernel,
        out_shape=engine.out_shapes(),
        in_specs=engine.in_specs(),
        out_specs=engine.out_specs(),
        scratch_shapes=engine.scratch(),
        compiler_params=pltpu.CompilerParams(collective_id=collective_id, has_side_effects=True),
        name=name,
    )(*operands)


class Product:
    def __init__(self, left_ref, right_ref, pair_ref, engine):
        self.left, self.right, self.pairs, self.engine = left_ref, right_ref, pair_ref, engine

    def sent(self, a, g, q):
        rows = self.engine.shapes[a][0]
        start, _, wide = self.engine.groups[a][0][g]
        core = lax.axis_index("shard") % 2
        return self.pairs.at[q, aligned((1 - core) * rows, rows), start : start + wide]

    def make(self, a, g, q, owner, core, own_ref):
        rows = self.engine.shapes[a][0]
        start, _, wide = self.engine.groups[a][0][g]
        cols = slice(start, start + wide)
        self.pairs[q, :, cols] = mm(self.left[aligned(owner * rows, 2 * rows), :], self.right[:, cols]).astype(bf16)
        own_ref[q, :, cols] = self.pairs[q, aligned(core * rows, rows), cols]


def finish_kernel(engine, n, replicas, *refs):
    left_ref, right_ref, first_ref, second_ref, in_ref, out0_ref, out1_ref = refs[:7]
    in_total_ref, out_total_ref, total_ref = refs[7:10]
    pair_ref, mine_ref, plane_ref, across_ref, whole_ref, in_buf, out_buf = refs[10:17]
    plane_sem, across_sem, share_sem, copy_sem, *scratch = refs[17:]
    me, mine = lax.axis_index("shard"), lax.axis_index("replica")
    width = mine_ref.shape[2]
    feed = Product(left_ref, right_ref, pair_ref, engine)
    _, tracks = engine.tracks((None,), (in_total_ref.at[0],), scratch, feed)
    greet([(me + s) % n for s in range(1, n)], [(mine + s) % replicas for s in range(1, replicas)])
    moves = [(in_ref, in_buf, in_total_ref.at[1]), (out0_ref, out_buf.at[0], out_total_ref.at[0]), (out1_ref, out_buf.at[1], out_total_ref.at[1])]
    fetches = [pltpu.make_async_copy(src, via, copy_sem.at[0, i]) for i, (src, via, _) in enumerate(moves)]
    stores = [pltpu.make_async_copy(via, dst, copy_sem.at[1, i]) for i, (_, via, dst) in enumerate(moves)]
    for fetch in fetches:
        fetch.start()
    spots = [(k // (n // 2), k % (n // 2) * width) for k in range(n)]
    for k, (half, at) in enumerate(spots):
        mine_ref[k] = (second_ref if half else first_ref)[:, at : at + width]

    def plane(s):
        to = (me + s) % n
        return remote(mine_ref.at[to], plane_ref.at[s], plane_sem.at[0, s], plane_sem.at[1, s], "shard", to)

    def across(s):
        return remote(across_ref.at[0], across_ref.at[s], across_sem.at[0, s], across_sem.at[1, s], "replica", (mine + s) % replicas)

    def share(s):
        return remote(whole_ref.at[me], whole_ref.at[me], share_sem.at[0, s], share_sem.at[1, s], "shard", (me + s) % n)

    def sharing(s):
        owner = (me + n - s) % n
        return remote(whole_ref.at[owner], whole_ref.at[owner], share_sem.at[0, s], share_sem.at[1, s], "shard", (me + s) % n)

    def send_small():
        for s in range(1, n):
            plane(s).start()

    def sum_plane():
        value = mine_ref[me]
        for s in range(1, n):
            plane(s).wait_recv()
            value = value + plane_ref[s]
        across_ref[0] = value
        for s in range(1, replicas):
            across(s).start()

    def sum_across():
        for s in range(1, replicas):
            across(s).wait_recv()
        zero = jnp.zeros((8, width), f32)
        whole_ref[me] = lax.fori_loop(0, replicas, lambda i, acc: acc + across_ref[(mine - i + replicas) % replicas], zero)
        for s in range(1, n):
            share(s).start()

    def give_small():
        for s in range(1, n):
            sharing(s).wait_recv()
        for k, (half, at) in enumerate(spots):
            total_ref[8 * half : 8 * half + 8, at : at + width] = whole_ref[k]

    plan = {}
    for g, track in enumerate(tracks):
        for i, stage in enumerate(track):
            plan.setdefault((g + (2 * i - 1 if i else 0), -i), []).append(stage)
    meet(n + replicas - 2)
    slots = sorted(plan)
    for k, slot in enumerate(slots):
        for stage in plan[slot]:
            stage()
        if k == 0:
            send_small()
        if k == len(slots) // 4:
            sum_plane()
            for fetch, store in zip(fetches, stores):
                fetch.wait()
                store.start()
        if k == len(slots) // 2:
            sum_across()
    give_small()
    for s in range(1, n):
        plane(s).wait_send()
        share(s).wait_send()
    for s in range(1, replicas):
        across(s).wait_send()
    for store in stores:
        store.wait()


def finish(left, right, sums, in_grad, out_grads, n, replicas, collective_id):
    engine = Reduce(n, replicas, [(left.shape[0], right.shape[1])], [7])
    rows, width = engine.shapes[0]
    anywhere, vmem = pl.BlockSpec(memory_space=pl.ANY), pl.BlockSpec(memory_space=pltpu.VMEM)
    dma = pltpu.SemaphoreType.DMA
    small = (8, 2 * SUMS // n)
    return pl.pallas_call(
        lambda *refs: finish_kernel(engine, n, replicas, *refs),
        out_shape=[
            jax.ShapeDtypeStruct((LAYERS, rows, width), f32),
            jax.ShapeDtypeStruct((LAYERS,) + out_grads[0].shape, f32),
            jax.ShapeDtypeStruct((LAYERS * 8, SUMS), f32),
        ],
        in_specs=[vmem] * 4 + [anywhere] * 3,
        out_specs=[anywhere, anywhere, vmem],
        scratch_shapes=[
            pltpu.VMEM((n // 2, 2 * rows, width), bf16),
            pltpu.VMEM((n,) + small, f32),
            pltpu.VMEM((n,) + small, f32),
            pltpu.VMEM((replicas,) + small, f32),
            pltpu.VMEM((n,) + small, f32),
            pltpu.VMEM((rows, width), f32),
            pltpu.VMEM((LAYERS,) + out_grads[0].shape, f32),
            dma((2, n)), dma((2, replicas)), dma((2, n)), dma((2, 3)),
        ] + engine.scratch(),
        compiler_params=pltpu.CompilerParams(collective_id=collective_id, has_side_effects=True, vmem_limit_bytes=60 * 2**20),
        name="finish",
    )(left, right, *sums, in_grad, *out_grads)


def small_kernel(total_ref, a_log_ref, gain_ref, conv_w_ref, conv_b_ref, dt_bias_ref, a_log_grad_ref, d_skip_ref, out_gain_ref):
    column = lax.broadcasted_iota(jnp.int32, (DI, LANE), 1)
    owner = lax.broadcasted_iota(jnp.int32, (DI, LANE), 0) // HEAD
    gather = (column == owner).astype(f32).astype(bf16)
    for l in range(LAYERS):
        here, row = slice(l, l + 1), 8 * l
        gain_ref[here] = total_ref[row + 7 : row + 8, 2 * LANE : 2 * LANE + D]
        conv_w_ref[l] = total_ref[row : row + KW, :CONV_CH]
        conv_b_ref[here] = total_ref[row + 4 : row + 5, :CONV_CH]
        dt_bias_ref[here] = total_ref[row + 7 : row + 8, 0:NH]
        a_log_grad_ref[here] = -jnp.exp(a_log_ref[here]) * total_ref[row + 7 : row + 8, LANE : LANE + NH]
        out_gain_ref[here] = total_ref[row + 6 : row + 7, :DI]
        value = total_ref[row : row + 8, :DI]
        high = value.astype(bf16)
        middle = (value - high.astype(f32)).astype(bf16)
        low = (value - high.astype(f32) - middle.astype(f32)).astype(bf16)
        summed = mm(high, gather) + mm(middle, gather) + mm(low, gather)
        d_skip_ref[here] = summed[5:6, 0:NH]


def small_results(total, params):
    return pl.pallas_call(
        small_kernel,
        out_shape=[jax.ShapeDtypeStruct(p.shape, f32) for p in params],
        name="small_results",
    )(total, params[4])


def product_kernel(left_ref, right_ref, out_ref):
    out_ref[...] = mm(left_ref[...], right_ref[...]).astype(bf16)


def product(left, right, wide):
    (rows, depth), width = left.shape, right.shape[1]
    return pl.pallas_call(
        product_kernel,
        grid=(pl.cdiv(width, wide),),
        in_specs=[pl.BlockSpec((rows, depth), lambda c: (0, 0)), pl.BlockSpec((depth, wide), lambda c: (0, c))],
        out_specs=pl.BlockSpec((rows, wide), lambda c: (0, c)),
        out_shape=jax.ShapeDtypeStruct((rows, width), bf16),
        compiler_params=pltpu.CompilerParams(vmem_limit_bytes=48 * 2**20),
        name="product",
    )(left, right)


def fixed(shape):
    return pl.BlockSpec(shape, lambda r, c: (0,) * len(shape))


def held(shape):
    return pl.BlockSpec(shape, lambda r, c: (0,) * len(shape), pipeline_mode=pl.Buffered(1))


def grid_call(body, grid, operands, in_specs, out_specs, out_shapes, scratch, name, extra):
    engine, given, times, collective_id = extra
    kernel = beside(body, (len(in_specs), len(out_specs), len(scratch)), engine, times, grid[0] * grid[1])
    return pl.pallas_call(
        kernel, grid=grid, in_specs=in_specs + engine.in_specs(), out_specs=out_specs + engine.out_specs(),
        out_shape=out_shapes + engine.out_shapes(), scratch_shapes=scratch + engine.scratch(),
        compiler_params=pltpu.CompilerParams(
            dimension_semantics=("arbitrary", "arbitrary"), vmem_limit_bytes=60 * 2**20,
            collective_id=collective_id, has_side_effects=True,
        ),
        name=name,
    )(*operands, *given)


def layer_forward(layer, tokens, w_in, before, w_out, params, chunks, extra):
    count = tokens.shape[0]
    block = lambda r, c: (r * chunks + c, 0)
    later = layer > 0
    rows = lambda width: pl.BlockSpec((CH, width), block)
    return grid_call(
        lambda *refs: forward_kernel(layer, *refs),
        (count // (chunks * CH), chunks),
        (*params, tokens, w_in) + ((before, w_out) if later else ()),
        [held(p.shape) for p in params] + [rows(D), held((D, NIN))] + ([rows(DI), held((DI, D))] if later else []),
        ([rows(D)] if later else [])
        + [pl.BlockSpec((D, CH), lambda r, c: (0, r * chunks + c)), rows(NIN), rows(DI), rows(DI), pl.BlockSpec((NSTATE, DI), block)],
        ([jax.ShapeDtypeStruct((count, D), f32)] if later else [])
        + [
            jax.ShapeDtypeStruct((D, count), bf16),
            jax.ShapeDtypeStruct((count, NIN), f32),
            jax.ShapeDtypeStruct((count, DI), bf16),
            jax.ShapeDtypeStruct((count, DI), f32),
            jax.ShapeDtypeStruct((count // CH * NSTATE, DI), bf16),
        ],
        table_scratch()
        + [
            pltpu.VMEM((CH + 8, CONV_CH), f32),
            pltpu.VMEM((CH, LANE), f32),
            pltpu.VMEM((NSTATE, DI), f32),
            pltpu.VMEM((CH, DI), f32),
            pltpu.VMEM((CH, DI), bf16),
        ],
        f"layer_forward_{layer}", extra,
    )


def layer_backward(layer, upstream, stream, w_in, w_out, projected, scanned, saved, mixed, length, params, chunks, extra):
    count = projected.shape[0]
    block = lambda r, c: (r * chunks + chunks - 1 - c, 0)
    ahead = lambda r, c: (jnp.maximum((r * chunks + chunks - 1 - c) * (CH // 8) - 1, 0), 0)
    rows = lambda width: pl.BlockSpec((CH, width), block)
    top = layer == LAYERS - 1
    return grid_call(
        lambda *refs: backward_kernel(layer, *refs),
        (count // (chunks * CH), chunks),
        (*params, upstream, stream, w_in, w_out, projected, projected, scanned, saved) + ((mixed, length) if top else ()),
        [held(p.shape) for p in params]
        + [rows(D), rows(D), held((D, NIN)), held((DI, D)), rows(NIN), pl.BlockSpec((8, NIN), ahead), rows(DI), pl.BlockSpec((NSTATE, DI), block)]
        + ([rows(DI), pl.BlockSpec((8, LANE), lambda r, c: (r, 0))] if top else []),
        ([rows(D)] if top else []) + [rows(NIN), rows(D), fixed((8, SUMS))],
        ([jax.ShapeDtypeStruct((count, D), bf16)] if top else [])
        + [
            jax.ShapeDtypeStruct((count, NIN), bf16),
            jax.ShapeDtypeStruct((count, D), f32),
            jax.ShapeDtypeStruct((8, SUMS), f32),
        ],
        table_scratch()
        + [
            pltpu.VMEM((DI, LANE), bf16),
            pltpu.VMEM((CH, DI), bf16),
            pltpu.VMEM((CH + 8, CONV_CH), f32),
            pltpu.VMEM((CH, LANE), f32),
            pltpu.VMEM((NSTATE, DI), f32),
            pltpu.VMEM((CH, CONV_CH), f32),
            pltpu.VMEM((CH, CONV_CH), f32),
            pltpu.VMEM((CH, DI), f32),
            pltpu.VMEM((CH + 8, CONV_CH), f32),
            pltpu.VMEM((CH, DI), bf16),
            pltpu.VMEM((CH, DI), bf16),
            pltpu.VMEM((CH, DI), bf16),
            pltpu.VMEM((CH, DI), bf16),
            pltpu.VMEM((CH, DI), bf16),
            pltpu.VMEM((8, DI), f32),
        ],
        f"layer_backward_{layer}", extra,
    )


def shards(
    tokens, cotangent, lengths, dealing, in_gain, w_in, conv_w, conv_b, dt_bias, a_log, d_skip, out_gain, w_out,
):
    n, replicas = lax.axis_size("shard"), lax.axis_size("replica")
    row_total = replicas * n
    row_index = lax.axis_index("replica") * n + lax.axis_index("shard")
    slot_count = tokens.shape[2]
    chunks = slot_count // CH
    count = MICRO * slot_count
    params = (in_gain, conv_w, conv_b, dt_bias, a_log, d_skip, out_gain)
    flat = tokens.reshape(count, D)

    (first_in,) = move(Gather(n, [w_in], [(0, 0, c, min(CUT, NIN - c)) for c in range(0, NIN, CUT)]), (w_in,), 1, "gather_first")
    engine = Gather(n, [w_out, w_in], [(0, 0, 0, D), (1, 1, 0, CUT), (1, 1, CUT, NIN - CUT)])
    normed0, projected0, mixed0, scanned0, states0, first_out, second_in = layer_forward(
        0, flat, first_in, None, None, params, chunks, (engine, (w_out, w_in), GATHER_BOTH, 2)
    )
    engine = Gather(n, [w_out], [(0, 1, 0, D)])
    stream, normed1, projected1, mixed1, scanned1, states1, second_out = layer_forward(
        1, flat, second_in, mixed0, first_out, params, chunks, (engine, (w_out,), GATHER_LAST, 3)
    )

    global_rows = jnp.arange(MICRO) * row_total + row_index
    sequence = jnp.sum(jnp.where(jnp.arange(dealing.shape[0])[None] == global_rows[:, None], dealing[None], 0), axis=1)
    seq_length = jnp.sum(jnp.where(jnp.arange(lengths.shape[0])[None] == sequence[:, None], lengths[None], 0), axis=1)
    valid = jnp.arange(slot_count)[None] < seq_length[:, None]
    upstream = jnp.where(valid[:, :, None], cotangent[:, 0], 0).astype(bf16).reshape(count, D)
    length = jnp.broadcast_to(seq_length[:, None, None], (MICRO, 8, LANE)).reshape(MICRO * 8, LANE)

    out_grad1 = t_mm(mixed1, upstream).astype(bf16)
    engine = Reduce(n, replicas, [out_grad1.shape], [1])
    result, project_grad1, upstream1, sums1, out_total1 = layer_backward(
        1, upstream, stream, second_in, second_out, projected1, scanned1, states1, mixed1, length, params, chunks,
        (engine, (out_grad1,), REDUCE_OUT, 4),
    )
    in_grad1 = product(normed1, project_grad1, 512)
    out_grad0 = t_mm(mixed0, upstream1.astype(bf16)).astype(bf16)
    engine = Reduce(n, replicas, [out_grad0.shape, in_grad1.shape], [1, 2])
    project_grad0, upstream0, sums0, out_total0, in_total1 = layer_backward(
        0, upstream1, flat, first_in, first_out, projected0, scanned0, states0, None, None, params, chunks,
        (engine, (out_grad0, in_grad1), REDUCE_BOTH, 5),
    )
    in_total, out_total, small = finish(
        normed0, project_grad0, (sums0, sums1), in_total1, (out_total0, out_total1), n, replicas, 6
    )
    gain_grad, *small = small_results(small, params)
    shape = (MICRO, 1, slot_count, D)
    return (result.reshape(shape), upstream0.reshape(shape), gain_grad, in_total, *small, out_total)


def solution(mesh):
    rows = P(None, ("replica", "shard"), None, None)
    split = P(None, "shard", None)
    in_specs = (rows, rows, P(), P(), P(), split, P(), P(), P(), P(), P(), P(), split)
    out_specs = (rows, rows, P(), split, P(), P(), P(), P(), P(), P(), split)
    return jax.shard_map(shards, mesh=mesh, in_specs=in_specs, out_specs=out_specs, check_vma=False)
```

```python
import jax
import jax.numpy as jnp
from jax import lax
from jax.experimental import pallas as pl
from jax.experimental.pallas import tpu as pltpu
from jax.sharding import PartitionSpec as P

D = 768
DI = 1536
NH = 24
HEAD = 64
NSTATE = 128
KW = 4
CONV_CH = 1792
NIN = 3352
LAYERS = 2
MICRO = 2
CH = 128
PAIRS = NH // 2
LANE = 128
DUP = 32
LOG2E = 1.4426950408889634
SUMS = 2048
CUT = 1664
GATHER_BOTH = ((0, 3, 7, 8), (0, 5, 8, 8), (0, 7, 8, 8))
GATHER_LAST = ((1, 4, 6, 8),)
REDUCE_OUT = ((1, 2, 3, 4, 5, 6, 7, 8),)
REDUCE_BOTH = ((0, 1, 2, 3, 4, 5, 6, 7), (0, 1, 2, 4, 5, 6, 7, 8), (0, 3, 5, 7, 8))

epsilon = 1e-05
f32 = jnp.float32
bf16 = jnp.bfloat16
MESH = pl.DeviceIdType.MESH


def mm(a, b):
    return jnp.dot(a, b, preferred_element_type=f32)


def mm_t(a, b):
    return lax.dot_general(a, b, (((1,), (1,)), ((), ())), preferred_element_type=f32)


def t_mm(a, b):
    return lax.dot_general(a, b, (((0,), (0,)), ((), ())), preferred_element_type=f32)


def sigmoid(v):
    return 0.5 * jnp.tanh(0.5 * v) + 0.5


def softplus(v):
    return jnp.maximum(v, 0.0) + jnp.log1p(jnp.exp(-jnp.abs(v)))


def lanes(j, base=0):
    return slice(base + LANE * j, base + LANE * (j + 1))


def norm_scale(stream):
    return lax.rsqrt(jnp.mean(stream * stream, axis=-1, keepdims=True) + epsilon)


def split_pair(v):
    left = lax.broadcasted_iota(jnp.int32, v.shape, 1) < HEAD
    zero = jnp.zeros_like(v)
    return jnp.concatenate([jnp.where(left, v, zero), jnp.where(left, zero, v)], axis=0)


def high_low(v):
    high = v.astype(bf16)
    return high, (v - high.astype(f32)).astype(bf16)


def widen(spread, *values):
    parts = []
    for v in values:
        high, low = high_low(v)
        first = lax.broadcasted_iota(jnp.int32, v.shape, 1) < DUP
        parts.append(jnp.where(first, high, low))
    rows = values[0].shape[0]
    wide = mm(jnp.concatenate(parts, axis=0), spread)
    return [wide[i * rows : (i + 1) * rows] for i in range(len(values))]


def exact_mm(mask, v):
    high, low = high_low(v)
    rest = (v - high.astype(f32) - low.astype(f32)).astype(bf16)
    out = mm(mask.astype(f32).astype(bf16), jnp.concatenate([high, low, rest], axis=1))
    return out[:, :LANE] + out[:, LANE : 2 * LANE] + out[:, 2 * LANE :]


def step_parts(proj_ref, raw_ref, head_ref):
    raw = proj_ref[:, DI + CONV_CH :]
    raw_ref[:, 0:NH] = raw
    raw_ref[:, DUP : DUP + NH] = raw
    shifted = raw_ref[...] + head_ref[0:1]
    step = softplus(shifted)
    rows = lax.broadcasted_iota(jnp.int32, (CH, CH), 0)
    cols = lax.broadcasted_iota(jnp.int32, (CH, CH), 1)
    cum = jnp.dot((cols <= rows).astype(f32), head_ref[1:2] * step, precision=lax.Precision.HIGHEST, preferred_element_type=f32)
    grow = jnp.exp2(cum)
    remain = jnp.exp2(cum[CH - 1 : CH] - cum)
    return shifted, step, cum, cum.T, grow, remain, rows, cols


def conv_block(ext_ref, conv_ref, j):
    total = conv_ref[4:5, lanes(j)]
    for k in range(KW):
        total = total + conv_ref[k : k + 1, lanes(j)] * ext_ref[5 + k : 5 + k + CH, lanes(j)]
    return total


def prepare(layer, params, tables, gather_ref=None):
    in_gain_ref, conv_w_ref, conv_b_ref, dt_bias_ref, a_log_ref, d_skip_ref, out_gain_ref = params
    conv_ref, head_ref, wide_ref, spread_ref = tables
    conv_ref[0:KW] = conv_w_ref[layer]
    conv_ref[KW : KW + 1] = conv_b_ref[layer : layer + 1]
    head_ref[...] = jnp.zeros_like(head_ref)
    rate = -jnp.exp(a_log_ref[layer : layer + 1])
    for row, value in enumerate((dt_bias_ref[layer : layer + 1], rate * LOG2E, rate, d_skip_ref[layer : layer + 1])):
        head_ref[row : row + 1, 0:NH] = value
        head_ref[row : row + 1, DUP : DUP + NH] = value
    column = lax.broadcasted_iota(jnp.int32, (LANE, DI), 0)
    owner = lax.broadcasted_iota(jnp.int32, (LANE, DI), 1) // HEAD
    spread_ref[...] = ((column % DUP == owner) & (column < 2 * DUP)).astype(f32).astype(bf16)
    wide_ref[...] = widen(spread_ref[...], head_ref[...])[0]
    wide_ref[0:1] = wide_ref[3:4]
    wide_ref[1:2] = out_gain_ref[layer : layer + 1]
    if gather_ref is not None:
        column = lax.broadcasted_iota(jnp.int32, (DI, LANE), 1)
        owner = lax.broadcasted_iota(jnp.int32, (DI, LANE), 0) // HEAD
        gather_ref[...] = ((column % DUP == owner) & (column < 2 * DUP)).astype(f32).astype(bf16)


def table_scratch():
    return [
        pltpu.VMEM((8, CONV_CH), f32), pltpu.VMEM((8, LANE), f32), pltpu.VMEM((8, DI), f32), pltpu.VMEM((LANE, DI), bf16),
    ]


def forward_kernel(layer, *refs):
    params, (tokens_ref, w_in_ref), refs = refs[:7], refs[7:9], refs[9:]
    if layer > 0:
        before_ref, w_out_ref, stream_ref, *refs = refs
    normed_ref, proj_ref, mixed_ref, scan_ref, saved_ref, act_ref, slope_ref, *refs = refs
    tables, (ext_ref, raw_ref, state_ref, gated_ref, keep_ref) = refs[:4], refs[4:]
    conv_ref, head_ref, wide_ref, spread_ref = tables

    @pl.when(pl.program_id(1) == 0)
    def _():
        state_ref[...] = jnp.zeros_like(state_ref)
        ext_ref[0:8] = jnp.zeros_like(ext_ref[0:8])

    @pl.when((pl.program_id(0) == 0) & (pl.program_id(1) == 0))
    def _():
        raw_ref[...] = jnp.zeros_like(raw_ref)
        prepare(layer, params, tables)

    stream = tokens_ref[...].astype(f32)
    if layer > 0:
        stream = stream + mm(before_ref[...], w_out_ref[...])
        stream_ref[...] = stream
    normed = stream * norm_scale(stream) * params[0][layer : layer + 1]
    normed_ref[...] = normed.T.astype(bf16)
    proj_ref[...] = mm(normed.astype(bf16), w_in_ref[...])
    ext_ref[8 : 8 + CH] = proj_ref[:, DI : DI + CONV_CH]
    shifted, step, cum, cum_t, grow, remain, rows, cols = step_parts(proj_ref, raw_ref, head_ref)
    step_w, grow_w, remain_w = [widen(spread_ref[...], v)[0] for v in (step, grow, remain * step)]

    def activated(j):
        value = conv_block(ext_ref, conv_ref, j)
        share = sigmoid(value)
        result = value * share
        act_ref[:, lanes(j)] = result
        slope_ref[:, lanes(j)] = share + result * (1.0 - share)
        return result

    b_low = activated(PAIRS).astype(bf16)
    c_low = activated(PAIRS + 1).astype(bf16)
    affinity = jnp.where(cols <= rows, mm_t(c_low, b_low), 0.0)
    state_low = state_ref[...].astype(bf16)
    saved_ref[...] = state_low
    carried = grow_w * mm(c_low, state_low)
    square = jnp.zeros((CH, LANE), f32)
    for j in range(PAIRS):
        xs = activated(j)
        mixing = []
        for h in (2 * j, 2 * j + 1):
            differ = jnp.minimum(cum[:, h : h + 1] - cum_t[h : h + 1], 0.0)
            mixing.append((jnp.exp2(differ) * affinity).astype(bf16))
        keep_ref[:, lanes(j)] = (xs * remain_w[:, lanes(j)]).astype(bf16)
        x_split = split_pair((xs * step_w[:, lanes(j)]).astype(bf16))
        scanned = mm(jnp.concatenate(mixing, axis=1), x_split) + carried[:, lanes(j)]
        scan_ref[:, lanes(j)] = scanned
        gate = proj_ref[:, lanes(j)]
        gated = (scanned + wide_ref[0:1, lanes(j)] * xs) * (gate * sigmoid(gate))
        gated_ref[:, lanes(j)] = gated
        square = square + gated * gated
    state_ref[...] = grow_w[CH - 1 : CH] * state_ref[...] + t_mm(b_low, keep_ref[...])
    scale = lax.rsqrt(jnp.sum(square, axis=1, keepdims=True) * (1.0 / DI) + epsilon)
    mixed_ref[...] = (gated_ref[...] * scale * wide_ref[1:2]).astype(bf16)
    ext_ref[0:8] = ext_ref[CH : CH + 8]


def backward_kernel(layer, *refs):
    params, refs = refs[:7], refs[7:]
    upstream_ref, stream_ref, w_in_ref, w_out_ref, proj_ref, scan_ref, saved_ref, act_ref, slope_ref, *refs = refs
    top = layer == LAYERS - 1
    if top:
        mixed_ref, length_ref, result_ref, *refs = refs
    out_ref, down_ref, sum_ref, *refs = refs
    tables, refs = refs[:4], refs[4:]
    conv_ref, head_ref, wide_ref, spread_ref = tables
    gather_ref, grad_ref, raw_ref, state_ref, gate_ref, dconv_ref, *refs = refs
    keep_ref, grown_ref, terms_ref, row_ref = refs
    chunk = pl.num_programs(1) - 1 - pl.program_id(1)

    @pl.when(pl.program_id(1) == 0)
    def _():
        state_ref[...] = jnp.zeros_like(state_ref)
        dconv_ref[CH : CH + 8] = jnp.zeros_like(dconv_ref[CH : CH + 8])

    @pl.when((pl.program_id(0) == 0) & (pl.program_id(1) == 0))
    def _():
        raw_ref[...] = jnp.zeros_like(raw_ref)
        row_ref[...] = jnp.zeros_like(row_ref)
        sum_ref[...] = jnp.zeros_like(sum_ref)
        prepare(layer, params, tables, gather_ref)

    if top:
        slot = lax.broadcasted_iota(jnp.int32, (CH, D), 0) + chunk * CH
        result = stream_ref[...] + mm(mixed_ref[...], w_out_ref[...])
        result_ref[...] = jnp.where(slot < length_ref[0:1, 0:1], result, 0.0).astype(bf16)
    upstream = upstream_ref[...].astype(f32)
    grad_ref[...] = mm_t(upstream.astype(bf16), w_out_ref[...]).astype(bf16)
    shifted, step, cum, cum_t, grow, remain, rows, cols = step_parts(proj_ref, raw_ref, head_ref)
    step_w, grow_w, remain_w = [widen(spread_ref[...], v)[0] for v in (step, grow, remain)]

    square = jnp.zeros((CH, LANE), f32)
    along = jnp.zeros((CH, LANE), f32)
    for j in range(PAIRS):
        xs = act_ref[:, lanes(j)]
        gate = proj_ref[:, lanes(j)]
        open_share = sigmoid(gate)
        gate_ref[:, lanes(j)] = open_share
        gated = (scan_ref[:, lanes(j)] + wide_ref[0:1, lanes(j)] * xs) * (gate * open_share)
        square = square + gated * gated
        along = along + gated * (grad_ref[:, lanes(j)].astype(f32) * wide_ref[1:2, lanes(j)])
    scale = lax.rsqrt(jnp.sum(square, axis=1, keepdims=True) * (1.0 / DI) + epsilon)
    pull = scale * scale * scale * (jnp.sum(along, axis=1, keepdims=True) * (1.0 / DI))

    b_low = act_ref[:, lanes(PAIRS)].astype(bf16)
    c_low = act_ref[:, lanes(PAIRS + 1)].astype(bf16)
    affinity_t = jnp.where(rows <= cols, mm_t(b_low, c_low), 0.0)
    state = state_ref[...]
    state_low = state.astype(bf16)
    row_ref[1:2] = jnp.sum(saved_ref[...].astype(f32) * state, axis=0, keepdims=True)
    back = remain_w * mm(b_low, state_low)
    affinity_grad = jnp.zeros((CH, CH), f32)
    for j in range(PAIRS):
        xs = act_ref[:, lanes(j)]
        skip = wide_ref[0:1, lanes(j)]
        grad = grad_ref[:, lanes(j)].astype(f32)
        gate = proj_ref[:, lanes(j)]
        open_share = gate_ref[:, lanes(j)]
        opened = gate * open_share
        scanned = scan_ref[:, lanes(j)]
        outer = scanned + skip * xs
        gated = outer * opened
        gated_grad = scale * (grad * wide_ref[1:2, lanes(j)]) - pull * gated
        sum_ref[6:7, lanes(j)] += jnp.sum(grad * (gated * scale), axis=0, keepdims=True)
        dy = gated_grad * opened
        out_ref[:, lanes(j)] = (gated_grad * outer * (open_share + opened * (1.0 - open_share))).astype(bf16)
        sum_ref[5:6, lanes(j)] += jnp.sum(dy * xs, axis=0, keepdims=True)
        dy_low = dy.astype(bf16)
        grown_ref[:, lanes(j)] = (grow_w[:, lanes(j)] * dy).astype(bf16)
        scaled = xs * step_w[:, lanes(j)]
        x_low = scaled.astype(bf16)
        keep_ref[:, lanes(j)] = (scaled * remain_w[:, lanes(j)]).astype(bf16)
        dy_split = split_pair(dy_low)
        kernels = []
        for h in (2 * j, 2 * j + 1):
            differ = jnp.minimum(cum_t[h : h + 1] - cum[:, h : h + 1], 0.0)
            kernels.append(jnp.exp2(differ))
        mixing_t = jnp.concatenate([(k * affinity_t).astype(bf16) for k in kernels], axis=1)
        arrived = back[:, lanes(j)]
        x_grad = mm(mixing_t, dy_split) + arrived
        mixing_grad = mm_t(x_low, dy_split)
        affinity_grad = affinity_grad + mixing_grad[:, :CH] * kernels[0] + mixing_grad[:, CH:] * kernels[1]
        x_back = x_low.astype(f32)
        row_ref[0:1, lanes(j)] = jnp.sum(x_back * arrived, axis=0, keepdims=True)
        high, low = high_low(dy_low.astype(f32) * scanned - x_back * x_grad)
        terms_ref[0:CH, lanes(j)] = high
        terms_ref[CH : 2 * CH, lanes(j)] = low
        terms_ref[2 * CH :, lanes(j)] = (x_grad * xs).astype(bf16)
        dconv_ref[0:CH, lanes(j)] = (step_w[:, lanes(j)] * x_grad + skip * dy) * slope_ref[:, lanes(j)]
    affinity_low = jnp.where(rows <= cols, affinity_grad, 0.0).astype(bf16)
    grown = grown_ref[...]
    b_grad = mm(affinity_low, c_low) + mm_t(keep_ref[...], state_low)
    c_grad = t_mm(affinity_low, b_low) + mm_t(grown, saved_ref[...])
    dconv_ref[0:CH, lanes(PAIRS)] = b_grad * slope_ref[:, lanes(PAIRS)]
    dconv_ref[0:CH, lanes(PAIRS + 1)] = c_grad * slope_ref[:, lanes(PAIRS + 1)]

    gather = gather_ref[...]
    row_sums = mm(jnp.concatenate(high_low(row_ref[...]), axis=0), gather)
    row_sums = row_sums[:8] + row_sums[8:]
    last_grad = row_sums[0:1] + grow[CH - 1 : CH] * row_sums[1:2]
    cum_grad = mm(terms_ref[0:CH], gather) + mm(terms_ref[CH : 2 * CH], gather)
    decay_grad = jnp.dot((cols >= rows).astype(f32), cum_grad, precision=lax.Precision.HIGHEST, preferred_element_type=f32) + last_grad
    step_grad = mm(terms_ref[2 * CH :], gather) + head_ref[2:3] * decay_grad
    raw_grad = step_grad * sigmoid(shifted)
    out_ref[:, DI + CONV_CH :] = raw_grad[:, :NH].astype(bf16)
    sum_ref[7:8, 0:LANE] += jnp.sum(raw_grad, axis=0, keepdims=True)
    sum_ref[7:8, LANE : 2 * LANE] += jnp.sum(decay_grad * step, axis=0, keepdims=True)
    state_ref[...] = grow_w[CH - 1 : CH] * state + t_mm(c_low, grown)

    for j in range(PAIRS + 2):
        taps = [dconv_ref[3 - k : 3 - k + CH, lanes(j)] for k in range(KW)]
        total = conv_ref[0:1, lanes(j)] * taps[0]
        for k in range(1, KW):
            total = total + conv_ref[k : k + 1, lanes(j)] * taps[k]
        out_ref[:, lanes(j, DI)] = total.astype(bf16)
        value = proj_ref[:, lanes(j, DI)]
        for k in range(KW):
            sum_ref[k : k + 1, lanes(j)] += jnp.sum(taps[k] * value, axis=0, keepdims=True)
        sum_ref[4:5, lanes(j)] += jnp.sum(taps[3], axis=0, keepdims=True)
    dconv_ref[CH : CH + 8] = dconv_ref[0:8]

    edge = DI + CONV_CH
    normed_grad = mm_t(out_ref[:, :edge], w_in_ref[:, :edge]) + mm_t(out_ref[:, edge:], w_in_ref[:, edge:])
    stream = stream_ref[...].astype(f32)
    scale = norm_scale(stream)
    sum_ref[7:8, 2 * LANE : 2 * LANE + D] += jnp.sum(normed_grad * (stream * scale), axis=0, keepdims=True)
    inner = normed_grad * params[0][layer : layer + 1]
    pull = scale * scale * scale * jnp.mean(inner * stream, axis=-1, keepdims=True)
    down_ref[...] = upstream_ref[...].astype(f32) + scale * inner - pull * stream


def ring_place(n):
    wide = n // 4
    me = lax.axis_index("shard")
    chip, core = me // 2, me % 2
    row, col = chip // wide, chip % wide
    place = row * (2 * wide - 1 - col) + (1 - row) * col

    def shard_of(at, c):
        at = at % (2 * wide)
        r = at // wide
        x = r * (2 * wide - 1 - at) + (1 - r) * at
        return (r * wide + x) * 2 + c

    return place, core, shard_of


def halves(rows):
    first = rows // 2 // 16 * 16
    return (0, first), (first, rows - first)


def aligned(start, size, unit=16):
    return pl.ds(pl.multiple_of(start, unit), size)


def column_groups(width, replicas, parts):
    unit = LANE * replicas
    units = -(-width // unit)
    parts = min(parts, units)
    groups, start = [], 0
    for g in range(parts):
        size = (units // parts + (g < units % parts)) * unit
        groups.append((start, size, min(size, width - start)))
        start += size
    return groups, start


def remote(src, dst, send, recv, axis, to):
    return pltpu.make_async_remote_copy(
        src_ref=src, dst_ref=dst, send_sem=send, recv_sem=recv, device_id={axis: to}, device_id_type=MESH
    )


def greet(near, across):
    barrier = pltpu.get_barrier_semaphore()
    for to in near:
        pl.semaphore_signal(barrier, inc=1, device_id={"shard": to}, device_id_type=MESH)
    for to in across:
        pl.semaphore_signal(barrier, inc=1, device_id={"replica": to}, device_id_type=MESH)


def meet(count):
    pl.semaphore_wait(pltpu.get_barrier_semaphore(), count)


def bits(count):
    levels = count.bit_length() - 1
    assert 1 << levels == count
    return levels


class Gather:
    def __init__(self, n, arrays, items):
        self.n, self.half = n, n // 4
        self.arrays, self.items = arrays, items
        self.rows = [arrays[i[0]].shape[1] for i in items]

    def in_specs(self):
        return [pl.BlockSpec(memory_space=pl.ANY)] * len(self.arrays)

    out_specs = in_specs

    def out_shapes(self):
        return [jax.ShapeDtypeStruct((a.shape[1] * self.n, a.shape[2]), a.dtype) for a in self.arrays]

    def scratch(self):
        count = len(self.items)
        dma = pltpu.SemaphoreType.DMA
        own = [pltpu.VMEM((rows, i[3]), self.arrays[i[0]].dtype) for rows, i in zip(self.rows, self.items)]
        return [dma((count, self.half, 2, 2)), dma((count, self.half + 1, 2, 2)), dma((count, 2))] + own

    def tracks(self, parts, wholes, scratch):
        ring_sem, pair_sem, own_sem, *own_refs = scratch
        n, half = self.n, self.half
        place, core, shard_of = ring_place(n)
        right, left, pair = shard_of(place + 1, core), shard_of(place + n // 2 - 1, core), shard_of(place, 1 - core)
        me = shard_of(place, core)
        ways = ((0, right), (1, left))

        def rows_of(i, s, d):
            return (0, self.rows[i]) if s < half else halves(self.rows[i])[d]

        def part_at(i, part):
            a, layer, first, wide = self.items[i]
            return parts[a].at[layer, part[0] : part[0] + part[1], first : first + wide]

        def whole_at(i, owner, part):
            a, _, first, wide = self.items[i]
            return wholes[a].at[aligned(owner * self.rows[i] + part[0], part[1]), first : first + wide]

        def hop(i, s, d, to):
            owner = shard_of(place + (n // 2 - (s - 1) if d == 0 else s - 1), core)
            part = rows_of(i, s, d)
            src = part_at(i, part) if s == 1 else whole_at(i, owner, part)
            return remote(src, whole_at(i, owner, part), ring_sem.at[i, s - 1, d, 0], ring_sem.at[i, s - 1, d, 1], "shard", to)

        def cross(i, s, d):
            owner = me if s == 0 else shard_of(place + (n // 2 - s if d == 0 else s), core)
            part = (0, self.rows[i]) if s == 0 else rows_of(i, s, d)
            src = part_at(i, part) if s == 0 else whole_at(i, owner, part)
            return remote(src, whole_at(i, owner, part), pair_sem.at[i, s, d, 0], pair_sem.at[i, s, d, 1], "shard", pair)

        def own_in(i):
            return pltpu.make_async_copy(part_at(i, (0, self.rows[i])), own_refs[i], own_sem.at[i, 0])

        def own_out(i):
            return pltpu.make_async_copy(own_refs[i], whole_at(i, me, (0, self.rows[i])), own_sem.at[i, 1])

        crossings = [(0, 0)] + [(s, d) for s in range(1, half + 1) for d in (0, 1)]

        def start(i):
            for d, to in ways:
                hop(i, 1, d, to).start()
            cross(i, 0, 0).start()
            own_in(i).start()

        def forward(i, s):
            if s == 1:
                own_in(i).wait()
                own_out(i).start()
            for d, to in ways:
                hop(i, s, d, to).wait_recv()
                if s < half:
                    hop(i, s + 1, d, to).start()
                cross(i, s, d).start()

        def last(i):
            for s, d in crossings:
                cross(i, s, d).wait_recv()
            for s, d in crossings:
                cross(i, s, d).wait_send()
            for s in range(1, half + 1):
                for d, to in ways:
                    hop(i, s, d, to).wait_send()
            own_out(i).wait()

        hello = [lambda: greet((right, left, pair), ()), lambda: meet(3)]
        return hello, [
            [lambda i=i: start(i)]
            + [lambda i=i, s=s: forward(i, s) for s in range(1, half + 1)]
            + [lambda i=i: last(i)]
            for i in range(len(self.items))
        ]


class Reduce:
    def __init__(self, n, replicas, shapes, groups, modes=None):
        self.n, self.replicas = n, replicas
        self.chips, self.half, self.levels = n // 2, n // 4, bits(replicas)
        self.shapes = [(r // n, w) for r, w in shapes]
        self.groups = [column_groups(w, replicas, count) for (_, w), count in zip(self.shapes, groups)]
        self.modes = modes or ["full"] * len(shapes)
        self.work = [(a, g) for a in range(len(shapes)) for g in range(len(self.groups[a][0]))]

    def in_specs(self):
        return [pl.BlockSpec(memory_space=pl.ANY)] * len(self.shapes)

    out_specs = in_specs

    def out_shapes(self):
        return [
            jax.ShapeDtypeStruct((rows, padded), bf16) if mode == "head" else jax.ShapeDtypeStruct((rows, width), f32)
            for (rows, width), (_, padded), mode in zip(self.shapes, self.groups, self.modes)
        ]

    each = 12

    def scratch(self):
        dma = pltpu.SemaphoreType.DMA
        items = []
        for (rows, width), (groups, padded), mode in zip(self.shapes, self.groups, self.modes):
            g = len(groups)
            plane = (rows, width) if mode != "tail" else (16, LANE)
            far = (rows, padded) if mode != "head" else (16, LANE)
            items += [
                pltpu.VMEM((self.chips,) + plane, bf16),
                pltpu.VMEM((self.chips,) + plane, bf16),
                pltpu.VMEM((self.half, 2) + plane, bf16),
                pltpu.VMEM((self.half, 2) + plane, bf16),
                pltpu.VMEM((rows, padded), bf16),
                pltpu.VMEM((self.levels,) + far, bf16),
                pltpu.VMEM(far, bf16),
                pltpu.VMEM((rows, width) if mode != "head" else (16, LANE), f32),
                dma((g, self.chips, 3)), dma((g, self.half, 2, 2)), dma((g, 2 * self.levels, 2)), dma((g,)),
            ]
        return items

    def tracks(self, ins, outs, scratch, feed=None):
        n, replicas, chips, half, levels = self.n, self.replicas, self.chips, self.half, self.levels
        place, core, shard_of = ring_place(n)
        right, left, pair = shard_of(place + 1, core), shard_of(place + chips - 1, core), shard_of(place, 1 - core)
        mine = lax.axis_index("replica")
        ways = ((0, right), (1, left))
        order = [half] + [v for s in range(half - 1, 0, -1) for v in (s, chips - s)] + [0]
        buffers = [scratch[self.each * a : self.each * (a + 1)] for a in range(len(self.shapes))]

        def partner(j):
            bit = mine // (1 << j) % 2
            return mine + (1 - 2 * bit) * (1 << j), bit

        def cols_of(a, g):
            start, _, wide = self.groups[a][0][g]
            return slice(start, start + wide)

        def piece(a, g, owner):
            rows = self.shapes[a][0]
            return ins[a].at[aligned(owner * rows, rows), cols_of(a, g)]

        def pairing(a, g, q):
            sem = buffers[a][8]
            return remote(piece(a, g, shard_of(place + q, 1 - core)), buffers[a][1].at[q, :, cols_of(a, g)], sem.at[g, q, 0], sem.at[g, q, 1], "shard", pair)

        def loading(a, g, q):
            return pltpu.make_async_copy(
                piece(a, g, shard_of(place + q, core)), buffers[a][0].at[q, :, cols_of(a, g)], buffers[a][8].at[g, q, 2]
            )

        def part_of(a, k, d):
            rows = self.shapes[a][0]
            return halves(rows)[d] if k == 1 else (0, rows)

        def ringing(a, g, k, d, to):
            first, count = part_of(a, k, d)
            sem = buffers[a][9]
            return remote(
                buffers[a][2].at[k - 1, d, first : first + count, cols_of(a, g)],
                buffers[a][3].at[k - 1, d, first : first + count, cols_of(a, g)],
                sem.at[g, k - 1, d, 0], sem.at[g, k - 1, d, 1], "shard", to,
            )

        def region(a, g, j, keep):
            start, size, _ = self.groups[a][0][g]
            at = start
            for i in range(j + 1):
                bit = mine // (1 << i) % 2
                at = at + (bit if keep or i < j else 1 - bit) * (size >> (i + 1))
            return aligned(at, size >> (j + 1), LANE)

        def halving(a, g, j):
            cols = region(a, g, j, False)
            sem = buffers[a][10]
            return remote(
                buffers[a][4].at[:, cols], buffers[a][5].at[j, :, cols], sem.at[g, j, 0], sem.at[g, j, 1], "replica", partner(j)[0]
            )

        def doubling(a, g, j):
            cols = region(a, g, j, True)
            sem = buffers[a][10]
            return remote(
                buffers[a][6].at[:, cols], buffers[a][6].at[:, cols],
                sem.at[g, levels + j, 0], sem.at[g, levels + j, 1], "replica", partner(j)[0],
            )

        def storing(a, g):
            cols = cols_of(a, g)
            return pltpu.make_async_copy(buffers[a][7].at[:, cols], outs[a].at[:, cols], buffers[a][11].at[g])

        def both(a, g, q, part):
            first, count = part
            rows, cols = slice(first, first + count), cols_of(a, g)
            return buffers[a][0][q, rows, cols].astype(f32) + buffers[a][1][q, rows, cols].astype(f32)

        def arrived(a, g, q):
            if not (feed and a == 0):
                loading(a, g, q).wait()
            pairing(a, g, q).wait_recv()

        def begin(a, g):
            fed = feed and a == 0
            if fed:
                feed(g, cols_of(a, g))
            for q in order:
                pairing(a, g, q).start()
                if fed:
                    buffers[a][0][q, :, cols_of(a, g)] = piece(a, g, shard_of(place + q, core))[...]
                else:
                    loading(a, g, q).start()

        def turn(a, g, k):
            cols = cols_of(a, g)
            for d, to in ways:
                q = half - k + 1 if d == 0 else chips - (half - k + 1)
                if k > 1 or d == 0:
                    arrived(a, g, q)
                if k > 1:
                    ringing(a, g, k - 1, d, to).wait_recv()
                pieces = [part_of(a, 1, d)] if k == 1 else halves(self.shapes[a][0]) if k == 2 else [part_of(a, k, d)]
                for e, (at, many) in enumerate(pieces):
                    value = both(a, g, q, (at, many))
                    if k > 2 or (k == 2 and e == d):
                        value = value + buffers[a][3][k - 2, d, at : at + many, cols].astype(f32)
                    buffers[a][2][k - 1, d, at : at + many, cols] = value.astype(bf16)
                ringing(a, g, k, d, to).start()

        def settle(a, g):
            cols = cols_of(a, g)
            start, size, wide = self.groups[a][0][g]
            rows = self.shapes[a][0]
            arrived(a, g, 0)
            value = both(a, g, 0, (0, rows))
            for d, to in ways:
                ringing(a, g, half, d, to).wait_recv()
                value = value + buffers[a][3][half - 1, d, :, cols].astype(f32)
            buffers[a][4][:, cols] = value.astype(bf16)
            if wide < size:
                buffers[a][4][:, start + wide : start + size] = jnp.zeros((rows, size - wide), bf16)
            if self.modes[a] == "head":
                handing(a, g).start()
            else:
                halving(a, g, 0).start()

        def handing(a, g):
            start, size, _ = self.groups[a][0][g]
            cols = slice(start, start + size)
            here, there = buffers[a][4].at[:, cols], (outs if self.modes[a] == "head" else ins)[a].at[:, cols]
            if self.modes[a] == "tail":
                here, there = there, here
            return pltpu.make_async_copy(here, there, buffers[a][11].at[g])

        def resume(a, g):
            handing(a, g).wait()
            halving(a, g, 0).start()

        def halve(a, g, j):
            halving(a, g, j).wait_recv()
            cols = region(a, g, j, True)
            value = (buffers[a][4][:, cols].astype(f32) + buffers[a][5][j, :, cols].astype(f32)).astype(bf16)
            if j + 1 < levels:
                buffers[a][4][:, cols] = value
                halving(a, g, j + 1).start()
            else:
                buffers[a][6][:, cols] = value
                doubling(a, g, j).start()

        def double(a, g, j):
            doubling(a, g, j).wait_recv()
            if j > 0:
                doubling(a, g, j - 1).start()

        def last(a, g):
            double(a, g, 0)
            cols = cols_of(a, g)
            buffers[a][7][:, cols] = buffers[a][6][:, cols].astype(f32)
            storing(a, g).start()
            if self.modes[a] != "tail":
                leave(a, g)
            for j in range(levels):
                halving(a, g, j).wait_send()
                doubling(a, g, j).wait_send()
            storing(a, g).wait()

        def leave(a, g):
            for q in order:
                pairing(a, g, q).wait_send()
            for k in range(1, half + 1):
                for d, to in ways:
                    ringing(a, g, k, d, to).wait_send()

        def part(a, g):
            leave(a, g)
            handing(a, g).wait()

        across = [partner(j)[0] for j in range(levels)]
        hello = [lambda: greet((right, left, pair), across), lambda: meet(3 + levels)]
        def track(a, g):
            planes = (
                [lambda: begin(a, g)]
                + [lambda k=k: turn(a, g, k) for k in range(1, half + 1)]
                + [lambda: settle(a, g)]
            )
            rest = (
                [lambda j=j: halve(a, g, j) for j in range(levels)]
                + [lambda j=j: double(a, g, j) for j in range(levels - 1, 0, -1)]
                + [lambda: last(a, g)]
            )
            if self.modes[a] == "head":
                return planes + [lambda: part(a, g)]
            if self.modes[a] == "tail":
                return [lambda: handing(a, g).start(), lambda: resume(a, g)] + rest
            return planes + rest

        return hello, [track(a, g) for a, g in self.work]


def beside(body, counts, engine, times, hooks):
    ins, outs, scratch = counts

    def kernel(*refs):
        i = len(engine.in_specs())
        o = len(engine.out_specs())
        own_in, refs = refs[:ins], refs[ins:]
        far_in, refs = refs[:i], refs[i:]
        own_out, refs = refs[:outs], refs[outs:]
        far_out, refs = refs[:o], refs[o:]
        own_scratch, far_scratch = refs[:scratch], refs[scratch:]
        hello, tracks = engine.tracks(far_in, far_out, far_scratch)
        plan = {}
        plan[0] = [hello[0]]
        plan.setdefault(min(t[0] for t in times), []).append(hello[1])
        for t, track in enumerate(tracks):
            wanted = times[t]
            if len(wanted) != len(track):
                first = wanted[0]
                wanted = [first + (hooks - first) * i // (len(track) - 1) for i in range(len(track))]
            for at, stage in zip(wanted, track):
                plan.setdefault(min(at, hooks), []).append(stage)
        step = pl.program_id(0) * pl.num_programs(1) + pl.program_id(1)

        def run(at):
            for stage in plan[at]:
                stage()

        pl.when(step == 0)(lambda: run(0))
        body(*own_in, *own_out, *own_scratch)
        for at in sorted(plan):
            if at > 0:
                pl.when(step == at - 1)(lambda at=at: run(at))

    return kernel


def move(engine, operands, collective_id, name):
    def kernel(*refs):
        i, o = len(engine.in_specs()), len(engine.out_specs())
        hello, tracks = engine.tracks(refs[:i], refs[i : i + o], refs[i + o :])
        for stage in hello:
            stage()
        for at in range(max(map(len, tracks))):
            for track in tracks:
                if at < len(track):
                    track[at]()

    return pl.pallas_call(
        kernel,
        out_shape=engine.out_shapes(),
        in_specs=engine.in_specs(),
        out_specs=engine.out_specs(),
        scratch_shapes=engine.scratch(),
        compiler_params=pltpu.CompilerParams(collective_id=collective_id, has_side_effects=True),
        name=name,
    )(*operands)


def finish_kernel(engine, n, replicas, *refs):
    left_ref, right_hbm, first_ref, second_ref, in_ref, out0_ref, out1_ref = refs[:7]
    in_total_ref, out_total_ref, total_ref = refs[7:10]
    product_ref, right_ref, mine_ref, plane_ref, across_ref, whole_ref, in_buf, out_buf = refs[10:18]
    plane_sem, across_sem, share_sem, copy_sem, right_sem, *scratch = refs[18:]
    me, mine = lax.axis_index("shard"), lax.axis_index("replica")
    width = mine_ref.shape[2]

    def operand(g):
        start, _, wide = engine.groups[0][0][g]
        cols = slice(start, start + wide)
        return pltpu.make_async_copy(right_hbm.at[:, cols], right_ref.at[:, cols], right_sem.at[g])

    for g in range(len(engine.groups[0][0])):
        operand(g).start()

    ready = set()

    def feed(g, cols):
        if g in ready:
            return
        ready.add(g)
        operand(g).wait()
        product_ref[:, cols] = mm(left_ref[...], right_ref[:, cols]).astype(bf16)

    _, tracks = engine.tracks((product_ref, out0_ref), (in_total_ref.at[0], out_total_ref.at[0]), scratch, feed)
    greet([(me + s) % n for s in range(1, n)], [(mine + s) % replicas for s in range(1, replicas)])
    moves = [(in_ref, in_buf, in_total_ref.at[1]), (out1_ref, out_buf, out_total_ref.at[1])]
    fetches = [pltpu.make_async_copy(src, via, copy_sem.at[0, i]) for i, (src, via, _) in enumerate(moves)]
    stores = [pltpu.make_async_copy(via, dst, copy_sem.at[1, i]) for i, (_, via, dst) in enumerate(moves)]
    for fetch in fetches:
        fetch.start()
    spots = [(k // (n // 2), k % (n // 2) * width) for k in range(n)]
    for k, (half, at) in enumerate(spots):
        mine_ref[k] = (second_ref if half else first_ref)[:, at : at + width]

    def plane(s):
        to = (me + s) % n
        return remote(mine_ref.at[to], plane_ref.at[s], plane_sem.at[0, s], plane_sem.at[1, s], "shard", to)

    def across(s):
        return remote(across_ref.at[0], across_ref.at[s], across_sem.at[0, s], across_sem.at[1, s], "replica", (mine + s) % replicas)

    def share(s):
        return remote(whole_ref.at[me], whole_ref.at[me], share_sem.at[0, s], share_sem.at[1, s], "shard", (me + s) % n)

    def sharing(s):
        owner = (me + n - s) % n
        return remote(whole_ref.at[owner], whole_ref.at[owner], share_sem.at[0, s], share_sem.at[1, s], "shard", (me + s) % n)

    def send_small():
        for s in range(1, n):
            plane(s).start()

    def sum_plane():
        value = mine_ref[me]
        for s in range(1, n):
            plane(s).wait_recv()
            value = value + plane_ref[s]
        across_ref[0] = value
        for s in range(1, replicas):
            across(s).start()

    def sum_across():
        for s in range(1, replicas):
            across(s).wait_recv()
        zero = jnp.zeros((8, width), f32)
        whole_ref[me] = lax.fori_loop(0, replicas, lambda i, acc: acc + across_ref[(mine - i + replicas) % replicas], zero)
        for s in range(1, n):
            share(s).start()

    def give_small():
        for s in range(1, n):
            sharing(s).wait_recv()
        for k, (half, at) in enumerate(spots):
            total_ref[8 * half : 8 * half + 8, at : at + width] = whole_ref[k]

    plan = {}
    for (a, g), track in zip(engine.work, tracks):
        for i, stage in enumerate(track):
            plan.setdefault(((g if a == 0 else 0) + (2 * i - 1 if i else 0), i), []).append(stage)
    feed(0, slice(0, engine.groups[0][0][0][2]))
    meet(n + replicas - 2)
    slots = sorted(plan)
    for k, slot in enumerate(slots):
        for stage in plan[slot]:
            stage()
        if k == 0:
            send_small()
        if k == len(slots) // 4:
            sum_plane()
            for fetch, store in zip(fetches, stores):
                fetch.wait()
                store.start()
        if k == len(slots) // 2:
            sum_across()
    give_small()
    for s in range(1, n):
        plane(s).wait_send()
        share(s).wait_send()
    for s in range(1, replicas):
        across(s).wait_send()
    for store in stores:
        store.wait()


def finish(left, right, sums, in_grad, out_grads, n, replicas, collective_id):
    rows, width = left.shape[0] // n, right.shape[1]
    out_rows, out_width = out_grads[1].shape
    engine = Reduce(n, replicas, [(left.shape[0], width), (out_rows * n, out_width)], [7, 1], ["full", "tail"])
    anywhere, vmem = pl.BlockSpec(memory_space=pl.ANY), pl.BlockSpec(memory_space=pltpu.VMEM)
    dma = pltpu.SemaphoreType.DMA
    small = (8, 2 * SUMS // n)
    return pl.pallas_call(
        lambda *refs: finish_kernel(engine, n, replicas, *refs),
        out_shape=[
            jax.ShapeDtypeStruct((LAYERS, rows, width), f32),
            jax.ShapeDtypeStruct((LAYERS, out_rows, out_width), f32),
            jax.ShapeDtypeStruct((LAYERS * 8, SUMS), f32),
        ],
        in_specs=[vmem, anywhere, vmem, vmem] + [anywhere] * 3,
        out_specs=[anywhere, anywhere, vmem],
        scratch_shapes=[
            pltpu.VMEM((n * rows, width), bf16),
            pltpu.VMEM(right.shape, bf16),
            pltpu.VMEM((n,) + small, f32),
            pltpu.VMEM((n,) + small, f32),
            pltpu.VMEM((replicas,) + small, f32),
            pltpu.VMEM((n,) + small, f32),
            pltpu.VMEM((rows, width), f32),
            pltpu.VMEM((out_rows, out_width), f32),
            dma((2, n)), dma((2, replicas)), dma((2, n)), dma((2, 2)), dma((len(engine.groups[0][0]),)),
        ] + engine.scratch(),
        compiler_params=pltpu.CompilerParams(collective_id=collective_id, has_side_effects=True, vmem_limit_bytes=60 * 2**20),
        name="finish",
    )(left, right, *sums, in_grad, *out_grads)


def small_kernel(total_ref, a_log_ref, gain_ref, conv_w_ref, conv_b_ref, dt_bias_ref, a_log_grad_ref, d_skip_ref, out_gain_ref):
    column = lax.broadcasted_iota(jnp.int32, (DI, LANE), 1)
    owner = lax.broadcasted_iota(jnp.int32, (DI, LANE), 0) // HEAD
    gather = (column == owner).astype(f32).astype(bf16)
    for l in range(LAYERS):
        here, row = slice(l, l + 1), 8 * l
        gain_ref[here] = total_ref[row + 7 : row + 8, 2 * LANE : 2 * LANE + D]
        conv_w_ref[l] = total_ref[row : row + KW, :CONV_CH]
        conv_b_ref[here] = total_ref[row + 4 : row + 5, :CONV_CH]
        dt_bias_ref[here] = total_ref[row + 7 : row + 8, 0:NH]
        a_log_grad_ref[here] = -jnp.exp(a_log_ref[here]) * total_ref[row + 7 : row + 8, LANE : LANE + NH]
        out_gain_ref[here] = total_ref[row + 6 : row + 7, :DI]
        value = total_ref[row : row + 8, :DI]
        high = value.astype(bf16)
        middle = (value - high.astype(f32)).astype(bf16)
        low = (value - high.astype(f32) - middle.astype(f32)).astype(bf16)
        summed = mm(high, gather) + mm(middle, gather) + mm(low, gather)
        d_skip_ref[here] = summed[5:6, 0:NH]


def small_results(total, params):
    return pl.pallas_call(
        small_kernel,
        out_shape=[jax.ShapeDtypeStruct(p.shape, f32) for p in params],
        name="small_results",
    )(total, params[4])


def product_kernel(left_ref, right_ref, out_ref):
    out_ref[...] = mm(left_ref[...], right_ref[...]).astype(bf16)


def product(left, right, wide):
    (rows, depth), width = left.shape, right.shape[1]
    return pl.pallas_call(
        product_kernel,
        grid=(pl.cdiv(width, wide),),
        in_specs=[pl.BlockSpec((rows, depth), lambda c: (0, 0)), pl.BlockSpec((depth, wide), lambda c: (0, c))],
        out_specs=pl.BlockSpec((rows, wide), lambda c: (0, c)),
        out_shape=jax.ShapeDtypeStruct((rows, width), bf16),
        compiler_params=pltpu.CompilerParams(vmem_limit_bytes=62 * 2**20),
        name="product",
    )(left, right)


def turned_kernel(left_ref, right_ref, out_ref):
    out_ref[...] = t_mm(left_ref[...], right_ref[...].astype(bf16)).astype(bf16)


def turned_product(left, right, tall):
    (depth, rows), width = left.shape, right.shape[1]
    return pl.pallas_call(
        turned_kernel,
        grid=(rows // tall,),
        in_specs=[pl.BlockSpec((depth, tall), lambda r: (0, r)), pl.BlockSpec((depth, width), lambda r: (0, 0))],
        out_specs=pl.BlockSpec((tall, width), lambda r: (r, 0)),
        out_shape=jax.ShapeDtypeStruct((rows, width), bf16),
        compiler_params=pltpu.CompilerParams(vmem_limit_bytes=62 * 2**20),
        name="turned_product",
    )(left, right)


def top_kernel(row_total, slots, left_ref, cotangent_ref, lengths_ref, dealing_ref, out_ref, upstream_ref, length_ref):
    @pl.when(pl.program_id(0) == 0)
    def _():
        mine = lax.axis_index("replica") * lax.axis_size("shard") + lax.axis_index("shard")
        place = lax.broadcasted_iota(jnp.int32, lengths_ref.shape, 1)
        dealing, lengths = dealing_ref[...].astype(f32), lengths_ref[...].astype(f32)
        slot = lax.broadcasted_iota(jnp.int32, (slots, D), 0)
        for m in range(MICRO):
            sequence = jnp.sum(jnp.where(place == m * row_total + mine, dealing, 0.0), axis=1, keepdims=True)
            length = jnp.sum(jnp.where(place.astype(f32) == sequence, lengths, 0.0), axis=1, keepdims=True).astype(jnp.int32)
            length_ref[8 * m : 8 * m + 8] = jnp.broadcast_to(length, (8, LANE))
            here = slice(m * slots, (m + 1) * slots)
            upstream_ref[here] = jnp.where(slot < length, cotangent_ref[here].astype(f32), 0.0).astype(bf16)

    out_ref[...] = t_mm(left_ref[...], upstream_ref[...]).astype(bf16)


def top_product(left, cotangent, lengths, dealing, row_total, tall):
    (depth, rows), width = left.shape, cotangent.shape[1]
    whole = lambda shape: pl.BlockSpec(shape, lambda r: (0, 0))
    sequences = lengths.shape[0]
    return pl.pallas_call(
        lambda *refs: top_kernel(row_total, depth // MICRO, *refs),
        grid=(rows // tall,),
        in_specs=[pl.BlockSpec((depth, tall), lambda r: (0, r)), whole((depth, width)), whole((1, sequences)), whole((1, sequences))],
        out_specs=[pl.BlockSpec((tall, width), lambda r: (r, 0)), whole((depth, width)), whole((8 * MICRO, LANE))],
        out_shape=[
            jax.ShapeDtypeStruct((rows, width), bf16),
            jax.ShapeDtypeStruct((depth, width), bf16),
            jax.ShapeDtypeStruct((8 * MICRO, LANE), jnp.int32),
        ],
        compiler_params=pltpu.CompilerParams(vmem_limit_bytes=62 * 2**20),
        name="top_product",
    )(left, cotangent, lengths.reshape(1, sequences), dealing.reshape(1, sequences))


def fixed(shape):
    return pl.BlockSpec(shape, lambda r, c: (0,) * len(shape))


def held(shape):
    return pl.BlockSpec(shape, lambda r, c: (0,) * len(shape), pipeline_mode=pl.Buffered(1))


def grid_call(body, grid, operands, in_specs, out_specs, out_shapes, scratch, name, extra):
    engine, given, times, collective_id = extra
    kernel = beside(body, (len(in_specs), len(out_specs), len(scratch)), engine, times, grid[0] * grid[1])
    return pl.pallas_call(
        kernel, grid=grid, in_specs=in_specs + engine.in_specs(), out_specs=out_specs + engine.out_specs(),
        out_shape=out_shapes + engine.out_shapes(), scratch_shapes=scratch + engine.scratch(),
        compiler_params=pltpu.CompilerParams(
            dimension_semantics=("arbitrary", "arbitrary"), vmem_limit_bytes=60 * 2**20,
            collective_id=collective_id, has_side_effects=True,
        ),
        name=name,
    )(*operands, *given)


def layer_forward(layer, tokens, w_in, before, w_out, params, chunks, extra):
    count = tokens.shape[0]
    block = lambda r, c: (r * chunks + c, 0)
    later = layer > 0
    rows = lambda width: pl.BlockSpec((CH, width), block)
    return grid_call(
        lambda *refs: forward_kernel(layer, *refs),
        (count // (chunks * CH), chunks),
        (*params, tokens, w_in) + ((before, w_out) if later else ()),
        [held(p.shape) for p in params] + [rows(D), held((D, NIN))] + ([rows(DI), held((DI, D))] if later else []),
        ([rows(D)] if later else [])
        + [pl.BlockSpec((D, CH), lambda r, c: (0, r * chunks + c)), rows(NIN), rows(DI), rows(DI), pl.BlockSpec((NSTATE, DI), block), rows(CONV_CH), rows(CONV_CH)],
        ([jax.ShapeDtypeStruct((count, D), f32)] if later else [])
        + [
            jax.ShapeDtypeStruct((D, count), bf16),
            jax.ShapeDtypeStruct((count, NIN), f32),
            jax.ShapeDtypeStruct((count, DI), bf16),
            jax.ShapeDtypeStruct((count, DI), f32),
            jax.ShapeDtypeStruct((count // CH * NSTATE, DI), bf16),
            jax.ShapeDtypeStruct((count, CONV_CH), f32),
            jax.ShapeDtypeStruct((count, CONV_CH), f32),
        ],
        table_scratch()
        + [
            pltpu.VMEM((CH + 8, CONV_CH), f32),
            pltpu.VMEM((CH, LANE), f32),
            pltpu.VMEM((NSTATE, DI), f32),
            pltpu.VMEM((CH, DI), f32),
            pltpu.VMEM((CH, DI), bf16),
        ],
        f"layer_forward_{layer}", extra,
    )


def layer_backward(layer, upstream, stream, w_in, w_out, projected, kept, mixed, length, params, chunks, extra):
    count = projected.shape[0]
    block = lambda r, c: (r * chunks + chunks - 1 - c, 0)
    rows = lambda width: pl.BlockSpec((CH, width), block)
    top = layer == LAYERS - 1
    return grid_call(
        lambda *refs: backward_kernel(layer, *refs),
        (count // (chunks * CH), chunks),
        (*params, upstream, stream, w_in, w_out, projected, *kept) + ((mixed, length) if top else ()),
        [held(p.shape) for p in params]
        + [rows(D), rows(D), held((D, NIN)), held((DI, D)), rows(NIN), rows(DI), pl.BlockSpec((NSTATE, DI), block), rows(CONV_CH), rows(CONV_CH)]
        + ([rows(DI), pl.BlockSpec((8, LANE), lambda r, c: (r, 0))] if top else []),
        ([rows(D)] if top else []) + [rows(NIN), rows(D), fixed((8, SUMS))],
        ([jax.ShapeDtypeStruct((count, D), bf16)] if top else [])
        + [
            jax.ShapeDtypeStruct((count, NIN), bf16),
            jax.ShapeDtypeStruct((count, D), f32),
            jax.ShapeDtypeStruct((8, SUMS), f32),
        ],
        table_scratch()
        + [
            pltpu.VMEM((DI, LANE), bf16),
            pltpu.VMEM((CH, DI), bf16),
            pltpu.VMEM((CH, LANE), f32),
            pltpu.VMEM((NSTATE, DI), f32),
            pltpu.VMEM((CH, DI), f32),
            pltpu.VMEM((CH + 8, CONV_CH), f32),
            pltpu.VMEM((CH, DI), bf16),
            pltpu.VMEM((CH, DI), bf16),
            pltpu.VMEM((3 * CH, DI), bf16),
            pltpu.VMEM((8, DI), f32),
        ],
        f"layer_backward_{layer}", extra,
    )


def shards(
    tokens, cotangent, lengths, dealing, in_gain, w_in, conv_w, conv_b, dt_bias, a_log, d_skip, out_gain, w_out,
):
    n, replicas = lax.axis_size("shard"), lax.axis_size("replica")
    slot_count = tokens.shape[2]
    chunks = slot_count // CH
    count = MICRO * slot_count
    params = (in_gain, conv_w, conv_b, dt_bias, a_log, d_skip, out_gain)
    flat = tokens.reshape(count, D)

    (first_in,) = move(Gather(n, [w_in], [(0, 0, 0, CUT), (0, 0, CUT, NIN - CUT)]), (w_in,), 1, "gather_first")
    engine = Gather(n, [w_out, w_in], [(0, 0, 0, D), (1, 1, 0, CUT), (1, 1, CUT, NIN - CUT)])
    normed0, projected0, mixed0, *kept0, first_out, second_in = layer_forward(
        0, flat, first_in, None, None, params, chunks, (engine, (w_out, w_in), GATHER_BOTH, 2)
    )
    engine = Gather(n, [w_out], [(0, 1, 0, D)])
    stream, normed1, projected1, mixed1, *kept1, second_out = layer_forward(
        1, flat, second_in, mixed0, first_out, params, chunks, (engine, (w_out,), GATHER_LAST, 3)
    )

    out_grad1, upstream, length = top_product(mixed1, cotangent.reshape(count, D), lengths, dealing, replicas * n, 512)
    engine = Reduce(n, replicas, [out_grad1.shape], [1])
    result, project_grad1, upstream1, sums1, out_total1 = layer_backward(
        1, upstream, stream, second_in, second_out, projected1, kept1, mixed1, length, params, chunks,
        (engine, (out_grad1,), REDUCE_OUT, 4),
    )
    in_grad1 = product(normed1, project_grad1, 512)
    out_grad0 = turned_product(mixed0, upstream1, 512)
    engine = Reduce(n, replicas, [in_grad1.shape, out_grad0.shape], [2, 1], ["full", "head"])
    project_grad0, upstream0, sums0, in_total1, out_total0 = layer_backward(
        0, upstream1, flat, first_in, first_out, projected0, kept0, None, None, params, chunks,
        (engine, (in_grad1, out_grad0), REDUCE_BOTH, 5),
    )
    in_total, out_total, small = finish(
        normed0, project_grad0, (sums0, sums1), in_total1, (out_total0, out_total1), n, replicas, 6
    )
    gain_grad, *small = small_results(small, params)
    shape = (MICRO, 1, slot_count, D)
    return (result.reshape(shape), upstream0.reshape(shape), gain_grad, in_total, *small, out_total)


def solution(mesh):
    rows = P(None, ("replica", "shard"), None, None)
    split = P(None, "shard", None)
    in_specs = (rows, rows, P(), P(), P(), split, P(), P(), P(), P(), P(), P(), split)
    out_specs = (rows, rows, P(), split, P(), P(), P(), P(), P(), P(), split)
    return jax.shard_map(shards, mesh=mesh, in_specs=in_specs, out_specs=out_specs, check_vma=False)
```

```python
import jax
import jax.numpy as jnp
from jax import lax
from jax.experimental import pallas as pl
from jax.experimental.pallas import tpu as pltpu
from jax.sharding import PartitionSpec as P

D = 768
DI = 1536
NH = 24
HEAD = 64
NSTATE = 128
KW = 4
CONV_CH = 1792
NIN = 3352
LAYERS = 2
MICRO = 2
CH = 128
PAIRS = NH // 2
LANE = 128
DUP = 32
LOG2E = 1.4426950408889634
SUMS = 2048
CUT = 1664
GATHER_BOTH = ((0, 3, 7, 8), (0, 5, 8, 8), (0, 7, 8, 8))
GATHER_LAST = ((1, 4, 6, 8),)
REDUCE_OUT = ((1, 2, 3, 4, 5, 6, 7, 8),)
REDUCE_BOTH = ((0, 1, 2, 3, 4, 5, 6, 7), (0, 1, 2, 4, 5, 6, 7, 8), (0, 3, 5, 7, 8))

epsilon = 1e-05
f32 = jnp.float32
bf16 = jnp.bfloat16
MESH = pl.DeviceIdType.MESH


def mm(a, b):
    return jnp.dot(a, b, preferred_element_type=f32)


def mm_t(a, b):
    return lax.dot_general(a, b, (((1,), (1,)), ((), ())), preferred_element_type=f32)


def t_mm(a, b):
    return lax.dot_general(a, b, (((0,), (0,)), ((), ())), preferred_element_type=f32)


def sigmoid(v):
    return 0.5 * jnp.tanh(0.5 * v) + 0.5


def softplus(v):
    return jnp.maximum(v, 0.0) + jnp.log1p(jnp.exp(-jnp.abs(v)))


def lanes(j, base=0):
    return slice(base + LANE * j, base + LANE * (j + 1))


def norm_scale(stream):
    return lax.rsqrt(jnp.mean(stream * stream, axis=-1, keepdims=True) + epsilon)


def split_pair(v):
    left = lax.broadcasted_iota(jnp.int32, v.shape, 1) < HEAD
    zero = jnp.zeros_like(v)
    return jnp.concatenate([jnp.where(left, v, zero), jnp.where(left, zero, v)], axis=0)


def high_low(v):
    high = v.astype(bf16)
    return high, (v - high.astype(f32)).astype(bf16)


def widen(spread, *values):
    parts = []
    for v in values:
        high, low = high_low(v)
        first = lax.broadcasted_iota(jnp.int32, v.shape, 1) < DUP
        parts.append(jnp.where(first, high, low))
    rows = values[0].shape[0]
    wide = mm(jnp.concatenate(parts, axis=0), spread)
    return [wide[i * rows : (i + 1) * rows] for i in range(len(values))]


def exact_mm(mask, v):
    high, low = high_low(v)
    rest = (v - high.astype(f32) - low.astype(f32)).astype(bf16)
    out = mm(mask.astype(f32).astype(bf16), jnp.concatenate([high, low, rest], axis=1))
    return out[:, :LANE] + out[:, LANE : 2 * LANE] + out[:, 2 * LANE :]


def step_parts(proj_ref, raw_ref, head_ref):
    raw = proj_ref[:, DI + CONV_CH :]
    raw_ref[:, 0:NH] = raw
    raw_ref[:, DUP : DUP + NH] = raw
    shifted = raw_ref[...] + head_ref[0:1]
    step = softplus(shifted)
    rows = lax.broadcasted_iota(jnp.int32, (CH, CH), 0)
    cols = lax.broadcasted_iota(jnp.int32, (CH, CH), 1)
    cum = jnp.dot((cols <= rows).astype(f32), head_ref[1:2] * step, precision=lax.Precision.HIGHEST, preferred_element_type=f32)
    grow = jnp.exp2(cum)
    remain = jnp.exp2(cum[CH - 1 : CH] - cum)
    return shifted, step, cum, cum.T, grow, remain, rows, cols


def conv_block(ext_ref, conv_ref, j):
    total = conv_ref[4:5, lanes(j)]
    for k in range(KW):
        total = total + conv_ref[k : k + 1, lanes(j)] * ext_ref[5 + k : 5 + k + CH, lanes(j)]
    return total


def prepare(layer, params, tables, gather_ref=None):
    in_gain_ref, conv_w_ref, conv_b_ref, dt_bias_ref, a_log_ref, d_skip_ref, out_gain_ref = params
    conv_ref, head_ref, wide_ref, spread_ref = tables
    conv_ref[0:KW] = conv_w_ref[layer]
    conv_ref[KW : KW + 1] = conv_b_ref[layer : layer + 1]
    head_ref[...] = jnp.zeros_like(head_ref)
    rate = -jnp.exp(a_log_ref[layer : layer + 1])
    for row, value in enumerate((dt_bias_ref[layer : layer + 1], rate * LOG2E, rate, d_skip_ref[layer : layer + 1])):
        head_ref[row : row + 1, 0:NH] = value
        head_ref[row : row + 1, DUP : DUP + NH] = value
    column = lax.broadcasted_iota(jnp.int32, (LANE, DI), 0)
    owner = lax.broadcasted_iota(jnp.int32, (LANE, DI), 1) // HEAD
    spread_ref[...] = ((column % DUP == owner) & (column < 2 * DUP)).astype(f32).astype(bf16)
    wide_ref[...] = widen(spread_ref[...], head_ref[...])[0]
    wide_ref[0:1] = wide_ref[3:4]
    wide_ref[1:2] = out_gain_ref[layer : layer + 1]
    if gather_ref is not None:
        column = lax.broadcasted_iota(jnp.int32, (DI, LANE), 1)
        owner = lax.broadcasted_iota(jnp.int32, (DI, LANE), 0) // HEAD
        gather_ref[...] = ((column % DUP == owner) & (column < 2 * DUP)).astype(f32).astype(bf16)


def table_scratch():
    return [
        pltpu.VMEM((8, CONV_CH), f32), pltpu.VMEM((8, LANE), f32), pltpu.VMEM((8, DI), f32), pltpu.VMEM((LANE, DI), bf16),
    ]


def forward_kernel(layer, *refs):
    params, (tokens_ref, w_in_ref), refs = refs[:7], refs[7:9], refs[9:]
    if layer > 0:
        before_ref, w_out_ref, stream_ref, *refs = refs
    normed_ref, proj_ref, mixed_ref, scan_ref, saved_ref, act_ref, slope_ref, *refs = refs
    tables, (ext_ref, raw_ref, state_ref, gated_ref, keep_ref) = refs[:4], refs[4:]
    conv_ref, head_ref, wide_ref, spread_ref = tables

    @pl.when(pl.program_id(1) == 0)
    def _():
        state_ref[...] = jnp.zeros_like(state_ref)
        ext_ref[0:8] = jnp.zeros_like(ext_ref[0:8])

    @pl.when((pl.program_id(0) == 0) & (pl.program_id(1) == 0))
    def _():
        raw_ref[...] = jnp.zeros_like(raw_ref)
        prepare(layer, params, tables)

    stream = tokens_ref[...].astype(f32)
    if layer > 0:
        stream = stream + mm(before_ref[...], w_out_ref[...])
        stream_ref[...] = stream
    normed = stream * norm_scale(stream) * params[0][layer : layer + 1]
    normed_ref[...] = normed.T.astype(bf16)
    proj_ref[...] = mm(normed.astype(bf16), w_in_ref[...])
    ext_ref[8 : 8 + CH] = proj_ref[:, DI : DI + CONV_CH]
    shifted, step, cum, cum_t, grow, remain, rows, cols = step_parts(proj_ref, raw_ref, head_ref)
    step_w, grow_w, remain_w = [widen(spread_ref[...], v)[0] for v in (step, grow, remain * step)]

    def activated(j):
        value = conv_block(ext_ref, conv_ref, j)
        share = sigmoid(value)
        result = value * share
        act_ref[:, lanes(j)] = result
        slope_ref[:, lanes(j)] = share + result * (1.0 - share)
        return result

    b_low = activated(PAIRS).astype(bf16)
    c_low = activated(PAIRS + 1).astype(bf16)
    affinity = jnp.where(cols <= rows, mm_t(c_low, b_low), 0.0)
    state_low = state_ref[...].astype(bf16)
    saved_ref[...] = state_low
    carried = grow_w * mm(c_low, state_low)
    square = jnp.zeros((CH, LANE), f32)
    for j in range(PAIRS):
        xs = activated(j)
        mixing = []
        for h in (2 * j, 2 * j + 1):
            differ = jnp.minimum(cum[:, h : h + 1] - cum_t[h : h + 1], 0.0)
            mixing.append((jnp.exp2(differ) * affinity).astype(bf16))
        keep_ref[:, lanes(j)] = (xs * remain_w[:, lanes(j)]).astype(bf16)
        x_split = split_pair((xs * step_w[:, lanes(j)]).astype(bf16))
        scanned = mm(jnp.concatenate(mixing, axis=1), x_split) + carried[:, lanes(j)]
        scan_ref[:, lanes(j)] = scanned
        gate = proj_ref[:, lanes(j)]
        gated = (scanned + wide_ref[0:1, lanes(j)] * xs) * (gate * sigmoid(gate))
        gated_ref[:, lanes(j)] = gated
        square = square + gated * gated
    state_ref[...] = grow_w[CH - 1 : CH] * state_ref[...] + t_mm(b_low, keep_ref[...])
    scale = lax.rsqrt(jnp.sum(square, axis=1, keepdims=True) * (1.0 / DI) + epsilon)
    mixed_ref[...] = (gated_ref[...] * scale * wide_ref[1:2]).astype(bf16)
    ext_ref[0:8] = ext_ref[CH : CH + 8]


def backward_kernel(layer, *refs):
    params, refs = refs[:7], refs[7:]
    upstream_ref, stream_ref, w_in_ref, w_out_ref, proj_ref, scan_ref, saved_ref, act_ref, slope_ref, *refs = refs
    top = layer == LAYERS - 1
    if top:
        mixed_ref, length_ref, result_ref, *refs = refs
    out_ref, down_ref, sum_ref, *refs = refs
    tables, refs = refs[:4], refs[4:]
    conv_ref, head_ref, wide_ref, spread_ref = tables
    gather_ref, grad_ref, raw_ref, state_ref, gate_ref, dconv_ref, *refs = refs
    keep_ref, grown_ref, terms_ref, row_ref, back_ref = refs
    chunk = pl.num_programs(1) - 1 - pl.program_id(1)

    @pl.when(pl.program_id(1) == 0)
    def _():
        state_ref[...] = jnp.zeros_like(state_ref)
        dconv_ref[CH : CH + 8] = jnp.zeros_like(dconv_ref[CH : CH + 8])

    @pl.when((pl.program_id(0) == 0) & (pl.program_id(1) == 0))
    def _():
        raw_ref[...] = jnp.zeros_like(raw_ref)
        row_ref[...] = jnp.zeros_like(row_ref)
        sum_ref[...] = jnp.zeros_like(sum_ref)
        prepare(layer, params, tables, gather_ref)

    upstream = upstream_ref[...].astype(f32)
    grad_ref[...] = mm_t(upstream.astype(bf16), w_out_ref[...]).astype(bf16)
    shifted, step, cum, cum_t, grow, remain, rows, cols = step_parts(proj_ref, raw_ref, head_ref)
    step_w, grow_w, remain_w = [widen(spread_ref[...], v)[0] for v in (step, grow, remain)]

    square = jnp.zeros((CH, LANE), f32)
    along = jnp.zeros((CH, LANE), f32)
    for j in range(PAIRS):
        xs = act_ref[:, lanes(j)]
        gate = proj_ref[:, lanes(j)]
        open_share = sigmoid(gate)
        gate_ref[:, lanes(j)] = open_share
        gated = (scan_ref[:, lanes(j)] + wide_ref[0:1, lanes(j)] * xs) * (gate * open_share)
        square = square + gated * gated
        along = along + gated * (grad_ref[:, lanes(j)].astype(f32) * wide_ref[1:2, lanes(j)])
    scale = lax.rsqrt(jnp.sum(square, axis=1, keepdims=True) * (1.0 / DI) + epsilon)
    pull = scale * scale * scale * (jnp.sum(along, axis=1, keepdims=True) * (1.0 / DI))

    b_low = act_ref[:, lanes(PAIRS)].astype(bf16)
    c_low = act_ref[:, lanes(PAIRS + 1)].astype(bf16)
    affinity_t = jnp.where(rows <= cols, mm_t(b_low, c_low), 0.0)
    state = state_ref[...]
    state_low = state.astype(bf16)
    row_ref[1:2] = jnp.sum(saved_ref[...].astype(f32) * state, axis=0, keepdims=True)
    back = remain_w * mm(b_low, state_low)
    affinity_grad = jnp.zeros((CH, CH), f32)

    def back_from(first, end):
        part = mm_t(out_ref[:, first:end], w_in_ref[:, first:end])
        back_ref[...] = part if first == 0 else back_ref[...] + part

    for j in range(PAIRS):
        xs = act_ref[:, lanes(j)]
        skip = wide_ref[0:1, lanes(j)]
        grad = grad_ref[:, lanes(j)].astype(f32)
        gate = proj_ref[:, lanes(j)]
        open_share = gate_ref[:, lanes(j)]
        opened = gate * open_share
        scanned = scan_ref[:, lanes(j)]
        outer = scanned + skip * xs
        gated = outer * opened
        gated_grad = scale * (grad * wide_ref[1:2, lanes(j)]) - pull * gated
        sum_ref[6:7, lanes(j)] += jnp.sum(grad * (gated * scale), axis=0, keepdims=True)
        dy = gated_grad * opened
        out_ref[:, lanes(j)] = (gated_grad * outer * (open_share + opened * (1.0 - open_share))).astype(bf16)
        sum_ref[5:6, lanes(j)] += jnp.sum(dy * xs, axis=0, keepdims=True)
        dy_low = dy.astype(bf16)
        grown_ref[:, lanes(j)] = (grow_w[:, lanes(j)] * dy).astype(bf16)
        scaled = xs * step_w[:, lanes(j)]
        x_low = scaled.astype(bf16)
        keep_ref[:, lanes(j)] = (scaled * remain_w[:, lanes(j)]).astype(bf16)
        dy_split = split_pair(dy_low)
        kernels = []
        for h in (2 * j, 2 * j + 1):
            differ = jnp.minimum(cum_t[h : h + 1] - cum[:, h : h + 1], 0.0)
            kernels.append(jnp.exp2(differ))
        mixing_t = jnp.concatenate([(k * affinity_t).astype(bf16) for k in kernels], axis=1)
        arrived = back[:, lanes(j)]
        x_grad = mm(mixing_t, dy_split) + arrived
        mixing_grad = mm_t(x_low, dy_split)
        affinity_grad = affinity_grad + mixing_grad[:, :CH] * kernels[0] + mixing_grad[:, CH:] * kernels[1]
        x_back = x_low.astype(f32)
        row_ref[0:1, lanes(j)] = jnp.sum(x_back * arrived, axis=0, keepdims=True)
        high, low = high_low(dy_low.astype(f32) * scanned - x_back * x_grad)
        terms_ref[0:CH, lanes(j)] = high
        terms_ref[CH : 2 * CH, lanes(j)] = low
        terms_ref[2 * CH :, lanes(j)] = (x_grad * xs).astype(bf16)
        dconv_ref[0:CH, lanes(j)] = (step_w[:, lanes(j)] * x_grad + skip * dy) * slope_ref[:, lanes(j)]
        if j % 4 == 3:
            back_from(LANE * (j - 3), LANE * (j + 1))
    affinity_low = jnp.where(rows <= cols, affinity_grad, 0.0).astype(bf16)
    grown = grown_ref[...]
    b_grad = mm(affinity_low, c_low) + mm_t(keep_ref[...], state_low)
    c_grad = t_mm(affinity_low, b_low) + mm_t(grown, saved_ref[...])
    dconv_ref[0:CH, lanes(PAIRS)] = b_grad * slope_ref[:, lanes(PAIRS)]
    dconv_ref[0:CH, lanes(PAIRS + 1)] = c_grad * slope_ref[:, lanes(PAIRS + 1)]

    gather = gather_ref[...]
    row_sums = mm(jnp.concatenate(high_low(row_ref[...]), axis=0), gather)
    row_sums = row_sums[:8] + row_sums[8:]
    last_grad = row_sums[0:1] + grow[CH - 1 : CH] * row_sums[1:2]
    cum_grad = mm(terms_ref[0:CH], gather) + mm(terms_ref[CH : 2 * CH], gather)
    decay_grad = jnp.dot((cols >= rows).astype(f32), cum_grad, precision=lax.Precision.HIGHEST, preferred_element_type=f32) + last_grad
    step_grad = mm(terms_ref[2 * CH :], gather) + head_ref[2:3] * decay_grad
    raw_grad = step_grad * sigmoid(shifted)
    out_ref[:, DI + CONV_CH :] = raw_grad[:, :NH].astype(bf16)
    sum_ref[7:8, 0:LANE] += jnp.sum(raw_grad, axis=0, keepdims=True)
    sum_ref[7:8, LANE : 2 * LANE] += jnp.sum(decay_grad * step, axis=0, keepdims=True)
    state_ref[...] = grow_w[CH - 1 : CH] * state + t_mm(c_low, grown)

    for j in range(PAIRS + 2):
        taps = [dconv_ref[3 - k : 3 - k + CH, lanes(j)] for k in range(KW)]
        total = conv_ref[0:1, lanes(j)] * taps[0]
        for k in range(1, KW):
            total = total + conv_ref[k : k + 1, lanes(j)] * taps[k]
        out_ref[:, lanes(j, DI)] = total.astype(bf16)
        value = proj_ref[:, lanes(j, DI)]
        for k in range(KW):
            sum_ref[k : k + 1, lanes(j)] += jnp.sum(taps[k] * value, axis=0, keepdims=True)
        sum_ref[4:5, lanes(j)] += jnp.sum(taps[3], axis=0, keepdims=True)
        if top and j == 1:
            slot = lax.broadcasted_iota(jnp.int32, (CH, D), 0) + chunk * CH
            result = stream_ref[...] + mm(mixed_ref[...], w_out_ref[...])
            result_ref[...] = jnp.where(slot < length_ref[0:1, 0:1], result, 0.0).astype(bf16)
        if j in (3, 7, 11):
            back_from(DI + LANE * (j - 3), DI + LANE * (j + 1))
    dconv_ref[CH : CH + 8] = dconv_ref[0:8]

    back_from(2 * DI, DI + CONV_CH)
    back_from(DI + CONV_CH, NIN)
    normed_grad = back_ref[...]
    stream = stream_ref[...].astype(f32)
    scale = norm_scale(stream)
    sum_ref[7:8, 2 * LANE : 2 * LANE + D] += jnp.sum(normed_grad * (stream * scale), axis=0, keepdims=True)
    inner = normed_grad * params[0][layer : layer + 1]
    pull = scale * scale * scale * jnp.mean(inner * stream, axis=-1, keepdims=True)
    down_ref[...] = upstream_ref[...].astype(f32) + scale * inner - pull * stream


def ring_place(n):
    wide = n // 4
    me = lax.axis_index("shard")
    chip, core = me // 2, me % 2
    row, col = chip // wide, chip % wide
    place = row * (2 * wide - 1 - col) + (1 - row) * col

    def shard_of(at, c):
        at = at % (2 * wide)
        r = at // wide
        x = r * (2 * wide - 1 - at) + (1 - r) * at
        return (r * wide + x) * 2 + c

    return place, core, shard_of


def halves(rows):
    first = rows // 2 // 16 * 16
    return (0, first), (first, rows - first)


def aligned(start, size, unit=16):
    return pl.ds(pl.multiple_of(start, unit), size)


def column_groups(width, replicas, parts):
    unit = LANE * replicas
    units = -(-width // unit)
    parts = min(parts, units)
    groups, start = [], 0
    for g in range(parts):
        size = (units // parts + (g < units % parts)) * unit
        groups.append((start, size, min(size, width - start)))
        start += size
    return groups, start


def remote(src, dst, send, recv, axis, to):
    return pltpu.make_async_remote_copy(
        src_ref=src, dst_ref=dst, send_sem=send, recv_sem=recv, device_id={axis: to}, device_id_type=MESH
    )


def greet(near, across):
    barrier = pltpu.get_barrier_semaphore()
    for to in near:
        pl.semaphore_signal(barrier, inc=1, device_id={"shard": to}, device_id_type=MESH)
    for to in across:
        pl.semaphore_signal(barrier, inc=1, device_id={"replica": to}, device_id_type=MESH)


def meet(count):
    pl.semaphore_wait(pltpu.get_barrier_semaphore(), count)


def bits(count):
    levels = count.bit_length() - 1
    assert 1 << levels == count
    return levels


class Gather:
    def __init__(self, n, arrays, items):
        self.n, self.half = n, n // 4
        self.arrays, self.items = arrays, items
        self.rows = [arrays[i[0]].shape[1] for i in items]

    def in_specs(self):
        return [pl.BlockSpec(memory_space=pl.ANY)] * len(self.arrays)

    out_specs = in_specs

    def out_shapes(self):
        return [jax.ShapeDtypeStruct((a.shape[1] * self.n, a.shape[2]), a.dtype) for a in self.arrays]

    def scratch(self):
        count = len(self.items)
        dma = pltpu.SemaphoreType.DMA
        own = [pltpu.VMEM((rows, i[3]), self.arrays[i[0]].dtype) for rows, i in zip(self.rows, self.items)]
        return [dma((count, self.half, 2, 2)), dma((count, self.half + 1, 2, 2)), dma((count, 2))] + own

    def tracks(self, parts, wholes, scratch):
        ring_sem, pair_sem, own_sem, *own_refs = scratch
        n, half = self.n, self.half
        place, core, shard_of = ring_place(n)
        right, left, pair = shard_of(place + 1, core), shard_of(place + n // 2 - 1, core), shard_of(place, 1 - core)
        me = shard_of(place, core)
        ways = ((0, right), (1, left))

        def rows_of(i, s, d):
            return (0, self.rows[i]) if s < half else halves(self.rows[i])[d]

        def part_at(i, part):
            a, layer, first, wide = self.items[i]
            return parts[a].at[layer, part[0] : part[0] + part[1], first : first + wide]

        def whole_at(i, owner, part):
            a, _, first, wide = self.items[i]
            return wholes[a].at[aligned(owner * self.rows[i] + part[0], part[1]), first : first + wide]

        def hop(i, s, d, to):
            owner = shard_of(place + (n // 2 - (s - 1) if d == 0 else s - 1), core)
            part = rows_of(i, s, d)
            src = part_at(i, part) if s == 1 else whole_at(i, owner, part)
            return remote(src, whole_at(i, owner, part), ring_sem.at[i, s - 1, d, 0], ring_sem.at[i, s - 1, d, 1], "shard", to)

        def cross(i, s, d):
            owner = me if s == 0 else shard_of(place + (n // 2 - s if d == 0 else s), core)
            part = (0, self.rows[i]) if s == 0 else rows_of(i, s, d)
            src = part_at(i, part) if s == 0 else whole_at(i, owner, part)
            return remote(src, whole_at(i, owner, part), pair_sem.at[i, s, d, 0], pair_sem.at[i, s, d, 1], "shard", pair)

        def own_in(i):
            return pltpu.make_async_copy(part_at(i, (0, self.rows[i])), own_refs[i], own_sem.at[i, 0])

        def own_out(i):
            return pltpu.make_async_copy(own_refs[i], whole_at(i, me, (0, self.rows[i])), own_sem.at[i, 1])

        crossings = [(0, 0)] + [(s, d) for s in range(1, half + 1) for d in (0, 1)]

        def start(i):
            for d, to in ways:
                hop(i, 1, d, to).start()
            cross(i, 0, 0).start()
            own_in(i).start()

        def forward(i, s):
            if s == 1:
                own_in(i).wait()
                own_out(i).start()
            for d, to in ways:
                hop(i, s, d, to).wait_recv()
                if s < half:
                    hop(i, s + 1, d, to).start()
                cross(i, s, d).start()

        def last(i):
            for s, d in crossings:
                cross(i, s, d).wait_recv()
            for s, d in crossings:
                cross(i, s, d).wait_send()
            for s in range(1, half + 1):
                for d, to in ways:
                    hop(i, s, d, to).wait_send()
            own_out(i).wait()

        hello = [lambda: greet((right, left, pair), ()), lambda: meet(3)]
        return hello, [
            [lambda i=i: start(i)]
            + [lambda i=i, s=s: forward(i, s) for s in range(1, half + 1)]
            + [lambda i=i: last(i)]
            for i in range(len(self.items))
        ]


class Reduce:
    def __init__(self, n, replicas, shapes, groups, modes=None):
        self.n, self.replicas = n, replicas
        self.chips, self.half, self.levels = n // 2, n // 4, bits(replicas)
        self.shapes = [(r // n, w) for r, w in shapes]
        self.groups = [column_groups(w, replicas, count) for (_, w), count in zip(self.shapes, groups)]
        self.modes = modes or ["full"] * len(shapes)
        self.work = [(a, g) for a in range(len(shapes)) for g in range(len(self.groups[a][0]))]

    def in_specs(self):
        return [pl.BlockSpec(memory_space=pl.ANY)] * len(self.shapes)

    out_specs = in_specs

    def out_shapes(self):
        return [
            jax.ShapeDtypeStruct((rows, padded), bf16) if mode == "head" else jax.ShapeDtypeStruct((rows, width), f32)
            for (rows, width), (_, padded), mode in zip(self.shapes, self.groups, self.modes)
        ]

    each = 12

    def scratch(self):
        dma = pltpu.SemaphoreType.DMA
        items = []
        for (rows, width), (groups, padded), mode in zip(self.shapes, self.groups, self.modes):
            g = len(groups)
            plane = (rows, width) if mode != "tail" else (16, LANE)
            far = (rows, padded) if mode != "head" else (16, LANE)
            items += [
                pltpu.VMEM((self.chips,) + plane, bf16),
                pltpu.VMEM((self.chips,) + plane, bf16),
                pltpu.VMEM((self.half, 2) + plane, bf16),
                pltpu.VMEM((self.half, 2) + plane, bf16),
                pltpu.VMEM((rows, padded), bf16),
                pltpu.VMEM((self.levels,) + far, bf16),
                pltpu.VMEM(far, bf16),
                pltpu.VMEM((rows, width) if mode != "head" else (16, LANE), f32),
                dma((g, self.chips, 3)), dma((g, self.half, 2, 2)), dma((g, 2 * self.levels, 2)), dma((g,)),
            ]
        return items

    def tracks(self, ins, outs, scratch, feed=None):
        n, replicas, chips, half, levels = self.n, self.replicas, self.chips, self.half, self.levels
        place, core, shard_of = ring_place(n)
        right, left, pair = shard_of(place + 1, core), shard_of(place + chips - 1, core), shard_of(place, 1 - core)
        mine = lax.axis_index("replica")
        ways = ((0, right), (1, left))
        order = [half] + [v for s in range(half - 1, 0, -1) for v in (s, chips - s)] + [0]
        buffers = [scratch[self.each * a : self.each * (a + 1)] for a in range(len(self.shapes))]

        def partner(j):
            bit = mine // (1 << j) % 2
            return mine + (1 - 2 * bit) * (1 << j), bit

        def cols_of(a, g):
            start, _, wide = self.groups[a][0][g]
            return slice(start, start + wide)

        def piece(a, g, owner):
            rows = self.shapes[a][0]
            return ins[a].at[aligned(owner * rows, rows), cols_of(a, g)]

        def pairing(a, g, q):
            sem = buffers[a][8]
            return remote(piece(a, g, shard_of(place + q, 1 - core)), buffers[a][1].at[q, :, cols_of(a, g)], sem.at[g, q, 0], sem.at[g, q, 1], "shard", pair)

        def loading(a, g, q):
            return pltpu.make_async_copy(
                piece(a, g, shard_of(place + q, core)), buffers[a][0].at[q, :, cols_of(a, g)], buffers[a][8].at[g, q, 2]
            )

        def part_of(a, k, d):
            rows = self.shapes[a][0]
            return halves(rows)[d] if k == 1 else (0, rows)

        def ringing(a, g, k, d, to):
            first, count = part_of(a, k, d)
            sem = buffers[a][9]
            return remote(
                buffers[a][2].at[k - 1, d, first : first + count, cols_of(a, g)],
                buffers[a][3].at[k - 1, d, first : first + count, cols_of(a, g)],
                sem.at[g, k - 1, d, 0], sem.at[g, k - 1, d, 1], "shard", to,
            )

        def region(a, g, j, keep):
            start, size, _ = self.groups[a][0][g]
            at = start
            for i in range(j + 1):
                bit = mine // (1 << i) % 2
                at = at + (bit if keep or i < j else 1 - bit) * (size >> (i + 1))
            return aligned(at, size >> (j + 1), LANE)

        def halving(a, g, j):
            cols = region(a, g, j, False)
            sem = buffers[a][10]
            return remote(
                buffers[a][4].at[:, cols], buffers[a][5].at[j, :, cols], sem.at[g, j, 0], sem.at[g, j, 1], "replica", partner(j)[0]
            )

        def doubling(a, g, j):
            cols = region(a, g, j, True)
            sem = buffers[a][10]
            return remote(
                buffers[a][6].at[:, cols], buffers[a][6].at[:, cols],
                sem.at[g, levels + j, 0], sem.at[g, levels + j, 1], "replica", partner(j)[0],
            )

        def storing(a, g):
            cols = cols_of(a, g)
            return pltpu.make_async_copy(buffers[a][7].at[:, cols], outs[a].at[:, cols], buffers[a][11].at[g])

        def both(a, g, q, part):
            first, count = part
            rows, cols = slice(first, first + count), cols_of(a, g)
            return buffers[a][0][q, rows, cols].astype(f32) + buffers[a][1][q, rows, cols].astype(f32)

        def arrived(a, g, q):
            if not (feed and a == 0):
                loading(a, g, q).wait()
            pairing(a, g, q).wait_recv()

        def begin(a, g):
            fed = feed and a == 0
            if fed:
                feed(g, cols_of(a, g))
            for q in order:
                pairing(a, g, q).start()
                if fed:
                    buffers[a][0][q, :, cols_of(a, g)] = piece(a, g, shard_of(place + q, core))[...]
                else:
                    loading(a, g, q).start()

        def turn(a, g, k):
            cols = cols_of(a, g)
            for d, to in ways:
                q = half - k + 1 if d == 0 else chips - (half - k + 1)
                if k > 1 or d == 0:
                    arrived(a, g, q)
                if k > 1:
                    ringing(a, g, k - 1, d, to).wait_recv()
                pieces = [part_of(a, 1, d)] if k == 1 else halves(self.shapes[a][0]) if k == 2 else [part_of(a, k, d)]
                for e, (at, many) in enumerate(pieces):
                    value = both(a, g, q, (at, many))
                    if k > 2 or (k == 2 and e == d):
                        value = value + buffers[a][3][k - 2, d, at : at + many, cols].astype(f32)
                    buffers[a][2][k - 1, d, at : at + many, cols] = value.astype(bf16)
                ringing(a, g, k, d, to).start()

        def settle(a, g):
            cols = cols_of(a, g)
            start, size, wide = self.groups[a][0][g]
            rows = self.shapes[a][0]
            arrived(a, g, 0)
            value = both(a, g, 0, (0, rows))
            for d, to in ways:
                ringing(a, g, half, d, to).wait_recv()
                value = value + buffers[a][3][half - 1, d, :, cols].astype(f32)
            buffers[a][4][:, cols] = value.astype(bf16)
            if wide < size:
                buffers[a][4][:, start + wide : start + size] = jnp.zeros((rows, size - wide), bf16)
            if self.modes[a] == "head":
                handing(a, g).start()
            else:
                halving(a, g, 0).start()

        def handing(a, g):
            start, size, _ = self.groups[a][0][g]
            cols = slice(start, start + size)
            here, there = buffers[a][4].at[:, cols], (outs if self.modes[a] == "head" else ins)[a].at[:, cols]
            if self.modes[a] == "tail":
                here, there = there, here
            return pltpu.make_async_copy(here, there, buffers[a][11].at[g])

        def resume(a, g):
            handing(a, g).wait()
            halving(a, g, 0).start()

        def halve(a, g, j):
            halving(a, g, j).wait_recv()
            cols = region(a, g, j, True)
            value = (buffers[a][4][:, cols].astype(f32) + buffers[a][5][j, :, cols].astype(f32)).astype(bf16)
            if j + 1 < levels:
                buffers[a][4][:, cols] = value
                halving(a, g, j + 1).start()
            else:
                buffers[a][6][:, cols] = value
                doubling(a, g, j).start()

        def double(a, g, j):
            doubling(a, g, j).wait_recv()
            if j > 0:
                doubling(a, g, j - 1).start()

        def last(a, g):
            double(a, g, 0)
            cols = cols_of(a, g)
            buffers[a][7][:, cols] = buffers[a][6][:, cols].astype(f32)
            storing(a, g).start()
            if self.modes[a] != "tail":
                leave(a, g)
            for j in range(levels):
                halving(a, g, j).wait_send()
                doubling(a, g, j).wait_send()
            storing(a, g).wait()

        def leave(a, g):
            for q in order:
                pairing(a, g, q).wait_send()
            for k in range(1, half + 1):
                for d, to in ways:
                    ringing(a, g, k, d, to).wait_send()

        def part(a, g):
            leave(a, g)
            handing(a, g).wait()

        across = [partner(j)[0] for j in range(levels)]
        hello = [lambda: greet((right, left, pair), across), lambda: meet(3 + levels)]
        def track(a, g):
            planes = (
                [lambda: begin(a, g)]
                + [lambda k=k: turn(a, g, k) for k in range(1, half + 1)]
                + [lambda: settle(a, g)]
            )
            rest = (
                [lambda j=j: halve(a, g, j) for j in range(levels)]
                + [lambda j=j: double(a, g, j) for j in range(levels - 1, 0, -1)]
                + [lambda: last(a, g)]
            )
            if self.modes[a] == "head":
                return planes + [lambda: part(a, g)]
            if self.modes[a] == "tail":
                return [lambda: handing(a, g).start(), lambda: resume(a, g)] + rest
            return planes + rest

        return hello, [track(a, g) for a, g in self.work]


def beside(body, counts, engine, times, hooks):
    ins, outs, scratch = counts

    def kernel(*refs):
        i = len(engine.in_specs())
        o = len(engine.out_specs())
        own_in, refs = refs[:ins], refs[ins:]
        far_in, refs = refs[:i], refs[i:]
        own_out, refs = refs[:outs], refs[outs:]
        far_out, refs = refs[:o], refs[o:]
        own_scratch, far_scratch = refs[:scratch], refs[scratch:]
        hello, tracks = engine.tracks(far_in, far_out, far_scratch)
        plan = {}
        plan[0] = [hello[0]]
        plan.setdefault(min(t[0] for t in times), []).append(hello[1])
        for t, track in enumerate(tracks):
            wanted = times[t]
            if len(wanted) != len(track):
                first = wanted[0]
                wanted = [first + (hooks - first) * i // (len(track) - 1) for i in range(len(track))]
            for at, stage in zip(wanted, track):
                plan.setdefault(min(at, hooks), []).append(stage)
        step = pl.program_id(0) * pl.num_programs(1) + pl.program_id(1)

        def run(at):
            for stage in plan[at]:
                stage()

        pl.when(step == 0)(lambda: run(0))
        body(*own_in, *own_out, *own_scratch)
        for at in sorted(plan):
            if at > 0:
                pl.when(step == at - 1)(lambda at=at: run(at))

    return kernel


def move(engine, operands, collective_id, name):
    def kernel(*refs):
        i, o = len(engine.in_specs()), len(engine.out_specs())
        hello, tracks = engine.tracks(refs[:i], refs[i : i + o], refs[i + o :])
        for stage in hello:
            stage()
        for at in range(max(map(len, tracks))):
            for track in tracks:
                if at < len(track):
                    track[at]()

    return pl.pallas_call(
        kernel,
        out_shape=engine.out_shapes(),
        in_specs=engine.in_specs(),
        out_specs=engine.out_specs(),
        scratch_shapes=engine.scratch(),
        compiler_params=pltpu.CompilerParams(collective_id=collective_id, has_side_effects=True),
        name=name,
    )(*operands)


def finish_kernel(engine, n, replicas, *refs):
    left_ref, right_hbm, first_ref, second_ref, in_ref, out0_ref, out1_ref = refs[:7]
    in_total_ref, out_total_ref, total_ref = refs[7:10]
    product_ref, right_ref, mine_ref, plane_ref, across_ref, whole_ref, in_buf, out_buf = refs[10:18]
    plane_sem, across_sem, share_sem, copy_sem, right_sem, *scratch = refs[18:]
    me, mine = lax.axis_index("shard"), lax.axis_index("replica")
    width = mine_ref.shape[2]

    def operand(g):
        start, _, wide = engine.groups[0][0][g]
        cols = slice(start, start + wide)
        return pltpu.make_async_copy(right_hbm.at[:, cols], right_ref.at[:, cols], right_sem.at[g])

    for g in range(len(engine.groups[0][0])):
        operand(g).start()

    ready = set()

    def feed(g, cols):
        if g in ready:
            return
        ready.add(g)
        operand(g).wait()
        product_ref[:, cols] = mm(left_ref[...], right_ref[:, cols]).astype(bf16)

    _, tracks = engine.tracks((product_ref, out0_ref), (in_total_ref.at[0], out_total_ref.at[0]), scratch, feed)
    greet([(me + s) % n for s in range(1, n)], [(mine + s) % replicas for s in range(1, replicas)])
    moves = [(in_ref, in_buf, in_total_ref.at[1]), (out1_ref, out_buf, out_total_ref.at[1])]
    fetches = [pltpu.make_async_copy(src, via, copy_sem.at[0, i]) for i, (src, via, _) in enumerate(moves)]
    stores = [pltpu.make_async_copy(via, dst, copy_sem.at[1, i]) for i, (_, via, dst) in enumerate(moves)]
    for fetch in fetches:
        fetch.start()
    spots = [(k // (n // 2), k % (n // 2) * width) for k in range(n)]
    for k, (half, at) in enumerate(spots):
        mine_ref[k] = (second_ref if half else first_ref)[:, at : at + width]

    def plane(s):
        to = (me + s) % n
        return remote(mine_ref.at[to], plane_ref.at[s], plane_sem.at[0, s], plane_sem.at[1, s], "shard", to)

    def across(s):
        return remote(across_ref.at[0], across_ref.at[s], across_sem.at[0, s], across_sem.at[1, s], "replica", (mine + s) % replicas)

    def share(s):
        return remote(whole_ref.at[me], whole_ref.at[me], share_sem.at[0, s], share_sem.at[1, s], "shard", (me + s) % n)

    def sharing(s):
        owner = (me + n - s) % n
        return remote(whole_ref.at[owner], whole_ref.at[owner], share_sem.at[0, s], share_sem.at[1, s], "shard", (me + s) % n)

    def send_small():
        for s in range(1, n):
            plane(s).start()

    def sum_plane():
        value = mine_ref[me]
        for s in range(1, n):
            plane(s).wait_recv()
            value = value + plane_ref[s]
        across_ref[0] = value
        for s in range(1, replicas):
            across(s).start()

    def sum_across():
        for s in range(1, replicas):
            across(s).wait_recv()
        zero = jnp.zeros((8, width), f32)
        whole_ref[me] = lax.fori_loop(0, replicas, lambda i, acc: acc + across_ref[(mine - i + replicas) % replicas], zero)
        for s in range(1, n):
            share(s).start()

    def give_small():
        for s in range(1, n):
            sharing(s).wait_recv()
        for k, (half, at) in enumerate(spots):
            total_ref[8 * half : 8 * half + 8, at : at + width] = whole_ref[k]

    plan = {}
    for (a, g), track in zip(engine.work, tracks):
        for i, stage in enumerate(track):
            plan.setdefault(((g if a == 0 else 0) + (2 * i - 1 if i else 0), i), []).append(stage)
    feed(0, slice(0, engine.groups[0][0][0][2]))
    meet(n + replicas - 2)
    slots = sorted(plan)
    for k, slot in enumerate(slots):
        for stage in plan[slot]:
            stage()
        if k == 0:
            send_small()
        if k == len(slots) // 4:
            sum_plane()
            for fetch, store in zip(fetches, stores):
                fetch.wait()
                store.start()
        if k == len(slots) // 2:
            sum_across()
    give_small()
    for s in range(1, n):
        plane(s).wait_send()
        share(s).wait_send()
    for s in range(1, replicas):
        across(s).wait_send()
    for store in stores:
        store.wait()


def finish(left, right, sums, in_grad, out_grads, n, replicas, collective_id):
    rows, width = left.shape[0] // n, right.shape[1]
    out_rows, out_width = out_grads[1].shape
    engine = Reduce(n, replicas, [(left.shape[0], width), (out_rows * n, out_width)], [7, 1], ["full", "tail"])
    anywhere, vmem = pl.BlockSpec(memory_space=pl.ANY), pl.BlockSpec(memory_space=pltpu.VMEM)
    dma = pltpu.SemaphoreType.DMA
    small = (8, 2 * SUMS // n)
    return pl.pallas_call(
        lambda *refs: finish_kernel(engine, n, replicas, *refs),
        out_shape=[
            jax.ShapeDtypeStruct((LAYERS, rows, width), f32),
            jax.ShapeDtypeStruct((LAYERS, out_rows, out_width), f32),
            jax.ShapeDtypeStruct((LAYERS * 8, SUMS), f32),
        ],
        in_specs=[vmem, anywhere, vmem, vmem] + [anywhere] * 3,
        out_specs=[anywhere, anywhere, vmem],
        scratch_shapes=[
            pltpu.VMEM((n * rows, width), bf16),
            pltpu.VMEM(right.shape, bf16),
            pltpu.VMEM((n,) + small, f32),
            pltpu.VMEM((n,) + small, f32),
            pltpu.VMEM((replicas,) + small, f32),
            pltpu.VMEM((n,) + small, f32),
            pltpu.VMEM((rows, width), f32),
            pltpu.VMEM((out_rows, out_width), f32),
            dma((2, n)), dma((2, replicas)), dma((2, n)), dma((2, 2)), dma((len(engine.groups[0][0]),)),
        ] + engine.scratch(),
        compiler_params=pltpu.CompilerParams(collective_id=collective_id, has_side_effects=True, vmem_limit_bytes=60 * 2**20),
        name="finish",
    )(left, right, *sums, in_grad, *out_grads)


def results_kernel(count, total_ref, a_log_ref, *refs):
    from_refs, refs = refs[:count], refs[count:]
    to_refs, refs = refs[:count], refs[count:]
    gain_ref, conv_w_ref, conv_b_ref, dt_bias_ref, a_log_grad_ref, d_skip_ref, out_gain_ref, *refs = refs
    via_refs, sem = refs[:count], refs[count]
    fetches = [pltpu.make_async_copy(a, b, sem.at[0, i]) for i, (a, b) in enumerate(zip(from_refs, via_refs))]
    stores = [pltpu.make_async_copy(a, b, sem.at[1, i]) for i, (a, b) in enumerate(zip(via_refs, to_refs))]
    for fetch in fetches:
        fetch.start()
    for fetch, store in zip(fetches, stores):
        fetch.wait()
        store.start()
    column = lax.broadcasted_iota(jnp.int32, (DI, LANE), 1)
    owner = lax.broadcasted_iota(jnp.int32, (DI, LANE), 0) // HEAD
    gather = (column == owner).astype(f32).astype(bf16)
    for l in range(LAYERS):
        here, row = slice(l, l + 1), 8 * l
        gain_ref[here] = total_ref[row + 7 : row + 8, 2 * LANE : 2 * LANE + D]
        conv_w_ref[l] = total_ref[row : row + KW, :CONV_CH]
        conv_b_ref[here] = total_ref[row + 4 : row + 5, :CONV_CH]
        dt_bias_ref[here] = total_ref[row + 7 : row + 8, 0:NH]
        a_log_grad_ref[here] = -jnp.exp(a_log_ref[here]) * total_ref[row + 7 : row + 8, LANE : LANE + NH]
        out_gain_ref[here] = total_ref[row + 6 : row + 7, :DI]
        value = total_ref[row : row + 8, :DI]
        high = value.astype(bf16)
        middle = (value - high.astype(f32)).astype(bf16)
        low = (value - high.astype(f32) - middle.astype(f32)).astype(bf16)
        summed = mm(high, gather) + mm(middle, gather) + mm(low, gather)
        d_skip_ref[here] = summed[5:6, 0:NH]
    for store in stores:
        store.wait()


def results(total, params, moved):
    anywhere, vmem = pl.BlockSpec(memory_space=pl.ANY), pl.BlockSpec(memory_space=pltpu.VMEM)
    count = len(moved)
    out = pl.pallas_call(
        lambda *refs: results_kernel(count, *refs),
        in_specs=[vmem, vmem] + [anywhere] * count,
        out_specs=[anywhere] * count + [vmem] * len(params),
        out_shape=[jax.ShapeDtypeStruct(m.shape, m.dtype) for m in moved] + [jax.ShapeDtypeStruct(p.shape, f32) for p in params],
        scratch_shapes=[pltpu.VMEM(m.shape, m.dtype) for m in moved] + [pltpu.SemaphoreType.DMA((2, count))],
        compiler_params=pltpu.CompilerParams(vmem_limit_bytes=62 * 2**20),
        name="results",
    )(total, params[4], *moved)
    return out[:count], out[count:]


def product_kernel(left_ref, right_ref, from_ref, out_ref, to_ref, via_ref, sem):
    step, last = pl.program_id(0), pl.num_programs(0) - 1
    fetch = pltpu.make_async_copy(from_ref, via_ref, sem.at[0])
    store = pltpu.make_async_copy(via_ref, to_ref, sem.at[1])
    pl.when(step == 0)(fetch.start)
    out_ref[...] = mm(left_ref[...], right_ref[...]).astype(bf16)

    @pl.when(step == 1)
    def _():
        fetch.wait()
        store.start()

    pl.when(step == last)(store.wait)


def product(left, right, wide, moved):
    (rows, depth), width = left.shape, right.shape[1]
    anywhere = pl.BlockSpec(memory_space=pl.ANY)
    return pl.pallas_call(
        product_kernel,
        grid=(pl.cdiv(width, wide),),
        in_specs=[pl.BlockSpec((rows, depth), lambda c: (0, 0)), pl.BlockSpec((depth, wide), lambda c: (0, c)), anywhere],
        out_specs=[pl.BlockSpec((rows, wide), lambda c: (0, c)), anywhere],
        out_shape=[jax.ShapeDtypeStruct((rows, width), bf16), jax.ShapeDtypeStruct(moved.shape, moved.dtype)],
        scratch_shapes=[pltpu.VMEM(moved.shape, moved.dtype), pltpu.SemaphoreType.DMA((2,))],
        compiler_params=pltpu.CompilerParams(vmem_limit_bytes=62 * 2**20),
        name="product",
    )(left, right, moved)


def turned_kernel(left_ref, right_ref, out_ref):
    out_ref[...] = t_mm(left_ref[...], right_ref[...].astype(bf16)).astype(bf16)


def turned_product(left, right, tall):
    (depth, rows), width = left.shape, right.shape[1]
    return pl.pallas_call(
        turned_kernel,
        grid=(rows // tall,),
        in_specs=[pl.BlockSpec((depth, tall), lambda r: (0, r)), pl.BlockSpec((depth, width), lambda r: (0, 0))],
        out_specs=pl.BlockSpec((tall, width), lambda r: (r, 0)),
        out_shape=jax.ShapeDtypeStruct((rows, width), bf16),
        compiler_params=pltpu.CompilerParams(vmem_limit_bytes=62 * 2**20),
        name="turned_product",
    )(left, right)


def top_kernel(row_total, slots, left_ref, cotangent_ref, lengths_ref, dealing_ref, out_ref, upstream_ref, length_ref):
    @pl.when(pl.program_id(0) == 0)
    def _():
        mine = lax.axis_index("replica") * lax.axis_size("shard") + lax.axis_index("shard")
        place = lax.broadcasted_iota(jnp.int32, lengths_ref.shape, 1)
        dealing, lengths = dealing_ref[...].astype(f32), lengths_ref[...].astype(f32)
        slot = lax.broadcasted_iota(jnp.int32, (slots, D), 0)
        for m in range(MICRO):
            sequence = jnp.sum(jnp.where(place == m * row_total + mine, dealing, 0.0), axis=1, keepdims=True)
            length = jnp.sum(jnp.where(place.astype(f32) == sequence, lengths, 0.0), axis=1, keepdims=True).astype(jnp.int32)
            length_ref[8 * m : 8 * m + 8] = jnp.broadcast_to(length, (8, LANE))
            here = slice(m * slots, (m + 1) * slots)
            upstream_ref[here] = jnp.where(slot < length, cotangent_ref[here].astype(f32), 0.0).astype(bf16)

    out_ref[...] = t_mm(left_ref[...], upstream_ref[...]).astype(bf16)


def top_product(left, cotangent, lengths, dealing, row_total, tall):
    (depth, rows), width = left.shape, cotangent.shape[1]
    whole = lambda shape: pl.BlockSpec(shape, lambda r: (0, 0))
    sequences = lengths.shape[0]
    return pl.pallas_call(
        lambda *refs: top_kernel(row_total, depth // MICRO, *refs),
        grid=(rows // tall,),
        in_specs=[pl.BlockSpec((depth, tall), lambda r: (0, r)), whole((depth, width)), whole((1, sequences)), whole((1, sequences))],
        out_specs=[pl.BlockSpec((tall, width), lambda r: (r, 0)), whole((depth, width)), whole((8 * MICRO, LANE))],
        out_shape=[
            jax.ShapeDtypeStruct((rows, width), bf16),
            jax.ShapeDtypeStruct((depth, width), bf16),
            jax.ShapeDtypeStruct((8 * MICRO, LANE), jnp.int32),
        ],
        compiler_params=pltpu.CompilerParams(vmem_limit_bytes=62 * 2**20),
        name="top_product",
    )(left, cotangent, lengths.reshape(1, sequences), dealing.reshape(1, sequences))


def fixed(shape):
    return pl.BlockSpec(shape, lambda r, c: (0,) * len(shape))


def held(shape):
    return pl.BlockSpec(shape, lambda r, c: (0,) * len(shape), pipeline_mode=pl.Buffered(1))


def grid_call(body, grid, operands, in_specs, out_specs, out_shapes, scratch, name, extra):
    engine, given, times, collective_id = extra
    kernel = beside(body, (len(in_specs), len(out_specs), len(scratch)), engine, times, grid[0] * grid[1])
    return pl.pallas_call(
        kernel, grid=grid, in_specs=in_specs + engine.in_specs(), out_specs=out_specs + engine.out_specs(),
        out_shape=out_shapes + engine.out_shapes(), scratch_shapes=scratch + engine.scratch(),
        compiler_params=pltpu.CompilerParams(
            dimension_semantics=("arbitrary", "arbitrary"), vmem_limit_bytes=60 * 2**20,
            collective_id=collective_id, has_side_effects=True,
        ),
        name=name,
    )(*operands, *given)


def layer_forward(layer, tokens, w_in, before, w_out, params, chunks, extra):
    count = tokens.shape[0]
    block = lambda r, c: (r * chunks + c, 0)
    later = layer > 0
    rows = lambda width: pl.BlockSpec((CH, width), block)
    return grid_call(
        lambda *refs: forward_kernel(layer, *refs),
        (count // (chunks * CH), chunks),
        (*params, tokens, w_in) + ((before, w_out) if later else ()),
        [held(p.shape) for p in params] + [rows(D), held((D, NIN))] + ([rows(DI), held((DI, D))] if later else []),
        ([rows(D)] if later else [])
        + [pl.BlockSpec((D, CH), lambda r, c: (0, r * chunks + c)), rows(NIN), rows(DI), rows(DI), pl.BlockSpec((NSTATE, DI), block), rows(CONV_CH), rows(CONV_CH)],
        ([jax.ShapeDtypeStruct((count, D), f32)] if later else [])
        + [
            jax.ShapeDtypeStruct((D, count), bf16),
            jax.ShapeDtypeStruct((count, NIN), f32),
            jax.ShapeDtypeStruct((count, DI), bf16),
            jax.ShapeDtypeStruct((count, DI), f32),
            jax.ShapeDtypeStruct((count // CH * NSTATE, DI), bf16),
            jax.ShapeDtypeStruct((count, CONV_CH), f32),
            jax.ShapeDtypeStruct((count, CONV_CH), f32),
        ],
        table_scratch()
        + [
            pltpu.VMEM((CH + 8, CONV_CH), f32),
            pltpu.VMEM((CH, LANE), f32),
            pltpu.VMEM((NSTATE, DI), f32),
            pltpu.VMEM((CH, DI), f32),
            pltpu.VMEM((CH, DI), bf16),
        ],
        f"layer_forward_{layer}", extra,
    )


def layer_backward(layer, upstream, stream, w_in, w_out, projected, kept, mixed, length, params, chunks, extra):
    count = projected.shape[0]
    block = lambda r, c: (r * chunks + chunks - 1 - c, 0)
    rows = lambda width: pl.BlockSpec((CH, width), block)
    top = layer == LAYERS - 1
    return grid_call(
        lambda *refs: backward_kernel(layer, *refs),
        (count // (chunks * CH), chunks),
        (*params, upstream, stream, w_in, w_out, projected, *kept) + ((mixed, length) if top else ()),
        [held(p.shape) for p in params]
        + [rows(D), rows(D), held((D, NIN)), held((DI, D)), rows(NIN), rows(DI), pl.BlockSpec((NSTATE, DI), block), rows(CONV_CH), rows(CONV_CH)]
        + ([rows(DI), pl.BlockSpec((8, LANE), lambda r, c: (r, 0))] if top else []),
        ([rows(D)] if top else []) + [rows(NIN), rows(D), fixed((8, SUMS))],
        ([jax.ShapeDtypeStruct((count, D), bf16)] if top else [])
        + [
            jax.ShapeDtypeStruct((count, NIN), bf16),
            jax.ShapeDtypeStruct((count, D), f32),
            jax.ShapeDtypeStruct((8, SUMS), f32),
        ],
        table_scratch()
        + [
            pltpu.VMEM((DI, LANE), bf16),
            pltpu.VMEM((CH, DI), bf16),
            pltpu.VMEM((CH, LANE), f32),
            pltpu.VMEM((NSTATE, DI), f32),
            pltpu.VMEM((CH, DI), f32),
            pltpu.VMEM((CH + 8, CONV_CH), f32),
            pltpu.VMEM((CH, DI), bf16),
            pltpu.VMEM((CH, DI), bf16),
            pltpu.VMEM((3 * CH, DI), bf16),
            pltpu.VMEM((8, DI), f32),
            pltpu.VMEM((CH, D), f32),
        ],
        f"layer_backward_{layer}", extra,
    )


def shards(
    tokens, cotangent, lengths, dealing, in_gain, w_in, conv_w, conv_b, dt_bias, a_log, d_skip, out_gain, w_out,
):
    n, replicas = lax.axis_size("shard"), lax.axis_size("replica")
    slot_count = tokens.shape[2]
    chunks = slot_count // CH
    count = MICRO * slot_count
    params = (in_gain, conv_w, conv_b, dt_bias, a_log, d_skip, out_gain)
    flat = tokens.reshape(count, D)

    (first_in,) = move(Gather(n, [w_in], [(0, 0, 0, CUT), (0, 0, CUT, NIN - CUT)]), (w_in,), 1, "gather_first")
    engine = Gather(n, [w_out, w_in], [(0, 0, 0, D), (1, 1, 0, CUT), (1, 1, CUT, NIN - CUT)])
    normed0, projected0, mixed0, *kept0, first_out, second_in = layer_forward(
        0, flat, first_in, None, None, params, chunks, (engine, (w_out, w_in), GATHER_BOTH, 2)
    )
    engine = Gather(n, [w_out], [(0, 1, 0, D)])
    stream, normed1, projected1, mixed1, *kept1, second_out = layer_forward(
        1, flat, second_in, mixed0, first_out, params, chunks, (engine, (w_out,), GATHER_LAST, 3)
    )

    out_grad1, upstream, length = top_product(mixed1, cotangent.reshape(count, D), lengths, dealing, replicas * n, 512)
    engine = Reduce(n, replicas, [out_grad1.shape], [1])
    result, project_grad1, upstream1, sums1, out_total1 = layer_backward(
        1, upstream, stream, second_in, second_out, projected1, kept1, mixed1, length, params, chunks,
        (engine, (out_grad1,), REDUCE_OUT, 4),
    )
    in_grad1, result = product(normed1, project_grad1, 512, result)
    out_grad0 = turned_product(mixed0, upstream1, 512)
    engine = Reduce(n, replicas, [in_grad1.shape, out_grad0.shape], [2, 1], ["full", "head"])
    project_grad0, upstream0, sums0, in_total1, out_total0 = layer_backward(
        0, upstream1, flat, first_in, first_out, projected0, kept0, None, None, params, chunks,
        (engine, (in_grad1, out_grad0), REDUCE_BOTH, 5),
    )
    in_total, out_total, small = finish(
        normed0, project_grad0, (sums0, sums1), in_total1, (out_total0, out_total1), n, replicas, 6
    )
    (upstream0, in_total, out_total), (gain_grad, *small) = results(small, params, (upstream0, in_total, out_total))
    shape = (MICRO, 1, slot_count, D)
    return (result.reshape(shape), upstream0.reshape(shape), gain_grad, in_total, *small, out_total)


def solution(mesh):
    rows = P(None, ("replica", "shard"), None, None)
    split = P(None, "shard", None)
    in_specs = (rows, rows, P(), P(), P(), split, P(), P(), P(), P(), P(), P(), split)
    out_specs = (rows, rows, P(), split, P(), P(), P(), P(), P(), P(), split)
    return jax.shard_map(shards, mesh=mesh, in_specs=in_specs, out_specs=out_specs, check_vma=False)
```

```python
import jax
import jax.numpy as jnp
from jax import lax
from jax.experimental import pallas as pl
from jax.experimental.pallas import tpu as pltpu
from jax.sharding import PartitionSpec as P

D = 768
DI = 1536
NH = 24
HEAD = 64
NSTATE = 128
KW = 4
CONV_CH = 1792
NIN = 3352
LAYERS = 2
MICRO = 2
CH = 128
PAIRS = NH // 2
LANE = 128
DUP = 32
LOG2E = 1.4426950408889634
SUMS = 2048
CUT = 1664
GATHER_BOTH = ((0, 3, 7, 8), (0, 5, 8, 8), (0, 7, 8, 8))
GATHER_LAST = ((1, 4, 6, 8),)
REDUCE_OUT = ((1, 2, 3, 4, 5, 6, 7, 8),)
REDUCE_BOTH = ((0, 1, 2, 3, 4, 5, 6, 7), (0, 1, 2, 4, 5, 6, 7, 8), (0, 3, 5, 7, 8))

epsilon = 1e-05
f32 = jnp.float32
bf16 = jnp.bfloat16
MESH = pl.DeviceIdType.MESH


def mm(a, b):
    return jnp.dot(a, b, preferred_element_type=f32)


def mm_t(a, b):
    return lax.dot_general(a, b, (((1,), (1,)), ((), ())), preferred_element_type=f32)


def t_mm(a, b):
    return lax.dot_general(a, b, (((0,), (0,)), ((), ())), preferred_element_type=f32)


def sigmoid(v):
    return 0.5 * jnp.tanh(0.5 * v) + 0.5


def softplus(v):
    return jnp.maximum(v, 0.0) + jnp.log1p(jnp.exp(-jnp.abs(v)))


def lanes(j, base=0):
    return slice(base + LANE * j, base + LANE * (j + 1))


def norm_scale(stream):
    return lax.rsqrt(jnp.mean(stream * stream, axis=-1, keepdims=True) + epsilon)


def split_pair(v):
    left = lax.broadcasted_iota(jnp.int32, v.shape, 1) < HEAD
    zero = jnp.zeros_like(v)
    return jnp.concatenate([jnp.where(left, v, zero), jnp.where(left, zero, v)], axis=0)


def high_low(v):
    high = v.astype(bf16)
    return high, (v - high.astype(f32)).astype(bf16)


def widen(spread, *values):
    parts = []
    for v in values:
        high, low = high_low(v)
        first = lax.broadcasted_iota(jnp.int32, v.shape, 1) < DUP
        parts.append(jnp.where(first, high, low))
    rows = values[0].shape[0]
    wide = mm(jnp.concatenate(parts, axis=0), spread)
    return [wide[i * rows : (i + 1) * rows] for i in range(len(values))]


def exact_mm(mask, v):
    high, low = high_low(v)
    rest = (v - high.astype(f32) - low.astype(f32)).astype(bf16)
    out = mm(mask.astype(f32).astype(bf16), jnp.concatenate([high, low, rest], axis=1))
    return out[:, :LANE] + out[:, LANE : 2 * LANE] + out[:, 2 * LANE :]


def step_parts(proj_ref, raw_ref, head_ref):
    raw = proj_ref[:, DI + CONV_CH :]
    raw_ref[:, 0:NH] = raw
    raw_ref[:, DUP : DUP + NH] = raw
    shifted = raw_ref[...] + head_ref[0:1]
    step = softplus(shifted)
    rows = lax.broadcasted_iota(jnp.int32, (CH, CH), 0)
    cols = lax.broadcasted_iota(jnp.int32, (CH, CH), 1)
    cum = jnp.dot((cols <= rows).astype(f32), head_ref[1:2] * step, precision=lax.Precision.HIGHEST, preferred_element_type=f32)
    grow = jnp.exp2(cum)
    remain = jnp.exp2(cum[CH - 1 : CH] - cum)
    return shifted, step, cum, cum.T, grow, remain, rows, cols


def conv_block(ext_ref, conv_ref, j):
    total = conv_ref[4:5, lanes(j)]
    for k in range(KW):
        total = total + conv_ref[k : k + 1, lanes(j)] * ext_ref[5 + k : 5 + k + CH, lanes(j)]
    return total


def prepare(layer, params, tables, gather_ref=None):
    in_gain_ref, conv_w_ref, conv_b_ref, dt_bias_ref, a_log_ref, d_skip_ref, out_gain_ref = params
    conv_ref, head_ref, wide_ref, spread_ref = tables
    conv_ref[0:KW] = conv_w_ref[layer]
    conv_ref[KW : KW + 1] = conv_b_ref[layer : layer + 1]
    head_ref[...] = jnp.zeros_like(head_ref)
    rate = -jnp.exp(a_log_ref[layer : layer + 1])
    for row, value in enumerate((dt_bias_ref[layer : layer + 1], rate * LOG2E, rate, d_skip_ref[layer : layer + 1])):
        head_ref[row : row + 1, 0:NH] = value
        head_ref[row : row + 1, DUP : DUP + NH] = value
    column = lax.broadcasted_iota(jnp.int32, (LANE, DI), 0)
    owner = lax.broadcasted_iota(jnp.int32, (LANE, DI), 1) // HEAD
    spread_ref[...] = ((column % DUP == owner) & (column < 2 * DUP)).astype(f32).astype(bf16)
    wide_ref[...] = widen(spread_ref[...], head_ref[...])[0]
    wide_ref[0:1] = wide_ref[3:4]
    wide_ref[1:2] = out_gain_ref[layer : layer + 1]
    if gather_ref is not None:
        column = lax.broadcasted_iota(jnp.int32, (DI, LANE), 1)
        owner = lax.broadcasted_iota(jnp.int32, (DI, LANE), 0) // HEAD
        gather_ref[...] = ((column % DUP == owner) & (column < 2 * DUP)).astype(f32).astype(bf16)


def table_scratch():
    return [
        pltpu.VMEM((8, CONV_CH), f32), pltpu.VMEM((8, LANE), f32), pltpu.VMEM((8, DI), f32), pltpu.VMEM((LANE, DI), bf16),
    ]


def forward_kernel(layer, *refs):
    params, (tokens_ref, w_in_ref), refs = refs[:7], refs[7:9], refs[9:]
    if layer > 0:
        before_ref, w_out_ref, stream_ref, *refs = refs
    normed_ref, proj_ref, mixed_ref, scan_ref, saved_ref, act_ref, slope_ref, *refs = refs
    tables, (ext_ref, raw_ref, state_ref, gated_ref, keep_ref) = refs[:4], refs[4:]
    conv_ref, head_ref, wide_ref, spread_ref = tables

    @pl.when(pl.program_id(1) == 0)
    def _():
        state_ref[...] = jnp.zeros_like(state_ref)
        ext_ref[0:8] = jnp.zeros_like(ext_ref[0:8])

    @pl.when((pl.program_id(0) == 0) & (pl.program_id(1) == 0))
    def _():
        raw_ref[...] = jnp.zeros_like(raw_ref)
        prepare(layer, params, tables)

    stream = tokens_ref[...].astype(f32)
    if layer > 0:
        stream = stream + mm(before_ref[...], w_out_ref[...])
        stream_ref[...] = stream
    normed = stream * norm_scale(stream) * params[0][layer : layer + 1]
    normed_ref[...] = normed.T.astype(bf16)
    proj_ref[...] = mm(normed.astype(bf16), w_in_ref[...])
    ext_ref[8 : 8 + CH] = proj_ref[:, DI : DI + CONV_CH]
    shifted, step, cum, cum_t, grow, remain, rows, cols = step_parts(proj_ref, raw_ref, head_ref)
    step_w, grow_w, remain_w = [widen(spread_ref[...], v)[0] for v in (step, grow, remain * step)]

    def activated(j):
        value = conv_block(ext_ref, conv_ref, j)
        share = sigmoid(value)
        result = value * share
        act_ref[:, lanes(j)] = result
        slope_ref[:, lanes(j)] = share + result * (1.0 - share)
        return result

    b_low = activated(PAIRS).astype(bf16)
    c_low = activated(PAIRS + 1).astype(bf16)
    affinity = jnp.where(cols <= rows, mm_t(c_low, b_low), 0.0)
    state_low = state_ref[...].astype(bf16)
    saved_ref[...] = state_low
    carried = grow_w * mm(c_low, state_low)
    square = jnp.zeros((CH, LANE), f32)
    for j in range(PAIRS):
        xs = activated(j)
        mixing = []
        for h in (2 * j, 2 * j + 1):
            differ = jnp.minimum(cum[:, h : h + 1] - cum_t[h : h + 1], 0.0)
            mixing.append((jnp.exp2(differ) * affinity).astype(bf16))
        keep_ref[:, lanes(j)] = (xs * remain_w[:, lanes(j)]).astype(bf16)
        x_split = split_pair((xs * step_w[:, lanes(j)]).astype(bf16))
        scanned = mm(jnp.concatenate(mixing, axis=1), x_split) + carried[:, lanes(j)]
        scan_ref[:, lanes(j)] = scanned
        gate = proj_ref[:, lanes(j)]
        gated = (scanned + wide_ref[0:1, lanes(j)] * xs) * (gate * sigmoid(gate))
        gated_ref[:, lanes(j)] = gated
        square = square + gated * gated
    state_ref[...] = grow_w[CH - 1 : CH] * state_ref[...] + t_mm(b_low, keep_ref[...])
    scale = lax.rsqrt(jnp.sum(square, axis=1, keepdims=True) * (1.0 / DI) + epsilon)
    mixed_ref[...] = (gated_ref[...] * scale * wide_ref[1:2]).astype(bf16)
    ext_ref[0:8] = ext_ref[CH : CH + 8]


def backward_kernel(layer, *refs):
    params, refs = refs[:7], refs[7:]
    upstream_ref, stream_ref, w_in_ref, w_out_ref, proj_ref, scan_ref, saved_ref, act_ref, slope_ref, *refs = refs
    top = layer == LAYERS - 1
    if top:
        mixed_ref, length_ref, result_ref, *refs = refs
    out_ref, down_ref, sum_ref, *refs = refs
    tables, refs = refs[:4], refs[4:]
    conv_ref, head_ref, wide_ref, spread_ref = tables
    gather_ref, grad_ref, raw_ref, state_ref, gate_ref, dconv_ref, *refs = refs
    keep_ref, grown_ref, terms_ref, row_ref, back_ref = refs
    chunk = pl.num_programs(1) - 1 - pl.program_id(1)

    @pl.when(pl.program_id(1) == 0)
    def _():
        state_ref[...] = jnp.zeros_like(state_ref)
        dconv_ref[CH : CH + 8] = jnp.zeros_like(dconv_ref[CH : CH + 8])

    @pl.when((pl.program_id(0) == 0) & (pl.program_id(1) == 0))
    def _():
        raw_ref[...] = jnp.zeros_like(raw_ref)
        row_ref[...] = jnp.zeros_like(row_ref)
        sum_ref[...] = jnp.zeros_like(sum_ref)
        prepare(layer, params, tables, gather_ref)

    upstream = upstream_ref[...].astype(f32)
    grad_ref[...] = mm_t(upstream.astype(bf16), w_out_ref[...]).astype(bf16)
    shifted, step, cum, cum_t, grow, remain, rows, cols = step_parts(proj_ref, raw_ref, head_ref)
    step_w, grow_w, remain_w = [widen(spread_ref[...], v)[0] for v in (step, grow, remain)]

    square = jnp.zeros((CH, LANE), f32)
    along = jnp.zeros((CH, LANE), f32)
    for j in range(PAIRS):
        xs = act_ref[:, lanes(j)]
        gate = proj_ref[:, lanes(j)]
        open_share = sigmoid(gate)
        gate_ref[:, lanes(j)] = open_share
        gated = (scan_ref[:, lanes(j)] + wide_ref[0:1, lanes(j)] * xs) * (gate * open_share)
        square = square + gated * gated
        along = along + gated * (grad_ref[:, lanes(j)].astype(f32) * wide_ref[1:2, lanes(j)])
    scale = lax.rsqrt(jnp.sum(square, axis=1, keepdims=True) * (1.0 / DI) + epsilon)
    pull = scale * scale * scale * (jnp.sum(along, axis=1, keepdims=True) * (1.0 / DI))

    b_low = act_ref[:, lanes(PAIRS)].astype(bf16)
    c_low = act_ref[:, lanes(PAIRS + 1)].astype(bf16)
    affinity_t = jnp.where(rows <= cols, mm_t(b_low, c_low), 0.0)
    state = state_ref[...]
    state_low = state.astype(bf16)
    row_ref[1:2] = jnp.sum(saved_ref[...].astype(f32) * state, axis=0, keepdims=True)
    back = remain_w * mm(b_low, state_low)
    affinity_grad = jnp.zeros((CH, CH), f32)

    def back_from(first, end):
        part = mm_t(out_ref[:, first:end], w_in_ref[:, first:end])
        back_ref[...] = part if first == 0 else back_ref[...] + part

    for j in range(PAIRS):
        xs = act_ref[:, lanes(j)]
        skip = wide_ref[0:1, lanes(j)]
        grad = grad_ref[:, lanes(j)].astype(f32)
        gate = proj_ref[:, lanes(j)]
        open_share = gate_ref[:, lanes(j)]
        opened = gate * open_share
        scanned = scan_ref[:, lanes(j)]
        outer = scanned + skip * xs
        gated = outer * opened
        gated_grad = scale * (grad * wide_ref[1:2, lanes(j)]) - pull * gated
        sum_ref[6:7, lanes(j)] += jnp.sum(grad * (gated * scale), axis=0, keepdims=True)
        dy = gated_grad * opened
        out_ref[:, lanes(j)] = (gated_grad * outer * (open_share + opened * (1.0 - open_share))).astype(bf16)
        sum_ref[5:6, lanes(j)] += jnp.sum(dy * xs, axis=0, keepdims=True)
        dy_low = dy.astype(bf16)
        grown_ref[:, lanes(j)] = (grow_w[:, lanes(j)] * dy).astype(bf16)
        scaled = xs * step_w[:, lanes(j)]
        x_low = scaled.astype(bf16)
        keep_ref[:, lanes(j)] = (scaled * remain_w[:, lanes(j)]).astype(bf16)
        dy_split = split_pair(dy_low)
        kernels = []
        for h in (2 * j, 2 * j + 1):
            differ = jnp.minimum(cum_t[h : h + 1] - cum[:, h : h + 1], 0.0)
            kernels.append(jnp.exp2(differ))
        mixing_t = jnp.concatenate([(k * affinity_t).astype(bf16) for k in kernels], axis=1)
        arrived = back[:, lanes(j)]
        x_grad = mm(mixing_t, dy_split) + arrived
        mixing_grad = mm_t(x_low, dy_split)
        affinity_grad = affinity_grad + mixing_grad[:, :CH] * kernels[0] + mixing_grad[:, CH:] * kernels[1]
        x_back = x_low.astype(f32)
        row_ref[0:1, lanes(j)] = jnp.sum(x_back * arrived, axis=0, keepdims=True)
        high, low = high_low(dy_low.astype(f32) * scanned - x_back * x_grad)
        terms_ref[0:CH, lanes(j)] = high
        terms_ref[CH : 2 * CH, lanes(j)] = low
        terms_ref[2 * CH :, lanes(j)] = (x_grad * xs).astype(bf16)
        dconv_ref[0:CH, lanes(j)] = (step_w[:, lanes(j)] * x_grad + skip * dy) * slope_ref[:, lanes(j)]
        if j % 4 == 3:
            back_from(LANE * (j - 3), LANE * (j + 1))
    for j in range(PAIRS + 2):
        taps = [dconv_ref[3 - k : 3 - k + CH, lanes(j)] for k in range(KW)]
        total = conv_ref[0:1, lanes(j)] * taps[0]
        for k in range(1, KW):
            total = total + conv_ref[k : k + 1, lanes(j)] * taps[k]
        out_ref[:, lanes(j, DI)] = total.astype(bf16)
        value = proj_ref[:, lanes(j, DI)]
        for k in range(KW):
            sum_ref[k : k + 1, lanes(j)] += jnp.sum(taps[k] * value, axis=0, keepdims=True)
        sum_ref[4:5, lanes(j)] += jnp.sum(taps[3], axis=0, keepdims=True)
        if j == 3:
            affinity_low = jnp.where(rows <= cols, affinity_grad, 0.0).astype(bf16)
            grown = grown_ref[...]
            b_grad = mm(affinity_low, c_low) + mm_t(keep_ref[...], state_low)
            c_grad = t_mm(affinity_low, b_low) + mm_t(grown, saved_ref[...])
            dconv_ref[0:CH, lanes(PAIRS)] = b_grad * slope_ref[:, lanes(PAIRS)]
            dconv_ref[0:CH, lanes(PAIRS + 1)] = c_grad * slope_ref[:, lanes(PAIRS + 1)]
        if j == 8:
            gather = gather_ref[...]
            row_sums = mm(jnp.concatenate(high_low(row_ref[...]), axis=0), gather)
            row_sums = row_sums[:8] + row_sums[8:]
            last_grad = row_sums[0:1] + grow[CH - 1 : CH] * row_sums[1:2]
            cum_grad = mm(terms_ref[0:CH], gather) + mm(terms_ref[CH : 2 * CH], gather)
            decay_grad = jnp.dot((cols >= rows).astype(f32), cum_grad, precision=lax.Precision.HIGHEST, preferred_element_type=f32) + last_grad
            step_grad = mm(terms_ref[2 * CH :], gather) + head_ref[2:3] * decay_grad
            raw_grad = step_grad * sigmoid(shifted)
            out_ref[:, DI + CONV_CH :] = raw_grad[:, :NH].astype(bf16)
            sum_ref[7:8, 0:LANE] += jnp.sum(raw_grad, axis=0, keepdims=True)
            sum_ref[7:8, LANE : 2 * LANE] += jnp.sum(decay_grad * step, axis=0, keepdims=True)
        if j == 5:
            state_ref[...] = grow_w[CH - 1 : CH] * state + t_mm(c_low, grown)
        if top and j == 1:
            slot = lax.broadcasted_iota(jnp.int32, (CH, D), 0) + chunk * CH
            result = stream_ref[...] + mm(mixed_ref[...], w_out_ref[...])
            result_ref[...] = jnp.where(slot < length_ref[0:1, 0:1], result, 0.0).astype(bf16)
        if j in (3, 7, 11):
            back_from(DI + LANE * (j - 3), DI + LANE * (j + 1))
    dconv_ref[CH : CH + 8] = dconv_ref[0:8]

    back_from(2 * DI, DI + CONV_CH)
    back_from(DI + CONV_CH, NIN)
    normed_grad = back_ref[...]
    stream = stream_ref[...].astype(f32)
    scale = norm_scale(stream)
    sum_ref[7:8, 2 * LANE : 2 * LANE + D] += jnp.sum(normed_grad * (stream * scale), axis=0, keepdims=True)
    inner = normed_grad * params[0][layer : layer + 1]
    pull = scale * scale * scale * jnp.mean(inner * stream, axis=-1, keepdims=True)
    down_ref[...] = upstream_ref[...].astype(f32) + scale * inner - pull * stream


def ring_place(n):
    wide = n // 4
    me = lax.axis_index("shard")
    chip, core = me // 2, me % 2
    row, col = chip // wide, chip % wide
    place = row * (2 * wide - 1 - col) + (1 - row) * col

    def shard_of(at, c):
        at = at % (2 * wide)
        r = at // wide
        x = r * (2 * wide - 1 - at) + (1 - r) * at
        return (r * wide + x) * 2 + c

    return place, core, shard_of


def halves(rows):
    first = rows // 2 // 16 * 16
    return (0, first), (first, rows - first)


def aligned(start, size, unit=16):
    return pl.ds(pl.multiple_of(start, unit), size)


def column_groups(width, replicas, parts):
    unit = LANE * replicas
    units = -(-width // unit)
    parts = min(parts, units)
    groups, start = [], 0
    for g in range(parts):
        size = (units // parts + (g < units % parts)) * unit
        groups.append((start, size, min(size, width - start)))
        start += size
    return groups, start


def remote(src, dst, send, recv, axis, to):
    return pltpu.make_async_remote_copy(
        src_ref=src, dst_ref=dst, send_sem=send, recv_sem=recv, device_id={axis: to}, device_id_type=MESH
    )


def greet(near, across):
    barrier = pltpu.get_barrier_semaphore()
    for to in near:
        pl.semaphore_signal(barrier, inc=1, device_id={"shard": to}, device_id_type=MESH)
    for to in across:
        pl.semaphore_signal(barrier, inc=1, device_id={"replica": to}, device_id_type=MESH)


def meet(count):
    pl.semaphore_wait(pltpu.get_barrier_semaphore(), count)


def bits(count):
    levels = count.bit_length() - 1
    assert 1 << levels == count
    return levels


class Gather:
    def __init__(self, n, arrays, items):
        self.n, self.half = n, n // 4
        self.arrays, self.items = arrays, items
        self.rows = [arrays[i[0]].shape[1] for i in items]

    def in_specs(self):
        return [pl.BlockSpec(memory_space=pl.ANY)] * len(self.arrays)

    out_specs = in_specs

    def out_shapes(self):
        return [jax.ShapeDtypeStruct((a.shape[1] * self.n, a.shape[2]), a.dtype) for a in self.arrays]

    def scratch(self):
        count = len(self.items)
        dma = pltpu.SemaphoreType.DMA
        own = [pltpu.VMEM((rows, i[3]), self.arrays[i[0]].dtype) for rows, i in zip(self.rows, self.items)]
        return [dma((count, self.half, 2, 2)), dma((count, self.half + 1, 2, 2)), dma((count, 2))] + own

    def tracks(self, parts, wholes, scratch):
        ring_sem, pair_sem, own_sem, *own_refs = scratch
        n, half = self.n, self.half
        place, core, shard_of = ring_place(n)
        right, left, pair = shard_of(place + 1, core), shard_of(place + n // 2 - 1, core), shard_of(place, 1 - core)
        me = shard_of(place, core)
        ways = ((0, right), (1, left))

        def rows_of(i, s, d):
            return (0, self.rows[i]) if s < half else halves(self.rows[i])[d]

        def part_at(i, part):
            a, layer, first, wide = self.items[i]
            return parts[a].at[layer, part[0] : part[0] + part[1], first : first + wide]

        def whole_at(i, owner, part):
            a, _, first, wide = self.items[i]
            return wholes[a].at[aligned(owner * self.rows[i] + part[0], part[1]), first : first + wide]

        def hop(i, s, d, to):
            owner = shard_of(place + (n // 2 - (s - 1) if d == 0 else s - 1), core)
            part = rows_of(i, s, d)
            src = part_at(i, part) if s == 1 else whole_at(i, owner, part)
            return remote(src, whole_at(i, owner, part), ring_sem.at[i, s - 1, d, 0], ring_sem.at[i, s - 1, d, 1], "shard", to)

        def cross(i, s, d):
            owner = me if s == 0 else shard_of(place + (n // 2 - s if d == 0 else s), core)
            part = (0, self.rows[i]) if s == 0 else rows_of(i, s, d)
            src = part_at(i, part) if s == 0 else whole_at(i, owner, part)
            return remote(src, whole_at(i, owner, part), pair_sem.at[i, s, d, 0], pair_sem.at[i, s, d, 1], "shard", pair)

        def own_in(i):
            return pltpu.make_async_copy(part_at(i, (0, self.rows[i])), own_refs[i], own_sem.at[i, 0])

        def own_out(i):
            return pltpu.make_async_copy(own_refs[i], whole_at(i, me, (0, self.rows[i])), own_sem.at[i, 1])

        crossings = [(0, 0)] + [(s, d) for s in range(1, half + 1) for d in (0, 1)]

        def start(i):
            for d, to in ways:
                hop(i, 1, d, to).start()
            cross(i, 0, 0).start()
            own_in(i).start()

        def forward(i, s):
            if s == 1:
                own_in(i).wait()
                own_out(i).start()
            for d, to in ways:
                hop(i, s, d, to).wait_recv()
                if s < half:
                    hop(i, s + 1, d, to).start()
                cross(i, s, d).start()

        def last(i):
            for s, d in crossings:
                cross(i, s, d).wait_recv()
            for s, d in crossings:
                cross(i, s, d).wait_send()
            for s in range(1, half + 1):
                for d, to in ways:
                    hop(i, s, d, to).wait_send()
            own_out(i).wait()

        hello = [lambda: greet((right, left, pair), ()), lambda: meet(3)]
        return hello, [
            [lambda i=i: start(i)]
            + [lambda i=i, s=s: forward(i, s) for s in range(1, half + 1)]
            + [lambda i=i: last(i)]
            for i in range(len(self.items))
        ]


class Reduce:
    def __init__(self, n, replicas, shapes, groups, modes=None):
        self.n, self.replicas = n, replicas
        self.chips, self.half, self.levels = n // 2, n // 4, bits(replicas)
        self.shapes = [(r // n, w) for r, w in shapes]
        self.groups = [column_groups(w, replicas, count) for (_, w), count in zip(self.shapes, groups)]
        self.modes = modes or ["full"] * len(shapes)
        self.work = [(a, g) for a in range(len(shapes)) for g in range(len(self.groups[a][0]))]

    def in_specs(self):
        return [pl.BlockSpec(memory_space=pl.ANY)] * len(self.shapes)

    out_specs = in_specs

    def out_shapes(self):
        return [
            jax.ShapeDtypeStruct((rows, padded), bf16) if mode == "head" else jax.ShapeDtypeStruct((rows, width), f32)
            for (rows, width), (_, padded), mode in zip(self.shapes, self.groups, self.modes)
        ]

    each = 12

    def scratch(self):
        dma = pltpu.SemaphoreType.DMA
        items = []
        for (rows, width), (groups, padded), mode in zip(self.shapes, self.groups, self.modes):
            g = len(groups)
            plane = (rows, width) if mode != "tail" else (16, LANE)
            far = (rows, padded) if mode != "head" else (16, LANE)
            items += [
                pltpu.VMEM((self.chips,) + plane, bf16),
                pltpu.VMEM((self.chips,) + plane, bf16),
                pltpu.VMEM((self.half, 2) + plane, bf16),
                pltpu.VMEM((self.half, 2) + plane, bf16),
                pltpu.VMEM((rows, padded), bf16),
                pltpu.VMEM((self.levels,) + far, bf16),
                pltpu.VMEM(far, bf16),
                pltpu.VMEM((rows, width) if mode != "head" else (16, LANE), f32),
                dma((g, self.chips, 3)), dma((g, self.half, 2, 2)), dma((g, 2 * self.levels, 2)), dma((g,)),
            ]
        return items

    def tracks(self, ins, outs, scratch, feed=None):
        n, replicas, chips, half, levels = self.n, self.replicas, self.chips, self.half, self.levels
        place, core, shard_of = ring_place(n)
        right, left, pair = shard_of(place + 1, core), shard_of(place + chips - 1, core), shard_of(place, 1 - core)
        mine = lax.axis_index("replica")
        ways = ((0, right), (1, left))
        order = [half] + [v for s in range(half - 1, 0, -1) for v in (s, chips - s)] + [0]
        buffers = [scratch[self.each * a : self.each * (a + 1)] for a in range(len(self.shapes))]

        def partner(j):
            bit = mine // (1 << j) % 2
            return mine + (1 - 2 * bit) * (1 << j), bit

        def cols_of(a, g):
            start, _, wide = self.groups[a][0][g]
            return slice(start, start + wide)

        def piece(a, g, owner):
            rows = self.shapes[a][0]
            return ins[a].at[aligned(owner * rows, rows), cols_of(a, g)]

        def pairing(a, g, q):
            sem = buffers[a][8]
            return remote(piece(a, g, shard_of(place + q, 1 - core)), buffers[a][1].at[q, :, cols_of(a, g)], sem.at[g, q, 0], sem.at[g, q, 1], "shard", pair)

        def loading(a, g, q):
            return pltpu.make_async_copy(
                piece(a, g, shard_of(place + q, core)), buffers[a][0].at[q, :, cols_of(a, g)], buffers[a][8].at[g, q, 2]
            )

        def part_of(a, k, d):
            rows = self.shapes[a][0]
            return halves(rows)[d] if k == 1 else (0, rows)

        def ringing(a, g, k, d, to):
            first, count = part_of(a, k, d)
            sem = buffers[a][9]
            return remote(
                buffers[a][2].at[k - 1, d, first : first + count, cols_of(a, g)],
                buffers[a][3].at[k - 1, d, first : first + count, cols_of(a, g)],
                sem.at[g, k - 1, d, 0], sem.at[g, k - 1, d, 1], "shard", to,
            )

        def region(a, g, j, keep):
            start, size, _ = self.groups[a][0][g]
            at = start
            for i in range(j + 1):
                bit = mine // (1 << i) % 2
                at = at + (bit if keep or i < j else 1 - bit) * (size >> (i + 1))
            return aligned(at, size >> (j + 1), LANE)

        def halving(a, g, j):
            cols = region(a, g, j, False)
            sem = buffers[a][10]
            return remote(
                buffers[a][4].at[:, cols], buffers[a][5].at[j, :, cols], sem.at[g, j, 0], sem.at[g, j, 1], "replica", partner(j)[0]
            )

        def doubling(a, g, j):
            cols = region(a, g, j, True)
            sem = buffers[a][10]
            return remote(
                buffers[a][6].at[:, cols], buffers[a][6].at[:, cols],
                sem.at[g, levels + j, 0], sem.at[g, levels + j, 1], "replica", partner(j)[0],
            )

        def storing(a, g):
            cols = cols_of(a, g)
            return pltpu.make_async_copy(buffers[a][7].at[:, cols], outs[a].at[:, cols], buffers[a][11].at[g])

        def both(a, g, q, part):
            first, count = part
            rows, cols = slice(first, first + count), cols_of(a, g)
            return buffers[a][0][q, rows, cols].astype(f32) + buffers[a][1][q, rows, cols].astype(f32)

        def arrived(a, g, q):
            if not (feed and a == 0):
                loading(a, g, q).wait()
            pairing(a, g, q).wait_recv()

        def begin(a, g):
            fed = feed and a == 0
            if fed:
                feed(g, cols_of(a, g))
            for q in order:
                pairing(a, g, q).start()
                if fed:
                    buffers[a][0][q, :, cols_of(a, g)] = piece(a, g, shard_of(place + q, core))[...]
                else:
                    loading(a, g, q).start()

        def turn(a, g, k):
            cols = cols_of(a, g)
            for d, to in ways:
                q = half - k + 1 if d == 0 else chips - (half - k + 1)
                if k > 1 or d == 0:
                    arrived(a, g, q)
                if k > 1:
                    ringing(a, g, k - 1, d, to).wait_recv()
                pieces = [part_of(a, 1, d)] if k == 1 else halves(self.shapes[a][0]) if k == 2 else [part_of(a, k, d)]
                for e, (at, many) in enumerate(pieces):
                    value = both(a, g, q, (at, many))
                    if k > 2 or (k == 2 and e == d):
                        value = value + buffers[a][3][k - 2, d, at : at + many, cols].astype(f32)
                    buffers[a][2][k - 1, d, at : at + many, cols] = value.astype(bf16)
                ringing(a, g, k, d, to).start()

        def settle(a, g):
            cols = cols_of(a, g)
            start, size, wide = self.groups[a][0][g]
            rows = self.shapes[a][0]
            arrived(a, g, 0)
            value = both(a, g, 0, (0, rows))
            for d, to in ways:
                ringing(a, g, half, d, to).wait_recv()
                value = value + buffers[a][3][half - 1, d, :, cols].astype(f32)
            buffers[a][4][:, cols] = value.astype(bf16)
            if wide < size:
                buffers[a][4][:, start + wide : start + size] = jnp.zeros((rows, size - wide), bf16)
            if self.modes[a] == "head":
                handing(a, g).start()
            else:
                halving(a, g, 0).start()

        def handing(a, g):
            start, size, _ = self.groups[a][0][g]
            cols = slice(start, start + size)
            here, there = buffers[a][4].at[:, cols], (outs if self.modes[a] == "head" else ins)[a].at[:, cols]
            if self.modes[a] == "tail":
                here, there = there, here
            return pltpu.make_async_copy(here, there, buffers[a][11].at[g])

        def resume(a, g):
            handing(a, g).wait()
            halving(a, g, 0).start()

        def halve(a, g, j):
            halving(a, g, j).wait_recv()
            cols = region(a, g, j, True)
            value = (buffers[a][4][:, cols].astype(f32) + buffers[a][5][j, :, cols].astype(f32)).astype(bf16)
            if j + 1 < levels:
                buffers[a][4][:, cols] = value
                halving(a, g, j + 1).start()
            else:
                buffers[a][6][:, cols] = value
                doubling(a, g, j).start()

        def double(a, g, j):
            doubling(a, g, j).wait_recv()
            if j > 0:
                doubling(a, g, j - 1).start()

        def last(a, g):
            double(a, g, 0)
            cols = cols_of(a, g)
            buffers[a][7][:, cols] = buffers[a][6][:, cols].astype(f32)
            storing(a, g).start()
            if self.modes[a] != "tail":
                leave(a, g)
            for j in range(levels):
                halving(a, g, j).wait_send()
                doubling(a, g, j).wait_send()
            storing(a, g).wait()

        def leave(a, g):
            for q in order:
                pairing(a, g, q).wait_send()
            for k in range(1, half + 1):
                for d, to in ways:
                    ringing(a, g, k, d, to).wait_send()

        def part(a, g):
            leave(a, g)
            handing(a, g).wait()

        across = [partner(j)[0] for j in range(levels)]
        hello = [lambda: greet((right, left, pair), across), lambda: meet(3 + levels)]
        def track(a, g):
            planes = (
                [lambda: begin(a, g)]
                + [lambda k=k: turn(a, g, k) for k in range(1, half + 1)]
                + [lambda: settle(a, g)]
            )
            rest = (
                [lambda j=j: halve(a, g, j) for j in range(levels)]
                + [lambda j=j: double(a, g, j) for j in range(levels - 1, 0, -1)]
                + [lambda: last(a, g)]
            )
            if self.modes[a] == "head":
                return planes + [lambda: part(a, g)]
            if self.modes[a] == "tail":
                return [lambda: handing(a, g).start(), lambda: resume(a, g)] + rest
            return planes + rest

        return hello, [track(a, g) for a, g in self.work]


def beside(body, counts, engine, times, hooks):
    ins, outs, scratch = counts

    def kernel(*refs):
        i = len(engine.in_specs())
        o = len(engine.out_specs())
        own_in, refs = refs[:ins], refs[ins:]
        far_in, refs = refs[:i], refs[i:]
        own_out, refs = refs[:outs], refs[outs:]
        far_out, refs = refs[:o], refs[o:]
        own_scratch, far_scratch = refs[:scratch], refs[scratch:]
        hello, tracks = engine.tracks(far_in, far_out, far_scratch)
        plan = {}
        plan[0] = [hello[0]]
        plan.setdefault(min(t[0] for t in times), []).append(hello[1])
        for t, track in enumerate(tracks):
            wanted = times[t]
            if len(wanted) != len(track):
                first = wanted[0]
                wanted = [first + (hooks - first) * i // (len(track) - 1) for i in range(len(track))]
            for at, stage in zip(wanted, track):
                plan.setdefault(min(at, hooks), []).append(stage)
        step = pl.program_id(0) * pl.num_programs(1) + pl.program_id(1)

        def run(at):
            for stage in plan[at]:
                stage()

        pl.when(step == 0)(lambda: run(0))
        body(*own_in, *own_out, *own_scratch)
        for at in sorted(plan):
            if at > 0:
                pl.when(step == at - 1)(lambda at=at: run(at))

    return kernel


def move(engine, operands, collective_id, name):
    def kernel(*refs):
        i, o = len(engine.in_specs()), len(engine.out_specs())
        hello, tracks = engine.tracks(refs[:i], refs[i : i + o], refs[i + o :])
        for stage in hello:
            stage()
        for at in range(max(map(len, tracks))):
            for track in tracks:
                if at < len(track):
                    track[at]()

    return pl.pallas_call(
        kernel,
        out_shape=engine.out_shapes(),
        in_specs=engine.in_specs(),
        out_specs=engine.out_specs(),
        scratch_shapes=engine.scratch(),
        compiler_params=pltpu.CompilerParams(collective_id=collective_id, has_side_effects=True),
        name=name,
    )(*operands)


def finish_kernel(engine, n, replicas, *refs):
    left_ref, right_hbm, first_ref, second_ref, in_ref, out0_ref, out1_ref = refs[:7]
    in_total_ref, out_total_ref, total_ref = refs[7:10]
    product_ref, right_ref, mine_ref, plane_ref, across_ref, whole_ref, in_buf, out_buf = refs[10:18]
    plane_sem, across_sem, share_sem, copy_sem, right_sem, *scratch = refs[18:]
    me, mine = lax.axis_index("shard"), lax.axis_index("replica")
    width = mine_ref.shape[2]

    def operand(g):
        start, _, wide = engine.groups[0][0][g]
        cols = slice(start, start + wide)
        return pltpu.make_async_copy(right_hbm.at[:, cols], right_ref.at[:, cols], right_sem.at[g])

    for g in range(len(engine.groups[0][0])):
        operand(g).start()

    ready = set()

    def feed(g, cols):
        if g in ready:
            return
        ready.add(g)
        operand(g).wait()
        product_ref[:, cols] = mm(left_ref[...], right_ref[:, cols]).astype(bf16)

    _, tracks = engine.tracks((product_ref, out0_ref), (in_total_ref.at[0], out_total_ref.at[0]), scratch, feed)
    greet([(me + s) % n for s in range(1, n)], [(mine + s) % replicas for s in range(1, replicas)])
    moves = [(in_ref, in_buf, in_total_ref.at[1]), (out1_ref, out_buf, out_total_ref.at[1])]
    fetches = [pltpu.make_async_copy(src, via, copy_sem.at[0, i]) for i, (src, via, _) in enumerate(moves)]
    stores = [pltpu.make_async_copy(via, dst, copy_sem.at[1, i]) for i, (_, via, dst) in enumerate(moves)]
    for fetch in fetches:
        fetch.start()
    spots = [(k // (n // 2), k % (n // 2) * width) for k in range(n)]
    for k, (half, at) in enumerate(spots):
        mine_ref[k] = (second_ref if half else first_ref)[:, at : at + width]

    def plane(s):
        to = (me + s) % n
        return remote(mine_ref.at[to], plane_ref.at[s], plane_sem.at[0, s], plane_sem.at[1, s], "shard", to)

    def across(s):
        return remote(across_ref.at[0], across_ref.at[s], across_sem.at[0, s], across_sem.at[1, s], "replica", (mine + s) % replicas)

    def share(s):
        return remote(whole_ref.at[me], whole_ref.at[me], share_sem.at[0, s], share_sem.at[1, s], "shard", (me + s) % n)

    def sharing(s):
        owner = (me + n - s) % n
        return remote(whole_ref.at[owner], whole_ref.at[owner], share_sem.at[0, s], share_sem.at[1, s], "shard", (me + s) % n)

    def send_small():
        for s in range(1, n):
            plane(s).start()

    def sum_plane():
        value = mine_ref[me]
        for s in range(1, n):
            plane(s).wait_recv()
            value = value + plane_ref[s]
        across_ref[0] = value
        for s in range(1, replicas):
            across(s).start()

    def sum_across():
        for s in range(1, replicas):
            across(s).wait_recv()
        zero = jnp.zeros((8, width), f32)
        whole_ref[me] = lax.fori_loop(0, replicas, lambda i, acc: acc + across_ref[(mine - i + replicas) % replicas], zero)
        for s in range(1, n):
            share(s).start()

    def give_small():
        for s in range(1, n):
            sharing(s).wait_recv()
        for k, (half, at) in enumerate(spots):
            total_ref[8 * half : 8 * half + 8, at : at + width] = whole_ref[k]

    plan = {}
    for (a, g), track in zip(engine.work, tracks):
        for i, stage in enumerate(track):
            plan.setdefault(((g if a == 0 else 0) + (2 * i - 1 if i else 0), i), []).append(stage)
    feed(0, slice(0, engine.groups[0][0][0][2]))
    meet(n + replicas - 2)
    slots = sorted(plan)
    for k, slot in enumerate(slots):
        for stage in plan[slot]:
            stage()
        if k == 0:
            send_small()
        if k == len(slots) // 4:
            sum_plane()
            for fetch, store in zip(fetches, stores):
                fetch.wait()
                store.start()
        if k == len(slots) // 2:
            sum_across()
    give_small()
    for s in range(1, n):
        plane(s).wait_send()
        share(s).wait_send()
    for s in range(1, replicas):
        across(s).wait_send()
    for store in stores:
        store.wait()


def finish(left, right, sums, in_grad, out_grads, n, replicas, collective_id):
    rows, width = left.shape[0] // n, right.shape[1]
    out_rows, out_width = out_grads[1].shape
    engine = Reduce(n, replicas, [(left.shape[0], width), (out_rows * n, out_width)], [7, 1], ["full", "tail"])
    anywhere, vmem = pl.BlockSpec(memory_space=pl.ANY), pl.BlockSpec(memory_space=pltpu.VMEM)
    dma = pltpu.SemaphoreType.DMA
    small = (8, 2 * SUMS // n)
    return pl.pallas_call(
        lambda *refs: finish_kernel(engine, n, replicas, *refs),
        out_shape=[
            jax.ShapeDtypeStruct((LAYERS, rows, width), f32),
            jax.ShapeDtypeStruct((LAYERS, out_rows, out_width), f32),
            jax.ShapeDtypeStruct((LAYERS * 8, SUMS), f32),
        ],
        in_specs=[vmem, anywhere, vmem, vmem] + [anywhere] * 3,
        out_specs=[anywhere, anywhere, vmem],
        scratch_shapes=[
            pltpu.VMEM((n * rows, width), bf16),
            pltpu.VMEM(right.shape, bf16),
            pltpu.VMEM((n,) + small, f32),
            pltpu.VMEM((n,) + small, f32),
            pltpu.VMEM((replicas,) + small, f32),
            pltpu.VMEM((n,) + small, f32),
            pltpu.VMEM((rows, width), f32),
            pltpu.VMEM((out_rows, out_width), f32),
            dma((2, n)), dma((2, replicas)), dma((2, n)), dma((2, 2)), dma((len(engine.groups[0][0]),)),
        ] + engine.scratch(),
        compiler_params=pltpu.CompilerParams(collective_id=collective_id, has_side_effects=True, vmem_limit_bytes=60 * 2**20),
        name="finish",
    )(left, right, *sums, in_grad, *out_grads)


def results_kernel(count, total_ref, a_log_ref, *refs):
    from_refs, refs = refs[:count], refs[count:]
    to_refs, refs = refs[:count], refs[count:]
    gain_ref, conv_w_ref, conv_b_ref, dt_bias_ref, a_log_grad_ref, d_skip_ref, out_gain_ref, *refs = refs
    via_refs, sem = refs[:count], refs[count]
    fetches = [pltpu.make_async_copy(a, b, sem.at[0, i]) for i, (a, b) in enumerate(zip(from_refs, via_refs))]
    stores = [pltpu.make_async_copy(a, b, sem.at[1, i]) for i, (a, b) in enumerate(zip(via_refs, to_refs))]
    for fetch in fetches:
        fetch.start()
    for fetch, store in zip(fetches, stores):
        fetch.wait()
        store.start()
    column = lax.broadcasted_iota(jnp.int32, (DI, LANE), 1)
    owner = lax.broadcasted_iota(jnp.int32, (DI, LANE), 0) // HEAD
    gather = (column == owner).astype(f32).astype(bf16)
    for l in range(LAYERS):
        here, row = slice(l, l + 1), 8 * l
        gain_ref[here] = total_ref[row + 7 : row + 8, 2 * LANE : 2 * LANE + D]
        conv_w_ref[l] = total_ref[row : row + KW, :CONV_CH]
        conv_b_ref[here] = total_ref[row + 4 : row + 5, :CONV_CH]
        dt_bias_ref[here] = total_ref[row + 7 : row + 8, 0:NH]
        a_log_grad_ref[here] = -jnp.exp(a_log_ref[here]) * total_ref[row + 7 : row + 8, LANE : LANE + NH]
        out_gain_ref[here] = total_ref[row + 6 : row + 7, :DI]
        value = total_ref[row : row + 8, :DI]
        high = value.astype(bf16)
        middle = (value - high.astype(f32)).astype(bf16)
        low = (value - high.astype(f32) - middle.astype(f32)).astype(bf16)
        summed = mm(high, gather) + mm(middle, gather) + mm(low, gather)
        d_skip_ref[here] = summed[5:6, 0:NH]
    for store in stores:
        store.wait()


def results(total, params, moved):
    anywhere, vmem = pl.BlockSpec(memory_space=pl.ANY), pl.BlockSpec(memory_space=pltpu.VMEM)
    count = len(moved)
    out = pl.pallas_call(
        lambda *refs: results_kernel(count, *refs),
        in_specs=[vmem, vmem] + [anywhere] * count,
        out_specs=[anywhere] * count + [vmem] * len(params),
        out_shape=[jax.ShapeDtypeStruct(m.shape, m.dtype) for m in moved] + [jax.ShapeDtypeStruct(p.shape, f32) for p in params],
        scratch_shapes=[pltpu.VMEM(m.shape, m.dtype) for m in moved] + [pltpu.SemaphoreType.DMA((2, count))],
        compiler_params=pltpu.CompilerParams(vmem_limit_bytes=62 * 2**20),
        name="results",
    )(total, params[4], *moved)
    return out[:count], out[count:]


def product_kernel(left_ref, right_ref, from_ref, out_ref, to_ref, via_ref, sem):
    step, last = pl.program_id(0), pl.num_programs(0) - 1
    fetch = pltpu.make_async_copy(from_ref, via_ref, sem.at[0])
    store = pltpu.make_async_copy(via_ref, to_ref, sem.at[1])
    pl.when(step == 0)(fetch.start)
    out_ref[...] = mm(left_ref[...], right_ref[...]).astype(bf16)

    @pl.when(step == 1)
    def _():
        fetch.wait()
        store.start()

    pl.when(step == last)(store.wait)


def product(left, right, wide, moved):
    (rows, depth), width = left.shape, right.shape[1]
    anywhere = pl.BlockSpec(memory_space=pl.ANY)
    return pl.pallas_call(
        product_kernel,
        grid=(pl.cdiv(width, wide),),
        in_specs=[pl.BlockSpec((rows, depth), lambda c: (0, 0)), pl.BlockSpec((depth, wide), lambda c: (0, c)), anywhere],
        out_specs=[pl.BlockSpec((rows, wide), lambda c: (0, c)), anywhere],
        out_shape=[jax.ShapeDtypeStruct((rows, width), bf16), jax.ShapeDtypeStruct(moved.shape, moved.dtype)],
        scratch_shapes=[pltpu.VMEM(moved.shape, moved.dtype), pltpu.SemaphoreType.DMA((2,))],
        compiler_params=pltpu.CompilerParams(vmem_limit_bytes=62 * 2**20),
        name="product",
    )(left, right, moved)


def turned_kernel(left_ref, right_ref, out_ref):
    out_ref[...] = t_mm(left_ref[...], right_ref[...].astype(bf16)).astype(bf16)


def turned_product(left, right, tall):
    (depth, rows), width = left.shape, right.shape[1]
    return pl.pallas_call(
        turned_kernel,
        grid=(rows // tall,),
        in_specs=[pl.BlockSpec((depth, tall), lambda r: (0, r)), pl.BlockSpec((depth, width), lambda r: (0, 0))],
        out_specs=pl.BlockSpec((tall, width), lambda r: (r, 0)),
        out_shape=jax.ShapeDtypeStruct((rows, width), bf16),
        compiler_params=pltpu.CompilerParams(vmem_limit_bytes=62 * 2**20),
        name="turned_product",
    )(left, right)


def top_kernel(row_total, slots, left_ref, cotangent_ref, lengths_ref, dealing_ref, out_ref, upstream_ref, length_ref):
    @pl.when(pl.program_id(0) == 0)
    def _():
        mine = lax.axis_index("replica") * lax.axis_size("shard") + lax.axis_index("shard")
        place = lax.broadcasted_iota(jnp.int32, lengths_ref.shape, 1)
        dealing, lengths = dealing_ref[...].astype(f32), lengths_ref[...].astype(f32)
        slot = lax.broadcasted_iota(jnp.int32, (slots, D), 0)
        for m in range(MICRO):
            sequence = jnp.sum(jnp.where(place == m * row_total + mine, dealing, 0.0), axis=1, keepdims=True)
            length = jnp.sum(jnp.where(place.astype(f32) == sequence, lengths, 0.0), axis=1, keepdims=True).astype(jnp.int32)
            length_ref[8 * m : 8 * m + 8] = jnp.broadcast_to(length, (8, LANE))
            here = slice(m * slots, (m + 1) * slots)
            upstream_ref[here] = jnp.where(slot < length, cotangent_ref[here].astype(f32), 0.0).astype(bf16)

    out_ref[...] = t_mm(left_ref[...], upstream_ref[...]).astype(bf16)


def top_product(left, cotangent, lengths, dealing, row_total, tall):
    (depth, rows), width = left.shape, cotangent.shape[1]
    whole = lambda shape: pl.BlockSpec(shape, lambda r: (0, 0))
    sequences = lengths.shape[0]
    return pl.pallas_call(
        lambda *refs: top_kernel(row_total, depth // MICRO, *refs),
        grid=(rows // tall,),
        in_specs=[pl.BlockSpec((depth, tall), lambda r: (0, r)), whole((depth, width)), whole((1, sequences)), whole((1, sequences))],
        out_specs=[pl.BlockSpec((tall, width), lambda r: (r, 0)), whole((depth, width)), whole((8 * MICRO, LANE))],
        out_shape=[
            jax.ShapeDtypeStruct((rows, width), bf16),
            jax.ShapeDtypeStruct((depth, width), bf16),
            jax.ShapeDtypeStruct((8 * MICRO, LANE), jnp.int32),
        ],
        compiler_params=pltpu.CompilerParams(vmem_limit_bytes=62 * 2**20),
        name="top_product",
    )(left, cotangent, lengths.reshape(1, sequences), dealing.reshape(1, sequences))


def fixed(shape):
    return pl.BlockSpec(shape, lambda r, c: (0,) * len(shape))


def held(shape):
    return pl.BlockSpec(shape, lambda r, c: (0,) * len(shape), pipeline_mode=pl.Buffered(1))


def grid_call(body, grid, operands, in_specs, out_specs, out_shapes, scratch, name, extra):
    engine, given, times, collective_id = extra
    kernel = beside(body, (len(in_specs), len(out_specs), len(scratch)), engine, times, grid[0] * grid[1])
    return pl.pallas_call(
        kernel, grid=grid, in_specs=in_specs + engine.in_specs(), out_specs=out_specs + engine.out_specs(),
        out_shape=out_shapes + engine.out_shapes(), scratch_shapes=scratch + engine.scratch(),
        compiler_params=pltpu.CompilerParams(
            dimension_semantics=("arbitrary", "arbitrary"), vmem_limit_bytes=60 * 2**20,
            collective_id=collective_id, has_side_effects=True,
        ),
        name=name,
    )(*operands, *given)


def layer_forward(layer, tokens, w_in, before, w_out, params, chunks, extra):
    count = tokens.shape[0]
    block = lambda r, c: (r * chunks + c, 0)
    later = layer > 0
    rows = lambda width: pl.BlockSpec((CH, width), block)
    return grid_call(
        lambda *refs: forward_kernel(layer, *refs),
        (count // (chunks * CH), chunks),
        (*params, tokens, w_in) + ((before, w_out) if later else ()),
        [held(p.shape) for p in params] + [rows(D), held((D, NIN))] + ([rows(DI), held((DI, D))] if later else []),
        ([rows(D)] if later else [])
        + [pl.BlockSpec((D, CH), lambda r, c: (0, r * chunks + c)), rows(NIN), rows(DI), rows(DI), pl.BlockSpec((NSTATE, DI), block), rows(CONV_CH), rows(CONV_CH)],
        ([jax.ShapeDtypeStruct((count, D), f32)] if later else [])
        + [
            jax.ShapeDtypeStruct((D, count), bf16),
            jax.ShapeDtypeStruct((count, NIN), f32),
            jax.ShapeDtypeStruct((count, DI), bf16),
            jax.ShapeDtypeStruct((count, DI), f32),
            jax.ShapeDtypeStruct((count // CH * NSTATE, DI), bf16),
            jax.ShapeDtypeStruct((count, CONV_CH), f32),
            jax.ShapeDtypeStruct((count, CONV_CH), f32),
        ],
        table_scratch()
        + [
            pltpu.VMEM((CH + 8, CONV_CH), f32),
            pltpu.VMEM((CH, LANE), f32),
            pltpu.VMEM((NSTATE, DI), f32),
            pltpu.VMEM((CH, DI), f32),
            pltpu.VMEM((CH, DI), bf16),
        ],
        f"layer_forward_{layer}", extra,
    )


def layer_backward(layer, upstream, stream, w_in, w_out, projected, kept, mixed, length, params, chunks, extra):
    count = projected.shape[0]
    block = lambda r, c: (r * chunks + chunks - 1 - c, 0)
    rows = lambda width: pl.BlockSpec((CH, width), block)
    top = layer == LAYERS - 1
    return grid_call(
        lambda *refs: backward_kernel(layer, *refs),
        (count // (chunks * CH), chunks),
        (*params, upstream, stream, w_in, w_out, projected, *kept) + ((mixed, length) if top else ()),
        [held(p.shape) for p in params]
        + [rows(D), rows(D), held((D, NIN)), held((DI, D)), rows(NIN), rows(DI), pl.BlockSpec((NSTATE, DI), block), rows(CONV_CH), rows(CONV_CH)]
        + ([rows(DI), pl.BlockSpec((8, LANE), lambda r, c: (r, 0))] if top else []),
        ([rows(D)] if top else []) + [rows(NIN), rows(D), fixed((8, SUMS))],
        ([jax.ShapeDtypeStruct((count, D), bf16)] if top else [])
        + [
            jax.ShapeDtypeStruct((count, NIN), bf16),
            jax.ShapeDtypeStruct((count, D), f32),
            jax.ShapeDtypeStruct((8, SUMS), f32),
        ],
        table_scratch()
        + [
            pltpu.VMEM((DI, LANE), bf16),
            pltpu.VMEM((CH, DI), bf16),
            pltpu.VMEM((CH, LANE), f32),
            pltpu.VMEM((NSTATE, DI), f32),
            pltpu.VMEM((CH, DI), f32),
            pltpu.VMEM((CH + 8, CONV_CH), f32),
            pltpu.VMEM((CH, DI), bf16),
            pltpu.VMEM((CH, DI), bf16),
            pltpu.VMEM((3 * CH, DI), bf16),
            pltpu.VMEM((8, DI), f32),
            pltpu.VMEM((CH, D), f32),
        ],
        f"layer_backward_{layer}", extra,
    )


def shards(
    tokens, cotangent, lengths, dealing, in_gain, w_in, conv_w, conv_b, dt_bias, a_log, d_skip, out_gain, w_out,
):
    n, replicas = lax.axis_size("shard"), lax.axis_size("replica")
    slot_count = tokens.shape[2]
    chunks = slot_count // CH
    count = MICRO * slot_count
    params = (in_gain, conv_w, conv_b, dt_bias, a_log, d_skip, out_gain)
    flat = tokens.reshape(count, D)

    (first_in,) = move(Gather(n, [w_in], [(0, 0, 0, CUT), (0, 0, CUT, NIN - CUT)]), (w_in,), 1, "gather_first")
    engine = Gather(n, [w_out, w_in], [(0, 0, 0, D), (1, 1, 0, CUT), (1, 1, CUT, NIN - CUT)])
    normed0, projected0, mixed0, *kept0, first_out, second_in = layer_forward(
        0, flat, first_in, None, None, params, chunks, (engine, (w_out, w_in), GATHER_BOTH, 2)
    )
    engine = Gather(n, [w_out], [(0, 1, 0, D)])
    stream, normed1, projected1, mixed1, *kept1, second_out = layer_forward(
        1, flat, second_in, mixed0, first_out, params, chunks, (engine, (w_out,), GATHER_LAST, 3)
    )

    out_grad1, upstream, length = top_product(mixed1, cotangent.reshape(count, D), lengths, dealing, replicas * n, 512)
    engine = Reduce(n, replicas, [out_grad1.shape], [1])
    result, project_grad1, upstream1, sums1, out_total1 = layer_backward(
        1, upstream, stream, second_in, second_out, projected1, kept1, mixed1, length, params, chunks,
        (engine, (out_grad1,), REDUCE_OUT, 4),
    )
    in_grad1, result = product(normed1, project_grad1, 1024, result)
    out_grad0 = turned_product(mixed0, upstream1, 768)
    engine = Reduce(n, replicas, [in_grad1.shape, out_grad0.shape], [2, 1], ["full", "head"])
    project_grad0, upstream0, sums0, in_total1, out_total0 = layer_backward(
        0, upstream1, flat, first_in, first_out, projected0, kept0, None, None, params, chunks,
        (engine, (in_grad1, out_grad0), REDUCE_BOTH, 5),
    )
    in_total, out_total, small = finish(
        normed0, project_grad0, (sums0, sums1), in_total1, (out_total0, out_total1), n, replicas, 6
    )
    (upstream0, in_total, out_total), (gain_grad, *small) = results(small, params, (upstream0, in_total, out_total))
    shape = (MICRO, 1, slot_count, D)
    return (result.reshape(shape), upstream0.reshape(shape), gain_grad, in_total, *small, out_total)


def solution(mesh):
    rows = P(None, ("replica", "shard"), None, None)
    split = P(None, "shard", None)
    in_specs = (rows, rows, P(), P(), P(), split, P(), P(), P(), P(), P(), P(), split)
    out_specs = (rows, rows, P(), split, P(), P(), P(), P(), P(), P(), split)
    return jax.shard_map(shards, mesh=mesh, in_specs=in_specs, out_specs=out_specs, check_vma=False)
```
